32 devices in a mesh: groups: 2 (over y), seq: 4 (over z), weight: 4 (over x, core).
Axes of the slice: x: 2, y: 2, z: 4, core: 2. Of those that a mesh axis runs over, the one named last changes fastest.
Arguments:
- tokens: bfloat16 [8, 512, 1536], P(('groups', 'weight'), 'seq'), parts along dimension 0, may hold values from -20 to 20
- upstream_grad: bfloat16 [8, 512, 1536], P(('groups', 'weight'), 'seq'), parts along dimension 0, may hold values from -6 to 6
- norm_gain: float32 [1536], replicated, may hold values from 0.5 to 1.5
- norm_bias: float32 [1536], replicated, may hold values from -3 to 3
- input_codes: bfloat16 [1536, 2304], P('weight'), may hold values from -10 to 10
- input_scales: float32 [12, 18], P('weight'), may hold values from 0.02 to 0.06
- input_bias: float32 [2304], replicated, may hold values from -3 to 3
- output_codes: bfloat16 [768, 1536], replicated, may hold values from -4 to 4
- output_scales: float32 [6, 12], replicated, may hold values from 0.02 to 0.06
- layer_scale: float32 [1536], replicated, may hold values from 0.3 to 3
Outputs:
- input_grad: float32 [8, 512, 1536], P(('groups', 'weight'), 'seq'), parts along dimension 0
The draws below stay inside these ranges and needn't reach their ends.
There are 2 independent parts, one for each index of `groups`. The reference program is written for one: setup_inputs(seed, part) draws one part's arguments, and reference() takes and returns one part's arrays. A program takes and returns all parts, laid end to end along the dimension named above; an argument that names none is the same for every part. Nothing has to cross between parts.
All inputs are finite; a program needn't handle non-finite values.
Results may differ from the reference program's by a relative error of at most 0.024.
Values may be sent and summed in bfloat16 or wider, within the bound.
A program may use at most 128 MiB of HBM per device.

```python
import math
import jax
import jax.numpy as jnp
from jax import lax

D = 1536
HEADS = 12
HEAD_DIM = 64
QBLOCK = 128
TOK_DEV = 128
HD = 768
SEQ = 512
IMAGES = 4
N_SEQ = 4


def draw_tokens(key, part):
    first_key = jax.random.fold_in(key, 0)
    sample = jax.random.normal(first_key, (IMAGES, SEQ, D), jnp.float32)
    return jnp.clip(sample, -6.0, 6.0).astype(jnp.bfloat16)


def draw_input_codes(key, part):
    first_key = jax.random.fold_in(key, 0)
    sample = jnp.clip(jax.random.normal(first_key, (D, 3 * HD), jnp.float32), -4.0, 4.0)
    return sample.astype(jnp.bfloat16)


def levels(stream_key, shape, cuts, low, high):
    loudness = 1.0
    for axis_at, blocks in cuts:
        steps = jax.random.uniform(jax.random.fold_in(jax.random.fold_in(stream_key, 6), axis_at), (blocks,), jnp.float32, low / len(cuts), high / len(cuts))
        loudness = loudness * jnp.repeat(jnp.exp(steps), shape[axis_at] // blocks).reshape((-1,) + (1,) * (len(shape) - 1 - axis_at))
    return loudness


def normal_values(stream_key, shape, scale, bound, shards=(), dtype=jnp.bfloat16):
    result = jax.random.normal(stream_key, shape, jnp.float32) * scale
    if len(shards) > 0:
        result = levels(stream_key, shape, shards, -0.22, 0.18) * result
    return jnp.clip(result, min=-bound, max=bound).astype(dtype)


def setup_inputs(seed: int = 0, part: int = 0) -> dict:
    keys = jax.random.split(jax.random.key(seed), 11)
    part_splits = jax.random.split(jax.random.fold_in(keys[10], part), 11)
    return {
        "tokens": draw_tokens(jax.random.fold_in(jax.random.fold_in(keys[10], part), 71), part),
        "upstream_grad": normal_values(part_splits[1], (IMAGES, SEQ, D), 1.0, 6.0, ((0, 4), (1, 4))),
        "norm_gain": jnp.clip(1.0 + 0.1 * jax.random.normal(keys[2], (D,), jnp.float32), 0.5, 1.5),
        "norm_bias": normal_values(keys[3], (D,), 0.5, 3.0, (), jnp.float32),
        "input_codes": draw_input_codes(jax.random.fold_in(keys[10], 71), part),
        "input_scales": jnp.clip(jnp.exp(math.log(0.06) - 1.0986123 * jax.random.uniform(keys[5], (D // QBLOCK, 3 * HD // QBLOCK), jnp.float32) ** levels(keys[5], (D // QBLOCK, 3 * HD // QBLOCK), ((0, 4),), -0.2, 0.2)), 0.02, 0.06),
        "input_bias": normal_values(keys[6], (3 * HD,), 0.5, 3.0, (), jnp.float32),
        "output_codes": normal_values(keys[7], (HD, D), 1.0, 4.0),
        "output_scales": jnp.clip(jnp.exp(jax.random.uniform(keys[8], (HD // QBLOCK, D // QBLOCK), jnp.float32, math.log(0.02), math.log(0.06))), 0.02, 0.06),
        "layer_scale": jnp.clip(jnp.exp(jax.random.uniform(keys[9], (D,), jnp.float32, math.log(0.3), math.log(3.0))), 0.3, 3.0),
    }


def dequantize(codes, scales):
    expanded = jnp.repeat(jnp.repeat(scales, QBLOCK, axis=0), QBLOCK, axis=1)
    return (codes.astype(jnp.float32) * expanded).astype(jnp.bfloat16)

def normalize(rows, gain, shift):
    mean_value = lax.optimization_barrier(jnp.mean(rows, axis=-1, keepdims=True))
    centered = rows - mean_value
    variance = lax.optimization_barrier(jnp.mean(centered * centered, axis=-1, keepdims=True))
    inverse = lax.rsqrt(variance + 1e-06)
    normed = centered * inverse
    return (normed, inverse, (normed * gain + shift).astype(jnp.bfloat16))

def norm_backward(grad_norm, normed, inverse, gain):
    grad_hat = grad_norm * gain
    first_mean = lax.optimization_barrier(jnp.mean(grad_hat, axis=-1, keepdims=True))
    second_mean = lax.optimization_barrier(jnp.mean(grad_hat * normed, axis=-1, keepdims=True))
    return inverse * (grad_hat - first_mean - normed * second_mean)

def rounded_total(terms):
    rounded = lax.optimization_barrier(terms.astype(jnp.bfloat16))
    return lax.optimization_barrier(jnp.sum(rounded.astype(jnp.float32), axis=0))

def head_backward(queries, keys_head, values_head, grads_head):
    head_scale = HEAD_DIM ** (-0.5)
    scores = jnp.dot(queries, keys_head.T, preferred_element_type=jnp.float32) * head_scale
    row_top = lax.optimization_barrier(jnp.max(scores, axis=1, keepdims=True))
    log_total = row_top + jnp.log(lax.optimization_barrier(jnp.sum(jnp.exp(scores - row_top), axis=1, keepdims=True)))
    dprob = jnp.dot(grads_head, values_head.T, preferred_element_type=jnp.float32)
    weights = jnp.exp(scores - log_total)
    row_delta = lax.optimization_barrier(jnp.sum(weights * dprob, axis=1, keepdims=True))
    prob_weights = weights.astype(jnp.bfloat16)
    dscore = (weights * (dprob - row_delta)).astype(jnp.bfloat16)
    query_grad = jnp.dot(dscore, keys_head, preferred_element_type=jnp.float32) * head_scale
    dscore_parts = dscore.astype(jnp.float32).reshape(N_SEQ, TOK_DEV, SEQ)
    prob_parts = prob_weights.astype(jnp.float32).reshape(N_SEQ, TOK_DEV, SEQ)
    query_parts = queries.astype(jnp.float32).reshape(N_SEQ, TOK_DEV, HEAD_DIM)
    grad_parts = grads_head.astype(jnp.float32).reshape(N_SEQ, TOK_DEV, HEAD_DIM)
    key_grad = rounded_total(jnp.einsum('sqk,sqd->skd', dscore_parts, query_parts) * head_scale)
    value_grad = rounded_total(jnp.einsum('sqk,sqd->skd', prob_parts, grad_parts))
    return (query_grad, key_grad, value_grad)

def split_heads(columns):
    return columns.reshape(SEQ, HEADS, HEAD_DIM).transpose(1, 0, 2)

def merge_heads(stacked):
    return stacked.transpose(1, 0, 2).reshape(SEQ, HD)

def reference(tokens, upstream_grad, norm_gain, norm_bias, input_codes, input_scales, input_bias, output_codes, output_scales, layer_scale):
    input_weight = dequantize(input_codes, input_scales)
    output_weight = dequantize(output_codes, output_scales)

    def one_image(packed):
        image_rows, image_grads = packed
        normed, inverse, norm_out = normalize(image_rows.astype(jnp.float32), norm_gain, norm_bias)
        projected = (jnp.dot(norm_out, input_weight, preferred_element_type=jnp.float32) + input_bias).astype(jnp.bfloat16)
        scaled_grad = (image_grads.astype(jnp.float32) * layer_scale).astype(jnp.bfloat16)
        head_grads = jnp.dot(scaled_grad, output_weight.T, preferred_element_type=jnp.float32).astype(jnp.bfloat16)
        heads_in = (split_heads(projected[:, :HD]), split_heads(projected[:, HD:2 * HD]), split_heads(projected[:, 2 * HD:]), split_heads(head_grads))
        query_grad, key_grad, value_grad = lax.map(lambda member: head_backward(*member), heads_in)
        grad_proj = jnp.concatenate([merge_heads(query_grad), merge_heads(key_grad), merge_heads(value_grad)], axis=1).astype(jnp.bfloat16)
        grad_norm = jnp.dot(grad_proj, input_weight.T, preferred_element_type=jnp.float32)
        return norm_backward(grad_norm, normed, inverse, norm_gain)
    return lax.map(one_image, (tokens, upstream_grad))
```

```python
import functools
import math

import jax
import jax.numpy as jnp
from jax import lax
from jax.experimental import pallas as pl
from jax.experimental.pallas import tpu as pltpu
from jax.sharding import PartitionSpec as P

HEADS = 12
HEAD_DIM = 64
QBLOCK = 128
HD = 768


def dequantize(codes, scales):
    expanded = jnp.repeat(jnp.repeat(scales, QBLOCK, axis=0), QBLOCK, axis=1)
    return (codes.astype(jnp.float32) * expanded).astype(jnp.bfloat16)


def normalize(rows, gain, shift):
    mean_value = jnp.mean(rows, axis=-1, keepdims=True)
    centered = rows - mean_value
    variance = jnp.mean(centered * centered, axis=-1, keepdims=True)
    inverse = lax.rsqrt(variance + 1e-06)
    normed = centered * inverse
    return (normed, inverse, (normed * gain + shift).astype(jnp.bfloat16))


def norm_backward(grad_norm, normed, inverse, gain):
    grad_hat = grad_norm * gain
    first_mean = jnp.mean(grad_hat, axis=-1, keepdims=True)
    second_mean = jnp.mean(grad_hat * normed, axis=-1, keepdims=True)
    return inverse * (grad_hat - first_mean - normed * second_mean)


def score_block(queries, head_grads, pair_block):
    row_count = pair_block.shape[0]
    keys_blk = pair_block[:, :HD].reshape(row_count, HEADS, HEAD_DIM)
    values_blk = pair_block[:, HD:].reshape(row_count, HEADS, HEAD_DIM)
    scores = jnp.einsum(
        "qhd,khd->hqk", queries, keys_blk, preferred_element_type=jnp.float32
    ) * HEAD_DIM ** (-0.5)
    dprob = jnp.einsum("qhd,khd->hqk", head_grads, values_blk, preferred_element_type=jnp.float32)
    return (keys_blk, scores, dprob)


def update_stats(statistics, queries, head_grads, pair_rows):
    sub_size = math.gcd(pair_rows.shape[0], 512)

    def visit_block(block_index, running):
        run_max, run_total, run_mix = running
        pair_block = lax.dynamic_slice_in_dim(pair_rows, block_index * sub_size, sub_size, 0)
        keys_blk, scores, dprob = score_block(queries, head_grads, pair_block)
        new_max = jnp.maximum(run_max, jnp.max(scores, axis=-1))
        factor = jnp.exp(run_max - new_max)
        expo = jnp.exp(scores - new_max[..., None])
        return (
            new_max,
            run_total * factor + jnp.sum(expo, axis=-1),
            run_mix * factor + jnp.sum(expo * dprob, axis=-1),
        )

    return lax.fori_loop(0, pair_rows.shape[0] // sub_size, visit_block, statistics)


def block_backward(queries, head_grads, pair_block, log_total, row_delta):
    keys_blk, scores, dprob = score_block(queries, head_grads, pair_block)
    weights = jnp.exp(scores - log_total[..., None])
    prob_weights = weights.astype(jnp.bfloat16)
    dscore = (weights * (dprob - row_delta[..., None])).astype(jnp.bfloat16)
    return (keys_blk, prob_weights, dscore)


def key_terms_from(queries, head_grads, prob_weights, dscore):
    key_part = jnp.einsum(
        "hqk,qhd->khd", dscore, queries, preferred_element_type=jnp.float32
    ) * HEAD_DIM ** (-0.5)
    value_part = jnp.einsum(
        "hqk,qhd->khd", prob_weights, head_grads, preferred_element_type=jnp.float32
    )
    row_count = key_part.shape[0]
    return jnp.concatenate(
        [key_part.reshape(row_count, HD), value_part.reshape(row_count, HD)], axis=1
    )


def query_side(queries, head_grads, keys_values, local_rows):
    seq_rows = local_rows * lax.axis_size("seq")
    start_stats = (
        jnp.full((HEADS, local_rows), -1e30, jnp.float32),
        jnp.zeros((HEADS, local_rows), jnp.float32),
        jnp.zeros((HEADS, local_rows), jnp.float32),
    )
    all_pairs = lax.all_gather(keys_values, "seq", axis=0, tiled=True)
    statistics = update_stats(start_stats, queries, head_grads, all_pairs)
    row_max, row_total, row_mix = statistics
    log_total = row_max + jnp.log(row_total)
    row_delta = row_mix / row_total
    sub_size = math.gcd(seq_rows, 512)
    block_count = seq_rows // sub_size
    empty_query = jnp.zeros((local_rows, HEADS, HEAD_DIM), jnp.float32)

    def backward_step(block_index, running):
        query_grad, buffer = running
        pair_block = lax.dynamic_slice_in_dim(all_pairs, block_index * sub_size, sub_size, 0)
        keys_blk, prob_weights, dscore = block_backward(
            queries, head_grads, pair_block, log_total, row_delta
        )
        query_grad = query_grad + jnp.einsum(
            "hqk,khd->qhd", dscore, keys_blk, preferred_element_type=jnp.float32
        )
        block_terms = key_terms_from(queries, head_grads, prob_weights, dscore)
        buffer = lax.dynamic_update_slice_in_dim(buffer, block_terms, block_index * sub_size, 0)
        return (query_grad, buffer)

    empty_terms = jnp.zeros((seq_rows, 2 * HD), jnp.float32)
    query_grad, buffer = lax.fori_loop(0, block_count, backward_step, (empty_query, empty_terms))
    pair_grads = lax.psum_scatter(
        buffer.astype(jnp.bfloat16), "seq", scatter_dimension=0, tiled=True
    ).astype(jnp.float32)
    return (query_grad, pair_grads)


def general(
    tokens,
    upstream_grad,
    norm_gain,
    norm_bias,
    input_codes,
    input_scales,
    input_bias,
    output_codes,
    output_scales,
    layer_scale,
):
    all_codes, all_scales = (
        lax.all_gather(input_codes.astype(jnp.float32), "weight", axis=0, tiled=True).astype(
            input_codes.dtype
        ),
        lax.all_gather(input_scales, "weight", axis=0, tiled=True),
    )
    input_weight = dequantize(all_codes, all_scales)
    output_weight = dequantize(output_codes, output_scales)
    normed, inverse, norm_out = normalize(tokens[0].astype(jnp.float32), norm_gain, norm_bias)
    projected = (
        jnp.dot(norm_out, input_weight, preferred_element_type=jnp.float32) + input_bias
    ).astype(jnp.bfloat16)
    local_rows = projected.shape[0]
    queries = projected[:, :HD].reshape(local_rows, HEADS, HEAD_DIM)
    keys_values = projected[:, HD:]
    scaled_grad = (upstream_grad[0].astype(jnp.float32) * layer_scale).astype(jnp.bfloat16)
    head_grads = jnp.dot(scaled_grad, output_weight.T, preferred_element_type=jnp.float32).astype(
        jnp.bfloat16
    )
    head_grads = head_grads.reshape(local_rows, HEADS, HEAD_DIM)
    query_grad, pair_grads = query_side(queries, head_grads, keys_values, local_rows)
    query_grad = (query_grad * HEAD_DIM ** (-0.5)).reshape(local_rows, HD)
    grad_proj = jnp.concatenate([query_grad, pair_grads], axis=1).astype(jnp.bfloat16)
    grad_norm = jnp.dot(grad_proj, input_weight.T, preferred_element_type=jnp.float32)
    result = norm_backward(grad_norm, normed, inverse, norm_gain)
    return result[None]


WIDTH = 1536
ROWS = 128
SHARD = 384
HALF = 384
GROUP = 192
PARTS = 2
PART = ROWS // PARTS
BF16 = jnp.bfloat16
F32 = jnp.float32
MESH = pl.DeviceIdType.MESH
NT = (((1,), (1,)), ((), ()))


def fits(mesh):
    return dict(mesh.shape) == {"groups": 2, "seq": 4, "weight": 4}


def fused_kernel(
    tokens_hbm,
    upstream_hbm,
    gain_hbm,
    norm_bias_hbm,
    codes_hbm,
    in_scales_hbm,
    in_bias_hbm,
    out_codes_hbm,
    out_scales_hbm,
    layer_scale_hbm,
    out_ref,
    gain_ref,
    norm_bias_ref,
    in_scales,
    in_bias_ref,
    out_scales,
    layer_scale_ref,
    weight,
    codes,
    out_codes,
    out_weight,
    tokens,
    upstream,
    normed_buf,
    inverse_buf,
    raw,
    norm_out,
    scaled,
    packed,
    gathered,
    projected,
    grads,
    grad_proj,
    load_sem,
    w_send,
    w_recv,
    t_send,
    p_send,
    t_recv,
    a_send,
    a_recv,
    g_send,
    g_recv,
):
    g = lax.axis_index("groups")
    s = lax.axis_index("seq")
    w = lax.axis_index("weight")
    core = lax.rem(w, 2)
    across = lax.rem(w + 2, 4)
    sibling = w + 1 - 2 * core
    far_sibling = lax.rem(sibling + 2, 4)
    side = s // 2
    half = lax.rem(s, 2)
    home = core == side
    inner = lax.rem(s + side, 2) == 1
    owner = w - core + side
    place = 2 * half + core
    blocks = (s, s + 1 - 2 * half, 2 - side, 3 - 3 * side)

    def load(index, source, target):
        copy = pltpu.make_async_copy(source, target, load_sem.at[index])
        copy.start()
        return copy

    load_in_scales = load(4, in_scales_hbm, in_scales)
    load_codes = load(0, codes_hbm, codes)
    load_upstream = load(2, upstream_hbm.at[0], upstream)
    load_out_codes = load(3, out_codes_hbm, out_codes)
    load_tokens = load(1, tokens_hbm.at[0], tokens)
    load_out_scales = load(5, out_scales_hbm, out_scales)
    load_layer_scale = load(6, layer_scale_hbm, layer_scale_ref)
    load_gain = load(7, gain_hbm, gain_ref)
    load_norm_bias = load(8, norm_bias_hbm, norm_bias_ref)
    load_in_bias = load(9, in_bias_hbm, in_bias_ref)

    barrier = pltpu.get_barrier_semaphore()
    peers = [{"weight": across}, {"weight": sibling}, {"groups": 1 - g}]
    for k in (1, 2, 3):
        peers.append({"seq": lax.rem(s + k, 4)})
        peers.append({"seq": lax.rem(s + k, 4), "weight": sibling})
    for peer in peers:
        pl.semaphore_signal(barrier, inc=1, device_id=peer, device_id_type=MESH)

    def remote(source, target, send, recv, peer):
        return pltpu.make_async_remote_copy(
            src_ref=source,
            dst_ref=target,
            send_sem=send,
            recv_sem=recv,
            device_id=peer,
            device_id_type=MESH,
        )

    def half_of(j):
        return half if j < 3 else 1 - half

    def columns_of(j):
        return pl.ds(pl.multiple_of(768 * (j % 3) + HALF * half_of(j), 128), HALF)

    def dequantize_chunk(j):
        first = 6 * (j % 3) + 3 * half_of(j)
        for rb in range(3):
            for cb in range(3):
                cols = pl.ds(pl.multiple_of(128 * (first + cb), 128), 128)
                rows = pl.ds(pl.multiple_of(SHARD * w + 128 * rb, 128), 128)
                block = codes[128 * rb : 128 * (rb + 1), cols].astype(F32)
                weight[rows, cols] = (block * in_scales[rb, first + cb]).astype(BF16)

    def weight_copy(kind, j, row, count, peer):
        part = weight.at[pl.ds(pl.multiple_of(row, 64), count), columns_of(j)]
        return remote(part, part, w_send.at[kind, j], w_recv.at[kind, j], peer)

    def x_copy(j, shard):
        return weight_copy(0, j, SHARD * shard + GROUP * g, GROUP, {"weight": across})

    def y_copy(j, part):
        return weight_copy(1, j, SHARD * across + GROUP * part, GROUP, {"groups": 1 - g})

    def own_copy(j, shard):
        return weight_copy(2, j, SHARD * shard, SHARD, {"weight": sibling})

    def passed_copy(j, shard):
        return weight_copy(3, j, SHARD * shard, SHARD, {"weight": sibling})

    def start_own(j):
        x_copy(j, w).start()
        own_copy(j, w).start()

    def from_x(j):
        x_copy(j, across).wait_recv()
        y_copy(j, g).start()

    def from_y(j):
        y_copy(j, 1 - g).wait_recv()
        passed_copy(j, across).start()

    def weight_ready(j):
        own_copy(j, sibling).wait_recv()
        passed_copy(j, far_sibling).wait_recv()

    def part_rows(part):
        return pl.ds(PART * part, PART)

    def send_tokens(part):
        dest = jnp.where(home & inner, 3 * core, 1 + core)
        return remote(
            tokens_hbm.at[0, part_rows(part)],
            raw.at[s, part_rows(part)],
            t_send.at[0, part],
            t_recv.at[s, part],
            {"seq": dest},
        )

    def forward_tokens(slot, part):
        z = blocks[slot]
        rows = raw.at[z, part_rows(part)]
        return remote(
            rows, rows, t_send.at[slot - 1, part], t_recv.at[z, part], {"seq": 3 * core}
        )

    def pass_tokens(slot, part):
        z = blocks[slot]
        rows = raw.at[z, part_rows(part)]
        source = tokens_hbm.at[0, part_rows(part)] if slot == 0 else rows
        return remote(source, rows, p_send.at[slot, part], t_recv.at[z, part], {"weight": sibling})

    def tokens_here(slot, part):
        pass_tokens(slot, part).wait_recv()

    def relay(slot, part, forward):
        tokens_here(slot, part)
        if forward:
            forward_tokens(slot, part).start()
        pass_tokens(slot, part).start()

    def share(q):
        peer = {"seq": 2 * core + q // 2, "weight": w - core + q % 2}
        return remote(
            packed.at[GROUP * q : GROUP * (q + 1), :],
            gathered.at[s],
            a_send.at[q],
            a_recv.at[s],
            peer,
        )

    def share_done(z):
        return remote(
            packed.at[0:GROUP, :],
            gathered.at[z],
            a_send.at[0],
            a_recv.at[z],
            {"weight": sibling},
        )

    def stays(q):
        return home & (place == q)

    def head_gradients(part):
        for rb in range(3):
            rows = slice(HALF * part + 128 * rb, HALF * part + 128 * (rb + 1))
            for cb in range(12):
                cols = slice(128 * cb, 128 * (cb + 1))
                block = out_codes[rows, cols].astype(F32)
                out_weight[128 * rb : 128 * (rb + 1), cols] = (
                    block * out_scales[3 * part + rb, cb]
                ).astype(BF16)
        value = lax.dot_general(out_weight[...], scaled[...], NT, preferred_element_type=F32)
        packed[HALF * part : HALF * (part + 1), :] = value.astype(BF16)
        for q in (2 * part, 2 * part + 1):

            @pl.when(jnp.logical_not(stays(q)))
            def _():
                share(q).start()

            @pl.when(stays(q))
            def _():
                gathered[s] = packed[GROUP * q : GROUP * (q + 1), :]

    def normalize_slot(slot):
        norm_out[ROWS * slot : ROWS * (slot + 1), :] = normalize(
            raw[blocks[slot]].astype(F32), gain_ref[...][None], norm_bias_ref[...][None]
        )[2]

    def project(t, pair):
        first = pl.multiple_of(768 * t + HALF * half + 128 * core, 128)
        value = jnp.dot(
            norm_out[256 * pair : 256 * (pair + 1), :],
            weight[:, pl.ds(first, 256)],
            preferred_element_type=F32,
        )
        value = value + in_bias_ref[pl.ds(first, 256)][None]
        if t == 0:
            value = value * HEAD_DIM ** (-0.5)
        projected[t, :, 256 * pair : 256 * (pair + 1)] = value.T.astype(BF16)

    load_in_scales.wait()
    load_codes.wait()
    dequantize_chunk(0)
    pl.semaphore_wait(barrier, len(peers))
    for part in range(PARTS):
        send_tokens(part).start()
    start_own(0)

    @pl.when(home)
    def _():
        for part in range(PARTS):
            pass_tokens(0, part).start()

    dequantize_chunk(1)
    start_own(1)
    for j in range(2, 6):
        dequantize_chunk(j)

    load_layer_scale.wait()
    load_upstream.wait()
    scaled[...] = (upstream[...].astype(F32) * layer_scale_ref[...][None]).astype(BF16)
    load_out_scales.wait()
    load_out_codes.wait()
    head_gradients(0)
    head_gradients(1)

    load_gain.wait()
    load_norm_bias.wait()
    load_in_bias.wait()
    load_tokens.wait()
    normed, inverse, rounded = normalize(
        tokens[...].astype(F32), gain_ref[...][None], norm_bias_ref[...][None]
    )
    normed_buf[...] = normed
    inverse_buf[...] = inverse

    @pl.when(home)
    def _():
        norm_out[0:ROWS, :] = rounded

    from_x(0)
    start_own(2)

    @pl.when(home)
    def _():
        for part in range(PARTS):
            relay(1, part, False)

    @pl.when(home & inner)
    def _():
        for slot in (2, 3):
            relay(slot, 0, True)

    from_x(1)
    from_y(0)

    @pl.when(jnp.logical_not(home))
    def _():
        for slot in (0, 1):
            for part in range(PARTS):
                tokens_here(slot, part)
        normalize_slot(0)

    normalize_slot(1)

    @pl.when(home & inner)
    def _():
        for part in range(1, PARTS):
            for slot in (2, 3):
                relay(slot, part, True)

    from_x(2)
    start_own(3)
    start_own(4)
    from_y(1)
    weight_ready(0)
    project(0, 0)

    @pl.when(inner)
    def _():
        @pl.when(jnp.logical_not(home))
        def _():
            for slot in (2, 3):
                for part in range(PARTS):
                    tokens_here(slot, part)

        normalize_slot(2)
        normalize_slot(3)
        project(0, 1)

    weight_ready(1)
    project(1, 0)
    from_y(2)

    @pl.when(inner)
    def _():
        project(1, 1)

    weight_ready(2)
    project(2, 0)

    @pl.when(inner)
    def _():
        project(2, 1)

    @pl.when(jnp.logical_not(inner))
    def _():
        @pl.when(home)
        def _():
            for part in range(PARTS):
                for slot in (2, 3):
                    relay(slot, part, False)

        @pl.when(jnp.logical_not(home))
        def _():
            for part in range(PARTS):
                for slot in (2, 3):
                    tokens_here(slot, part)

        normalize_slot(2)
        normalize_slot(3)
        for t in range(3):
            project(t, 1)

    for z in range(4):

        @pl.when(jnp.logical_not(home & (s == z)))
        def _():
            share_done(z).wait_recv()

    def grad_copy(h, slot, q, peer):
        rows = pl.ds(pl.multiple_of(GROUP * q + HEAD_DIM * h, 64), HEAD_DIM)
        return remote(
            grads.at[h, slot],
            grad_proj.at[:, rows, :],
            g_send.at[h, slot],
            g_recv.at[h, q],
            peer,
        )

    def send_grads(h, slot):
        return grad_copy(h, slot, place, {"seq": blocks[slot], "weight": owner})

    for h in range(3):
        mine = pl.ds(pl.multiple_of(HEAD_DIM * core + HEAD_DIM * h, 64), HEAD_DIM)
        q_t, k_t, v_t = (projected[t, mine, :] for t in range(3))
        g_t = jnp.concatenate(
            [gathered[z, HEAD_DIM * h : HEAD_DIM * (h + 1), :] for z in blocks], axis=1
        )
        scores = jnp.dot(k_t.T, q_t, preferred_element_type=F32)
        dprob = jnp.dot(v_t.T, g_t, preferred_element_type=F32)
        expo = jnp.exp(scores - jnp.max(scores, axis=0, keepdims=True))
        probs = expo * (1.0 / jnp.sum(expo, axis=0, keepdims=True))
        delta = jnp.sum(probs * dprob, axis=0, keepdims=True)
        dscore = (probs * (dprob - delta)).astype(BF16)
        parts = (
            jnp.dot(k_t, dscore, preferred_element_type=F32) * HEAD_DIM ** (-0.5),
            lax.dot_general(q_t, dscore, NT, preferred_element_type=F32),
            lax.dot_general(g_t, probs.astype(BF16), NT, preferred_element_type=F32),
        )
        for t in range(3):
            value = parts[t].astype(BF16)
            for i in range(4):
                grads[h, i, t] = value[:, ROWS * i : ROWS * (i + 1)]
        for slot in (3, 2, 1):
            send_grads(h, slot).start()

        @pl.when(home)
        def _():
            own = pl.ds(pl.multiple_of(GROUP * place + HEAD_DIM * h, 64), HEAD_DIM)
            grad_proj[:, own, :] = grads[h, 0]

        @pl.when(jnp.logical_not(home))
        def _():
            send_grads(h, 0).start()

        from_x(3 + h)
        if h == 0:
            start_own(5)
        if h > 0:
            from_y(2 + h)
    from_y(5)
    for j in range(3, 6):
        weight_ready(j)

    def grads_ready(part):
        for h in range(3):
            for k in range(2):
                q = 2 * part + k

                @pl.when(jnp.logical_not(home & (place == q)))
                def _():
                    grad_copy(h, 0, q, {"weight": sibling}).wait_recv()

    def back(part):
        total = None
        for t in range(3):
            rows = pl.ds(pl.multiple_of(HALF * part, 128), HALF)
            cols = pl.ds(pl.multiple_of(768 * t + HALF * part, 128), HALF)
            term = lax.dot_general(
                grad_proj[t, rows, :].T, weight[:, cols], NT, preferred_element_type=F32
            )
            total = term if total is None else total + term
        return total

    grads_ready(1 - core)
    out_ref[0] = back(1 - core)
    grads_ready(core)
    grad_norm = out_ref[0] + back(core)
    out_ref[0] = norm_backward(grad_norm, normed_buf[...], inverse_buf[...], gain_ref[...][None])

    for j in range(6):
        x_copy(j, w).wait_send()
        own_copy(j, w).wait_send()
        y_copy(j, g).wait_send()
        passed_copy(j, across).wait_send()
    for part in range(PARTS):
        send_tokens(part).wait_send()

        @pl.when(home)
        def _():
            for slot in range(4):
                pass_tokens(slot, part).wait_send()

        @pl.when(home & inner)
        def _():
            for slot in (2, 3):
                forward_tokens(slot, part).wait_send()

    for q in range(4):

        @pl.when(jnp.logical_not(stays(q)))
        def _():
            share(q).wait_send()

    for h in range(3):
        for slot in (1, 2, 3):
            send_grads(h, slot).wait_send()

        @pl.when(jnp.logical_not(home))
        def _():
            send_grads(h, 0).wait_send()


def fused(
    tokens,
    upstream_grad,
    norm_gain,
    norm_bias,
    input_codes,
    input_scales,
    input_bias,
    output_codes,
    output_scales,
    layer_scale,
):
    hbm = pl.BlockSpec(memory_space=pltpu.HBM)
    vmem = pl.BlockSpec(memory_space=pltpu.VMEM)
    return pl.pallas_call(
        fused_kernel,
        out_shape=jax.ShapeDtypeStruct((1, ROWS, WIDTH), F32),
        in_specs=[hbm] * 10,
        out_specs=vmem,
        scratch_shapes=[
            pltpu.VMEM((WIDTH,), F32),
            pltpu.VMEM((WIDTH,), F32),
            pltpu.SMEM((3, 18), F32),
            pltpu.VMEM((3 * HD,), F32),
            pltpu.SMEM((6, 12), F32),
            pltpu.VMEM((WIDTH,), F32),
            pltpu.VMEM((WIDTH, 3 * HD), BF16),
            pltpu.VMEM((SHARD, 3 * HD), BF16),
            pltpu.VMEM((HD, WIDTH), BF16),
            pltpu.VMEM((HALF, WIDTH), BF16),
            pltpu.VMEM((ROWS, WIDTH), BF16),
            pltpu.VMEM((ROWS, WIDTH), BF16),
            pltpu.VMEM((ROWS, WIDTH), F32),
            pltpu.VMEM((ROWS, 1), F32),
            pltpu.VMEM((4, ROWS, WIDTH), BF16),
            pltpu.VMEM((4 * ROWS, WIDTH), BF16),
            pltpu.VMEM((ROWS, WIDTH), BF16),
            pltpu.VMEM((HD, ROWS), BF16),
            pltpu.VMEM((4, GROUP, ROWS), BF16),
            pltpu.VMEM((3, 256, 4 * ROWS), BF16),
            pltpu.VMEM((3, 4, 3, HEAD_DIM, ROWS), BF16),
            pltpu.VMEM((3, HD, ROWS), BF16),
            pltpu.SemaphoreType.DMA((10,)),
            pltpu.SemaphoreType.DMA((4, 6)),
            pltpu.SemaphoreType.DMA((4, 6)),
            pltpu.SemaphoreType.DMA((3, PARTS)),
            pltpu.SemaphoreType.DMA((4, PARTS)),
            pltpu.SemaphoreType.DMA((4, PARTS)),
            pltpu.SemaphoreType.DMA((4,)),
            pltpu.SemaphoreType.DMA((4,)),
            pltpu.SemaphoreType.DMA((3, 4)),
            pltpu.SemaphoreType.DMA((3, 4)),
        ],
        compiler_params=pltpu.CompilerParams(
            collective_id=0, has_side_effects=True, vmem_limit_bytes=64 * 1024 * 1024 - 65536
        ),
        cost_estimate=pl.CostEstimate(
            flops=2500000000, bytes_accessed=8000000, transcendentals=1000000
        ),
    )(
        tokens,
        upstream_grad,
        norm_gain,
        norm_bias,
        input_codes,
        input_scales,
        input_bias,
        output_codes,
        output_scales,
        layer_scale,
    )


def solution(mesh):
    in_specs = (
        P(("groups", "weight"), "seq", None),
        P(("groups", "weight"), "seq", None),
        P(),
        P(),
        P("weight", None),
        P("weight", None),
        P(),
        P(),
        P(),
        P(),
    )
    out_specs = P(("groups", "weight"), "seq", None)
    local = fused if fits(mesh) else general
    return jax.shard_map(local, mesh=mesh, in_specs=in_specs, out_specs=out_specs, check_vma=False)
```

```python
import functools
import math

import jax
import jax.numpy as jnp
from jax import lax
from jax.experimental import pallas as pl
from jax.experimental.pallas import tpu as pltpu
from jax.sharding import PartitionSpec as P

HEADS = 12
HEAD_DIM = 64
QBLOCK = 128
HD = 768


def dequantize(codes, scales):
    expanded = jnp.repeat(jnp.repeat(scales, QBLOCK, axis=0), QBLOCK, axis=1)
    return (codes.astype(jnp.float32) * expanded).astype(jnp.bfloat16)


def normalize(rows, gain, shift):
    mean_value = jnp.mean(rows, axis=-1, keepdims=True)
    centered = rows - mean_value
    variance = jnp.mean(centered * centered, axis=-1, keepdims=True)
    inverse = lax.rsqrt(variance + 1e-06)
    normed = centered * inverse
    return (normed, inverse, (normed * gain + shift).astype(jnp.bfloat16))


def norm_backward(grad_norm, normed, inverse, gain):
    grad_hat = grad_norm * gain
    first_mean = jnp.mean(grad_hat, axis=-1, keepdims=True)
    second_mean = jnp.mean(grad_hat * normed, axis=-1, keepdims=True)
    return inverse * (grad_hat - first_mean - normed * second_mean)


def score_block(queries, head_grads, pair_block):
    row_count = pair_block.shape[0]
    keys_blk = pair_block[:, :HD].reshape(row_count, HEADS, HEAD_DIM)
    values_blk = pair_block[:, HD:].reshape(row_count, HEADS, HEAD_DIM)
    scores = jnp.einsum(
        "qhd,khd->hqk", queries, keys_blk, preferred_element_type=jnp.float32
    ) * HEAD_DIM ** (-0.5)
    dprob = jnp.einsum("qhd,khd->hqk", head_grads, values_blk, preferred_element_type=jnp.float32)
    return (keys_blk, scores, dprob)


def update_stats(statistics, queries, head_grads, pair_rows):
    sub_size = math.gcd(pair_rows.shape[0], 512)

    def visit_block(block_index, running):
        run_max, run_total, run_mix = running
        pair_block = lax.dynamic_slice_in_dim(pair_rows, block_index * sub_size, sub_size, 0)
        keys_blk, scores, dprob = score_block(queries, head_grads, pair_block)
        new_max = jnp.maximum(run_max, jnp.max(scores, axis=-1))
        factor = jnp.exp(run_max - new_max)
        expo = jnp.exp(scores - new_max[..., None])
        return (
            new_max,
            run_total * factor + jnp.sum(expo, axis=-1),
            run_mix * factor + jnp.sum(expo * dprob, axis=-1),
        )

    return lax.fori_loop(0, pair_rows.shape[0] // sub_size, visit_block, statistics)


def block_backward(queries, head_grads, pair_block, log_total, row_delta):
    keys_blk, scores, dprob = score_block(queries, head_grads, pair_block)
    weights = jnp.exp(scores - log_total[..., None])
    prob_weights = weights.astype(jnp.bfloat16)
    dscore = (weights * (dprob - row_delta[..., None])).astype(jnp.bfloat16)
    return (keys_blk, prob_weights, dscore)


def key_terms_from(queries, head_grads, prob_weights, dscore):
    key_part = jnp.einsum(
        "hqk,qhd->khd", dscore, queries, preferred_element_type=jnp.float32
    ) * HEAD_DIM ** (-0.5)
    value_part = jnp.einsum(
        "hqk,qhd->khd", prob_weights, head_grads, preferred_element_type=jnp.float32
    )
    row_count = key_part.shape[0]
    return jnp.concatenate(
        [key_part.reshape(row_count, HD), value_part.reshape(row_count, HD)], axis=1
    )


def query_side(queries, head_grads, keys_values, local_rows):
    seq_rows = local_rows * lax.axis_size("seq")
    start_stats = (
        jnp.full((HEADS, local_rows), -1e30, jnp.float32),
        jnp.zeros((HEADS, local_rows), jnp.float32),
        jnp.zeros((HEADS, local_rows), jnp.float32),
    )
    all_pairs = lax.all_gather(keys_values, "seq", axis=0, tiled=True)
    statistics = update_stats(start_stats, queries, head_grads, all_pairs)
    row_max, row_total, row_mix = statistics
    log_total = row_max + jnp.log(row_total)
    row_delta = row_mix / row_total
    sub_size = math.gcd(seq_rows, 512)
    block_count = seq_rows // sub_size
    empty_query = jnp.zeros((local_rows, HEADS, HEAD_DIM), jnp.float32)

    def backward_step(block_index, running):
        query_grad, buffer = running
        pair_block = lax.dynamic_slice_in_dim(all_pairs, block_index * sub_size, sub_size, 0)
        keys_blk, prob_weights, dscore = block_backward(
            queries, head_grads, pair_block, log_total, row_delta
        )
        query_grad = query_grad + jnp.einsum(
            "hqk,khd->qhd", dscore, keys_blk, preferred_element_type=jnp.float32
        )
        block_terms = key_terms_from(queries, head_grads, prob_weights, dscore)
        buffer = lax.dynamic_update_slice_in_dim(buffer, block_terms, block_index * sub_size, 0)
        return (query_grad, buffer)

    empty_terms = jnp.zeros((seq_rows, 2 * HD), jnp.float32)
    query_grad, buffer = lax.fori_loop(0, block_count, backward_step, (empty_query, empty_terms))
    pair_grads = lax.psum_scatter(
        buffer.astype(jnp.bfloat16), "seq", scatter_dimension=0, tiled=True
    ).astype(jnp.float32)
    return (query_grad, pair_grads)


def general(
    tokens,
    upstream_grad,
    norm_gain,
    norm_bias,
    input_codes,
    input_scales,
    input_bias,
    output_codes,
    output_scales,
    layer_scale,
):
    all_codes, all_scales = (
        lax.all_gather(input_codes.astype(jnp.float32), "weight", axis=0, tiled=True).astype(
            input_codes.dtype
        ),
        lax.all_gather(input_scales, "weight", axis=0, tiled=True),
    )
    input_weight = dequantize(all_codes, all_scales)
    output_weight = dequantize(output_codes, output_scales)
    normed, inverse, norm_out = normalize(tokens[0].astype(jnp.float32), norm_gain, norm_bias)
    projected = (
        jnp.dot(norm_out, input_weight, preferred_element_type=jnp.float32) + input_bias
    ).astype(jnp.bfloat16)
    local_rows = projected.shape[0]
    queries = projected[:, :HD].reshape(local_rows, HEADS, HEAD_DIM)
    keys_values = projected[:, HD:]
    scaled_grad = (upstream_grad[0].astype(jnp.float32) * layer_scale).astype(jnp.bfloat16)
    head_grads = jnp.dot(scaled_grad, output_weight.T, preferred_element_type=jnp.float32).astype(
        jnp.bfloat16
    )
    head_grads = head_grads.reshape(local_rows, HEADS, HEAD_DIM)
    query_grad, pair_grads = query_side(queries, head_grads, keys_values, local_rows)
    query_grad = (query_grad * HEAD_DIM ** (-0.5)).reshape(local_rows, HD)
    grad_proj = jnp.concatenate([query_grad, pair_grads], axis=1).astype(jnp.bfloat16)
    grad_norm = jnp.dot(grad_proj, input_weight.T, preferred_element_type=jnp.float32)
    result = norm_backward(grad_norm, normed, inverse, norm_gain)
    return result[None]


WIDTH = 1536
ROWS = 128
SHARD = 384
HALF = 384
GROUP = 192
CHUNKS = ((0, 0, 192), (0, 192, 192), (1, 0, 192), (1, 192, 192), (2, 0, 192), (2, 192, 192))
CHUNKS += ((3, 0, 384), (4, 0, 384), (5, 0, 384))
PARTS = 4
PART = ROWS // PARTS
BF16 = jnp.bfloat16
F32 = jnp.float32
MESH = pl.DeviceIdType.MESH
NT = (((1,), (1,)), ((), ()))


def fits(mesh):
    return dict(mesh.shape) == {"groups": 2, "seq": 4, "weight": 4}


def fused_kernel(
    tokens_hbm,
    upstream_hbm,
    gain_hbm,
    norm_bias_hbm,
    codes_hbm,
    in_scales_hbm,
    in_bias_hbm,
    out_codes_hbm,
    out_scales_hbm,
    layer_scale_hbm,
    out_ref,
    gain_ref,
    norm_bias_ref,
    in_scales,
    in_bias_ref,
    out_scales,
    layer_scale_ref,
    weight,
    codes,
    out_codes,
    out_weight,
    tokens,
    upstream,
    normed_buf,
    inverse_buf,
    raw,
    norm_out,
    scaled,
    packed,
    gathered,
    projected,
    grads,
    grad_proj,
    load_sem,
    w_send,
    w_recv,
    t_send,
    p_send,
    t_recv,
    a_send,
    a_recv,
    g_send,
    g_recv,
):
    g = lax.axis_index("groups")
    s = lax.axis_index("seq")
    w = lax.axis_index("weight")
    core = lax.rem(w, 2)
    across = lax.rem(w + 2, 4)
    sibling = w + 1 - 2 * core
    far_sibling = lax.rem(sibling + 2, 4)
    side = s // 2
    half = lax.rem(s, 2)
    home = core == side
    inner = lax.rem(s + side, 2) == 1
    owner = w - core + side
    place = 2 * half + core
    blocks = (s, s + 1 - 2 * half, 2 - side, 3 - 3 * side)

    def load(index, source, target):
        copy = pltpu.make_async_copy(source, target, load_sem.at[index])
        copy.start()
        return copy

    load_in_scales = load(4, in_scales_hbm, in_scales)
    load_codes = load(0, codes_hbm, codes)
    load_upstream = load(2, upstream_hbm.at[0], upstream)
    load_out_codes = load(3, out_codes_hbm, out_codes)
    load_tokens = load(1, tokens_hbm.at[0], tokens)
    load_out_scales = load(5, out_scales_hbm, out_scales)
    load_layer_scale = load(6, layer_scale_hbm, layer_scale_ref)
    load_gain = load(7, gain_hbm, gain_ref)
    load_norm_bias = load(8, norm_bias_hbm, norm_bias_ref)
    load_in_bias = load(9, in_bias_hbm, in_bias_ref)

    barrier = pltpu.get_barrier_semaphore()
    peers = [{"weight": across}, {"weight": sibling}, {"groups": 1 - g}]
    for k in (1, 2, 3):
        peers.append({"seq": lax.rem(s + k, 4)})
        peers.append({"seq": lax.rem(s + k, 4), "weight": sibling})
    for peer in peers:
        pl.semaphore_signal(barrier, inc=1, device_id=peer, device_id_type=MESH)

    def remote(source, target, send, recv, peer):
        return pltpu.make_async_remote_copy(
            src_ref=source,
            dst_ref=target,
            send_sem=send,
            recv_sem=recv,
            device_id=peer,
            device_id_type=MESH,
        )

    def half_of(j):
        return half if j < 3 else 1 - half

    def columns_of(j):
        return pl.ds(pl.multiple_of(768 * (j % 3) + HALF * half_of(j), 128), HALF)

    def dequantize_chunk(j):
        first = 6 * (j % 3) + 3 * half_of(j)
        for rb in range(3):
            for cb in range(3):
                cols = pl.ds(pl.multiple_of(128 * (first + cb), 128), 128)
                rows = pl.ds(pl.multiple_of(SHARD * w + 128 * rb, 128), 128)
                block = codes[128 * rb : 128 * (rb + 1), cols].astype(F32)
                weight[rows, cols] = (block * in_scales[rb, first + cb]).astype(BF16)

    def weight_copy(kind, index, j, row, count, peer):
        part = weight.at[pl.ds(pl.multiple_of(row, 32), count), columns_of(j)]
        return remote(part, part, w_send.at[kind, index], w_recv.at[kind, index], peer)

    def x_copy(c, shard):
        j, first, count = CHUNKS[c]
        row = SHARD * shard + first + count // 2 * g
        return weight_copy(0, c, j, row, count // 2, {"weight": across})

    def y_copy(c, part):
        j, first, count = CHUNKS[c]
        row = SHARD * across + first + count // 2 * part
        return weight_copy(1, c, j, row, count // 2, {"groups": 1 - g})

    def own_copy(j, shard):
        return weight_copy(2, j, j, SHARD * shard, SHARD, {"weight": sibling})

    def passed_copy(c, shard):
        j, first, count = CHUNKS[c]
        return weight_copy(3, c, j, SHARD * shard + first, count, {"weight": sibling})

    def chunks_of(j):
        return [c for c in range(len(CHUNKS)) if CHUNKS[c][0] == j]

    def start_own(j):
        for c in chunks_of(j):
            x_copy(c, w).start()
        own_copy(j, w).start()

    def from_x(c):
        x_copy(c, across).wait_recv()
        y_copy(c, g).start()

    def from_y(c):
        y_copy(c, 1 - g).wait_recv()
        passed_copy(c, across).start()

    def weight_ready(j):
        own_copy(j, sibling).wait_recv()
        for c in chunks_of(j):
            passed_copy(c, far_sibling).wait_recv()

    def part_rows(part):
        return pl.ds(PART * part, PART)

    def send_tokens(part):
        dest = jnp.where(home & inner, 3 * core, 1 + core)
        return remote(
            tokens_hbm.at[0, part_rows(part)],
            raw.at[s, part_rows(part)],
            t_send.at[0, part],
            t_recv.at[s, part],
            {"seq": dest},
        )

    def forward_tokens(slot, part):
        z = blocks[slot]
        rows = raw.at[z, part_rows(part)]
        return remote(
            rows, rows, t_send.at[slot - 1, part], t_recv.at[z, part], {"seq": 3 * core}
        )

    def pass_tokens(slot, part):
        z = blocks[slot]
        rows = raw.at[z, part_rows(part)]
        source = tokens_hbm.at[0, part_rows(part)] if slot == 0 else rows
        return remote(source, rows, p_send.at[slot, part], t_recv.at[z, part], {"weight": sibling})

    def tokens_here(slot, part):
        pass_tokens(slot, part).wait_recv()

    def relay(slot, part, forward):
        tokens_here(slot, part)
        if forward:
            forward_tokens(slot, part).start()
        pass_tokens(slot, part).start()

    def share(q):
        peer = {"seq": 2 * core + q // 2, "weight": w - core + q % 2}
        return remote(
            packed.at[GROUP * q : GROUP * (q + 1), :],
            gathered.at[s],
            a_send.at[q],
            a_recv.at[s],
            peer,
        )

    def share_done(z):
        return remote(
            packed.at[0:GROUP, :],
            gathered.at[z],
            a_send.at[0],
            a_recv.at[z],
            {"weight": sibling},
        )

    def stays(q):
        return home & (place == q)

    def head_gradients(part):
        for rb in range(3):
            rows = slice(HALF * part + 128 * rb, HALF * part + 128 * (rb + 1))
            for cb in range(12):
                cols = slice(128 * cb, 128 * (cb + 1))
                block = out_codes[rows, cols].astype(F32)
                out_weight[128 * rb : 128 * (rb + 1), cols] = (
                    block * out_scales[3 * part + rb, cb]
                ).astype(BF16)
        value = lax.dot_general(out_weight[...], scaled[...], NT, preferred_element_type=F32)
        packed[HALF * part : HALF * (part + 1), :] = value.astype(BF16)
        for q in (2 * part, 2 * part + 1):

            @pl.when(jnp.logical_not(stays(q)))
            def _():
                share(q).start()

            @pl.when(stays(q))
            def _():
                gathered[s] = packed[GROUP * q : GROUP * (q + 1), :]

    def normalize_slot(slot):
        norm_out[ROWS * slot : ROWS * (slot + 1), :] = normalize(
            raw[blocks[slot]].astype(F32), gain_ref[...][None], norm_bias_ref[...][None]
        )[2]

    def project(t, pair):
        first = pl.multiple_of(768 * t + HALF * half + 128 * core, 128)
        value = jnp.dot(
            norm_out[256 * pair : 256 * (pair + 1), :],
            weight[:, pl.ds(first, 256)],
            preferred_element_type=F32,
        )
        value = value + in_bias_ref[pl.ds(first, 256)][None]
        if t == 0:
            value = value * HEAD_DIM ** (-0.5)
        projected[t, :, 256 * pair : 256 * (pair + 1)] = value.T.astype(BF16)

    load_in_scales.wait()
    load_codes.wait()
    dequantize_chunk(0)
    pl.semaphore_wait(barrier, len(peers))
    for part in range(PARTS):
        send_tokens(part).start()
    start_own(0)

    @pl.when(home)
    def _():
        for part in range(PARTS):
            pass_tokens(0, part).start()

    for j in range(1, 6):
        dequantize_chunk(j)
        start_own(j)

    load_layer_scale.wait()
    load_upstream.wait()
    scaled[...] = (upstream[...].astype(F32) * layer_scale_ref[...][None]).astype(BF16)
    load_out_scales.wait()
    load_out_codes.wait()
    head_gradients(0)
    head_gradients(1)

    load_gain.wait()
    load_norm_bias.wait()
    load_in_bias.wait()
    load_tokens.wait()
    normed, inverse, rounded = normalize(
        tokens[...].astype(F32), gain_ref[...][None], norm_bias_ref[...][None]
    )
    normed_buf[...] = normed
    inverse_buf[...] = inverse

    @pl.when(home)
    def _():
        norm_out[0:ROWS, :] = rounded

    def relay_inner(part):
        @pl.when(home & inner)
        def _():
            relay(2, part, True)
            relay(3, part, True)

        @pl.when(home)
        def _():
            relay(1, part, False)

    def relay_outer(part):
        @pl.when(home & jnp.logical_not(inner))
        def _():
            relay(2, part, False)
            relay(3, part, False)

    def await_tokens(slots):
        @pl.when(jnp.logical_not(home))
        def _():
            for part in range(PARTS):
                for slot in slots:
                    tokens_here(slot, part)

    from_x(0)
    relay_inner(0)
    from_x(1)
    relay_inner(1)
    from_x(2)
    from_y(0)
    relay_outer(0)
    relay_inner(2)
    from_x(3)
    from_y(1)
    relay_outer(1)
    from_x(4)
    relay_inner(3)
    from_y(2)
    await_tokens((0, 1))

    @pl.when(jnp.logical_not(home))
    def _():
        normalize_slot(0)

    normalize_slot(1)
    from_x(5)
    from_y(3)
    relay_outer(2)
    weight_ready(0)
    project(0, 0)

    @pl.when(inner)
    def _():
        await_tokens((2, 3))
        normalize_slot(2)
        normalize_slot(3)
        project(0, 1)

    from_y(4)
    relay_outer(3)
    weight_ready(1)
    project(1, 0)
    from_y(5)

    @pl.when(jnp.logical_not(inner))
    def _():
        await_tokens((2, 3))
        normalize_slot(2)
        normalize_slot(3)
        project(0, 1)

    project(1, 1)
    from_x(6)
    weight_ready(2)
    project(2, 0)
    project(2, 1)

    for z in range(4):

        @pl.when(jnp.logical_not(home & (s == z)))
        def _():
            share_done(z).wait_recv()

    def grad_copy(h, slot, q, peer):
        rows = pl.ds(pl.multiple_of(GROUP * q + HEAD_DIM * h, 64), HEAD_DIM)
        return remote(
            grads.at[h, slot],
            grad_proj.at[:, rows, :],
            g_send.at[h, slot],
            g_recv.at[h, q],
            peer,
        )

    def send_grads(h, slot):
        return grad_copy(h, slot, place, {"seq": blocks[slot], "weight": owner})

    for h in range(3):
        mine = pl.ds(pl.multiple_of(HEAD_DIM * core + HEAD_DIM * h, 64), HEAD_DIM)
        q_t, k_t, v_t = (projected[t, mine, :] for t in range(3))
        g_t = jnp.concatenate(
            [gathered[z, HEAD_DIM * h : HEAD_DIM * (h + 1), :] for z in blocks], axis=1
        )
        scores = jnp.dot(k_t.T, q_t, preferred_element_type=F32)
        dprob = jnp.dot(v_t.T, g_t, preferred_element_type=F32)
        expo = jnp.exp(scores - jnp.max(scores, axis=0, keepdims=True))
        probs = expo * (1.0 / jnp.sum(expo, axis=0, keepdims=True))
        delta = jnp.sum(probs * dprob, axis=0, keepdims=True)
        dscore = (probs * (dprob - delta)).astype(BF16)
        parts = (
            jnp.dot(k_t, dscore, preferred_element_type=F32) * HEAD_DIM ** (-0.5),
            lax.dot_general(q_t, dscore, NT, preferred_element_type=F32),
            lax.dot_general(g_t, probs.astype(BF16), NT, preferred_element_type=F32),
        )
        for t in range(3):
            value = parts[t].astype(BF16)
            for i in range(4):
                grads[h, i, t] = value[:, ROWS * i : ROWS * (i + 1)]
        for slot in (3, 2, 1):
            send_grads(h, slot).start()

        @pl.when(home)
        def _():
            own = pl.ds(pl.multiple_of(GROUP * place + HEAD_DIM * h, 64), HEAD_DIM)
            grad_proj[:, own, :] = grads[h, 0]

        @pl.when(jnp.logical_not(home))
        def _():
            send_grads(h, 0).start()

        if h == 0:
            from_x(7)
        if h == 1:
            from_y(6)
            from_x(8)
    from_y(7)
    from_y(8)
    for j in range(3, 6):
        weight_ready(j)

    def grads_ready(part):
        for h in range(3):
            for k in range(2):
                q = 2 * part + k

                @pl.when(jnp.logical_not(home & (place == q)))
                def _():
                    grad_copy(h, 0, q, {"weight": sibling}).wait_recv()

    def back(part):
        total = None
        for t in range(3):
            rows = pl.ds(pl.multiple_of(HALF * part, 128), HALF)
            cols = pl.ds(pl.multiple_of(768 * t + HALF * part, 128), HALF)
            term = lax.dot_general(
                grad_proj[t, rows, :].T, weight[:, cols], NT, preferred_element_type=F32
            )
            total = term if total is None else total + term
        return total

    grads_ready(1 - core)
    out_ref[0] = back(1 - core)
    grads_ready(core)
    grad_norm = out_ref[0] + back(core)
    out_ref[0] = norm_backward(grad_norm, normed_buf[...], inverse_buf[...], gain_ref[...][None])

    for c in range(len(CHUNKS)):
        x_copy(c, w).wait_send()
        y_copy(c, g).wait_send()
        passed_copy(c, across).wait_send()
    for j in range(6):
        own_copy(j, w).wait_send()
    for part in range(PARTS):
        send_tokens(part).wait_send()

        @pl.when(home)
        def _():
            for slot in range(4):
                pass_tokens(slot, part).wait_send()

        @pl.when(home & inner)
        def _():
            for slot in (2, 3):
                forward_tokens(slot, part).wait_send()

    for q in range(4):

        @pl.when(jnp.logical_not(stays(q)))
        def _():
            share(q).wait_send()

    for h in range(3):
        for slot in (1, 2, 3):
            send_grads(h, slot).wait_send()

        @pl.when(jnp.logical_not(home))
        def _():
            send_grads(h, 0).wait_send()


def fused(
    tokens,
    upstream_grad,
    norm_gain,
    norm_bias,
    input_codes,
    input_scales,
    input_bias,
    output_codes,
    output_scales,
    layer_scale,
):
    hbm = pl.BlockSpec(memory_space=pltpu.HBM)
    vmem = pl.BlockSpec(memory_space=pltpu.VMEM)
    return pl.pallas_call(
        fused_kernel,
        out_shape=jax.ShapeDtypeStruct((1, ROWS, WIDTH), F32),
        in_specs=[hbm] * 10,
        out_specs=vmem,
        scratch_shapes=[
            pltpu.VMEM((WIDTH,), F32),
            pltpu.VMEM((WIDTH,), F32),
            pltpu.SMEM((3, 18), F32),
            pltpu.VMEM((3 * HD,), F32),
            pltpu.SMEM((6, 12), F32),
            pltpu.VMEM((WIDTH,), F32),
            pltpu.VMEM((WIDTH, 3 * HD), BF16),
            pltpu.VMEM((SHARD, 3 * HD), BF16),
            pltpu.VMEM((HD, WIDTH), BF16),
            pltpu.VMEM((HALF, WIDTH), BF16),
            pltpu.VMEM((ROWS, WIDTH), BF16),
            pltpu.VMEM((ROWS, WIDTH), BF16),
            pltpu.VMEM((ROWS, WIDTH), F32),
            pltpu.VMEM((ROWS, 1), F32),
            pltpu.VMEM((4, ROWS, WIDTH), BF16),
            pltpu.VMEM((4 * ROWS, WIDTH), BF16),
            pltpu.VMEM((ROWS, WIDTH), BF16),
            pltpu.VMEM((HD, ROWS), BF16),
            pltpu.VMEM((4, GROUP, ROWS), BF16),
            pltpu.VMEM((3, 256, 4 * ROWS), BF16),
            pltpu.VMEM((3, 4, 3, HEAD_DIM, ROWS), BF16),
            pltpu.VMEM((3, HD, ROWS), BF16),
            pltpu.SemaphoreType.DMA((10,)),
            pltpu.SemaphoreType.DMA((4, len(CHUNKS))),
            pltpu.SemaphoreType.DMA((4, len(CHUNKS))),
            pltpu.SemaphoreType.DMA((3, PARTS)),
            pltpu.SemaphoreType.DMA((4, PARTS)),
            pltpu.SemaphoreType.DMA((4, PARTS)),
            pltpu.SemaphoreType.DMA((4,)),
            pltpu.SemaphoreType.DMA((4,)),
            pltpu.SemaphoreType.DMA((3, 4)),
            pltpu.SemaphoreType.DMA((3, 4)),
        ],
        compiler_params=pltpu.CompilerParams(
            collective_id=0, has_side_effects=True, vmem_limit_bytes=64 * 1024 * 1024 - 65536
        ),
        cost_estimate=pl.CostEstimate(
            flops=2500000000, bytes_accessed=8000000, transcendentals=1000000
        ),
    )(
        tokens,
        upstream_grad,
        norm_gain,
        norm_bias,
        input_codes,
        input_scales,
        input_bias,
        output_codes,
        output_scales,
        layer_scale,
    )


def solution(mesh):
    in_specs = (
        P(("groups", "weight"), "seq", None),
        P(("groups", "weight"), "seq", None),
        P(),
        P(),
        P("weight", None),
        P("weight", None),
        P(),
        P(),
        P(),
        P(),
    )
    out_specs = P(("groups", "weight"), "seq", None)
    local = fused if fits(mesh) else general
    return jax.shard_map(local, mesh=mesh, in_specs=in_specs, out_specs=out_specs, check_vma=False)
```

```python
import functools
import math

import jax
import jax.numpy as jnp
from jax import lax
from jax.experimental import pallas as pl
from jax.experimental.pallas import tpu as pltpu
from jax.sharding import PartitionSpec as P

HEADS = 12
HEAD_DIM = 64
QBLOCK = 128
HD = 768


def dequantize(codes, scales):
    expanded = jnp.repeat(jnp.repeat(scales, QBLOCK, axis=0), QBLOCK, axis=1)
    return (codes.astype(jnp.float32) * expanded).astype(jnp.bfloat16)


def normalize(rows, gain, shift):
    mean_value = jnp.mean(rows, axis=-1, keepdims=True)
    centered = rows - mean_value
    variance = jnp.mean(centered * centered, axis=-1, keepdims=True)
    inverse = lax.rsqrt(variance + 1e-06)
    normed = centered * inverse
    return (normed, inverse, (normed * gain + shift).astype(jnp.bfloat16))


def norm_backward(grad_norm, normed, inverse, gain):
    grad_hat = grad_norm * gain
    first_mean = jnp.mean(grad_hat, axis=-1, keepdims=True)
    second_mean = jnp.mean(grad_hat * normed, axis=-1, keepdims=True)
    return inverse * (grad_hat - first_mean - normed * second_mean)


def score_block(queries, head_grads, pair_block):
    row_count = pair_block.shape[0]
    keys_blk = pair_block[:, :HD].reshape(row_count, HEADS, HEAD_DIM)
    values_blk = pair_block[:, HD:].reshape(row_count, HEADS, HEAD_DIM)
    scores = jnp.einsum(
        "qhd,khd->hqk", queries, keys_blk, preferred_element_type=jnp.float32
    ) * HEAD_DIM ** (-0.5)
    dprob = jnp.einsum("qhd,khd->hqk", head_grads, values_blk, preferred_element_type=jnp.float32)
    return (keys_blk, scores, dprob)


def update_stats(statistics, queries, head_grads, pair_rows):
    sub_size = math.gcd(pair_rows.shape[0], 512)

    def visit_block(block_index, running):
        run_max, run_total, run_mix = running
        pair_block = lax.dynamic_slice_in_dim(pair_rows, block_index * sub_size, sub_size, 0)
        keys_blk, scores, dprob = score_block(queries, head_grads, pair_block)
        new_max = jnp.maximum(run_max, jnp.max(scores, axis=-1))
        factor = jnp.exp(run_max - new_max)
        expo = jnp.exp(scores - new_max[..., None])
        return (
            new_max,
            run_total * factor + jnp.sum(expo, axis=-1),
            run_mix * factor + jnp.sum(expo * dprob, axis=-1),
        )

    return lax.fori_loop(0, pair_rows.shape[0] // sub_size, visit_block, statistics)


def block_backward(queries, head_grads, pair_block, log_total, row_delta):
    keys_blk, scores, dprob = score_block(queries, head_grads, pair_block)
    weights = jnp.exp(scores - log_total[..., None])
    prob_weights = weights.astype(jnp.bfloat16)
    dscore = (weights * (dprob - row_delta[..., None])).astype(jnp.bfloat16)
    return (keys_blk, prob_weights, dscore)


def key_terms_from(queries, head_grads, prob_weights, dscore):
    key_part = jnp.einsum(
        "hqk,qhd->khd", dscore, queries, preferred_element_type=jnp.float32
    ) * HEAD_DIM ** (-0.5)
    value_part = jnp.einsum(
        "hqk,qhd->khd", prob_weights, head_grads, preferred_element_type=jnp.float32
    )
    row_count = key_part.shape[0]
    return jnp.concatenate(
        [key_part.reshape(row_count, HD), value_part.reshape(row_count, HD)], axis=1
    )


def query_side(queries, head_grads, keys_values, local_rows):
    seq_rows = local_rows * lax.axis_size("seq")
    start_stats = (
        jnp.full((HEADS, local_rows), -1e30, jnp.float32),
        jnp.zeros((HEADS, local_rows), jnp.float32),
        jnp.zeros((HEADS, local_rows), jnp.float32),
    )
    all_pairs = lax.all_gather(keys_values, "seq", axis=0, tiled=True)
    statistics = update_stats(start_stats, queries, head_grads, all_pairs)
    row_max, row_total, row_mix = statistics
    log_total = row_max + jnp.log(row_total)
    row_delta = row_mix / row_total
    sub_size = math.gcd(seq_rows, 512)
    block_count = seq_rows // sub_size
    empty_query = jnp.zeros((local_rows, HEADS, HEAD_DIM), jnp.float32)

    def backward_step(block_index, running):
        query_grad, buffer = running
        pair_block = lax.dynamic_slice_in_dim(all_pairs, block_index * sub_size, sub_size, 0)
        keys_blk, prob_weights, dscore = block_backward(
            queries, head_grads, pair_block, log_total, row_delta
        )
        query_grad = query_grad + jnp.einsum(
            "hqk,khd->qhd", dscore, keys_blk, preferred_element_type=jnp.float32
        )
        block_terms = key_terms_from(queries, head_grads, prob_weights, dscore)
        buffer = lax.dynamic_update_slice_in_dim(buffer, block_terms, block_index * sub_size, 0)
        return (query_grad, buffer)

    empty_terms = jnp.zeros((seq_rows, 2 * HD), jnp.float32)
    query_grad, buffer = lax.fori_loop(0, block_count, backward_step, (empty_query, empty_terms))
    pair_grads = lax.psum_scatter(
        buffer.astype(jnp.bfloat16), "seq", scatter_dimension=0, tiled=True
    ).astype(jnp.float32)
    return (query_grad, pair_grads)


def general(
    tokens,
    upstream_grad,
    norm_gain,
    norm_bias,
    input_codes,
    input_scales,
    input_bias,
    output_codes,
    output_scales,
    layer_scale,
):
    all_codes, all_scales = (
        lax.all_gather(input_codes.astype(jnp.float32), "weight", axis=0, tiled=True).astype(
            input_codes.dtype
        ),
        lax.all_gather(input_scales, "weight", axis=0, tiled=True),
    )
    input_weight = dequantize(all_codes, all_scales)
    output_weight = dequantize(output_codes, output_scales)
    normed, inverse, norm_out = normalize(tokens[0].astype(jnp.float32), norm_gain, norm_bias)
    projected = (
        jnp.dot(norm_out, input_weight, preferred_element_type=jnp.float32) + input_bias
    ).astype(jnp.bfloat16)
    local_rows = projected.shape[0]
    queries = projected[:, :HD].reshape(local_rows, HEADS, HEAD_DIM)
    keys_values = projected[:, HD:]
    scaled_grad = (upstream_grad[0].astype(jnp.float32) * layer_scale).astype(jnp.bfloat16)
    head_grads = jnp.dot(scaled_grad, output_weight.T, preferred_element_type=jnp.float32).astype(
        jnp.bfloat16
    )
    head_grads = head_grads.reshape(local_rows, HEADS, HEAD_DIM)
    query_grad, pair_grads = query_side(queries, head_grads, keys_values, local_rows)
    query_grad = (query_grad * HEAD_DIM ** (-0.5)).reshape(local_rows, HD)
    grad_proj = jnp.concatenate([query_grad, pair_grads], axis=1).astype(jnp.bfloat16)
    grad_norm = jnp.dot(grad_proj, input_weight.T, preferred_element_type=jnp.float32)
    result = norm_backward(grad_norm, normed, inverse, norm_gain)
    return result[None]


WIDTH = 1536
ROWS = 128
SHARD = 384
HALF = 384
CHUNKS = tuple((p, 192 * r) for p in range(6) for r in range(2))
CHUNK = 192
BLOCK = 128
PARTS = 4
PART = ROWS // PARTS
BF16 = jnp.bfloat16
F32 = jnp.float32
MESH = pl.DeviceIdType.MESH
NT = (((1,), (1,)), ((), ()))


def fits(mesh):
    return dict(mesh.shape) == {"groups": 2, "seq": 4, "weight": 4}


def fused_kernel(
    tokens_hbm,
    upstream_hbm,
    gain_hbm,
    norm_bias_hbm,
    codes_hbm,
    in_scales_hbm,
    in_bias_hbm,
    out_codes_hbm,
    out_scales_hbm,
    layer_scale_hbm,
    out_ref,
    gain_ref,
    norm_bias_ref,
    in_scales,
    in_bias_ref,
    out_scales,
    layer_scale_ref,
    weight,
    codes,
    out_codes,
    out_weight,
    tokens,
    upstream,
    normed_buf,
    inverse_buf,
    raw,
    norm_out,
    scaled,
    packed,
    gathered,
    projected,
    grads,
    grad_proj,
    load_sem,
    w_send,
    w_recv,
    t_send,
    p_send,
    t_recv,
    a_send,
    a_recv,
    g_send,
    g_recv,
):
    g = lax.axis_index("groups")
    s = lax.axis_index("seq")
    w = lax.axis_index("weight")
    core = lax.rem(w, 2)
    across = lax.rem(w + 2, 4)
    sibling = w + 1 - 2 * core
    far_sibling = lax.rem(sibling + 2, 4)
    side = s // 2
    home = core == side
    inner = lax.rem(s + side, 2) == 1
    outer = jnp.logical_not(inner)
    away = jnp.logical_not(home)
    owner = w - core + side
    blocks = (s, s + 1 - 2 * lax.rem(s, 2), 2 - side, 3 - 3 * side)

    def load(index, source, target):
        copy = pltpu.make_async_copy(source, target, load_sem.at[index])
        copy.start()
        return copy

    load_in_scales = load(4, in_scales_hbm, in_scales)
    load_codes = load(0, codes_hbm, codes)
    load_upstream = load(2, upstream_hbm.at[0], upstream)
    load_out_codes = load(3, out_codes_hbm, out_codes)
    load_tokens = load(1, tokens_hbm.at[0], tokens)
    load_out_scales = load(5, out_scales_hbm, out_scales)
    load_layer_scale = load(6, layer_scale_hbm, layer_scale_ref)
    load_gain = load(7, gain_hbm, gain_ref)
    load_norm_bias = load(8, norm_bias_hbm, norm_bias_ref)
    load_in_bias = load(9, in_bias_hbm, in_bias_ref)

    barrier = pltpu.get_barrier_semaphore()
    peers = [{"weight": across}, {"weight": sibling}, {"groups": 1 - g}]
    for k in (1, 2, 3):
        peers.append({"seq": lax.rem(s + k, 4)})
        peers.append({"seq": lax.rem(s + k, 4), "weight": sibling})
    for peer in peers:
        pl.semaphore_signal(barrier, inc=1, device_id=peer, device_id_type=MESH)

    def remote(source, target, send, recv, peer):
        return pltpu.make_async_remote_copy(
            src_ref=source,
            dst_ref=target,
            send_sem=send,
            recv_sem=recv,
            device_id=peer,
            device_id_type=MESH,
        )

    def block_at(p):
        return jnp.where(inner, p, lax.rem(p + 4, 6))

    def lanes(first):
        return pl.ds(pl.multiple_of(first, BLOCK), BLOCK)

    def dequantize_block(p):
        b = block_at(p)
        for t in range(3):
            for rb in range(3):
                rows = pl.ds(pl.multiple_of(SHARD * w + 128 * rb, 128), 128)
                block = codes[128 * rb : 128 * (rb + 1), lanes(HD * t + BLOCK * b)].astype(F32)
                weight[t, rows, lanes(BLOCK * b)] = (block * in_scales[rb, 6 * t + b]).astype(BF16)

    def weight_copy(kind, index, p, row, count, peer):
        rows = pl.ds(pl.multiple_of(row, 32), count)
        part = weight.at[:, rows, lanes(BLOCK * block_at(p))]
        return remote(part, part, w_send.at[kind, index], w_recv.at[kind, index], peer)

    def x_copy(c, shard):
        p, first = CHUNKS[c]
        row = SHARD * shard + first + CHUNK // 2 * g
        return weight_copy(0, c, p, row, CHUNK // 2, {"weight": across})

    def y_copy(c, part):
        p, first = CHUNKS[c]
        row = SHARD * across + first + CHUNK // 2 * part
        return weight_copy(1, c, p, row, CHUNK // 2, {"groups": 1 - g})

    def own_copy(p, shard):
        return weight_copy(2, p, p, SHARD * shard, SHARD, {"weight": sibling})

    def passed_copy(c, shard):
        p, first = CHUNKS[c]
        return weight_copy(3, c, p, SHARD * shard + first, CHUNK, {"weight": sibling})

    def start_own(p):
        for r in range(2):
            x_copy(2 * p + r, w).start()
        own_copy(p, w).start()

    def from_x(c):
        x_copy(c, across).wait_recv()
        y_copy(c, g).start()

    def from_y(c):
        y_copy(c, 1 - g).wait_recv()
        passed_copy(c, across).start()

    def weight_ready(p):
        own_copy(p, sibling).wait_recv()
        for r in range(2):
            row = SHARD * far_sibling + CHUNK * r
            weight_copy(3, 2 * p + r, p, row, CHUNK, {"weight": sibling}).wait_recv()

    def part_rows(part):
        return pl.ds(PART * part, PART)

    def send_tokens(part):
        dest = jnp.where(home & inner, 3 * core, 1 + core)
        return remote(
            tokens_hbm.at[0, part_rows(part)],
            raw.at[s, part_rows(part)],
            t_send.at[0, part],
            t_recv.at[s, part],
            {"seq": dest},
        )

    def forward_tokens(slot, part):
        z = blocks[slot]
        rows = raw.at[z, part_rows(part)]
        return remote(
            rows, rows, t_send.at[slot - 1, part], t_recv.at[z, part], {"seq": 3 * core}
        )

    def pass_tokens(slot, part):
        z = blocks[slot]
        rows = raw.at[z, part_rows(part)]
        source = tokens_hbm.at[0, part_rows(part)] if slot == 0 else rows
        return remote(source, rows, p_send.at[slot, part], t_recv.at[z, part], {"weight": sibling})

    def tokens_here(slot, part):
        pass_tokens(slot, part).wait_recv()

    def relay(slot, part, forward):
        tokens_here(slot, part)
        if forward:
            forward_tokens(slot, part).start()
        pass_tokens(slot, part).start()

    def share(d):
        count = 256 if d < 2 else 128
        first = 256 * d if d < 2 else 256 + 128 * d
        rows = packed.at[first : first + count, :]
        peer = {"seq": 1 + core if d < 2 else 3 * core, "weight": w - core + d % 2}
        return remote(rows, gathered.at[s, 0:count, :], a_send.at[d], a_recv.at[s], peer)

    def share_done(z, count):
        return remote(
            packed.at[0:count, :],
            gathered.at[z, 0:count, :],
            a_send.at[0],
            a_recv.at[z],
            {"weight": sibling},
        )

    def stays(d):
        return home & (inner if d < 2 else outer) & (core == d % 2)

    def head_gradients(part):
        for rb in range(3):
            rows = slice(HALF * part + 128 * rb, HALF * part + 128 * (rb + 1))
            for cb in range(12):
                cols = slice(128 * cb, 128 * (cb + 1))
                block = out_codes[rows, cols].astype(F32)
                out_weight[128 * rb : 128 * (rb + 1), cols] = (
                    block * out_scales[3 * part + rb, cb]
                ).astype(BF16)
        value = lax.dot_general(out_weight[...], scaled[...], NT, preferred_element_type=F32)
        value = value.astype(BF16)
        for rb in range(3):
            place = (0, 2, 1, 3, 4, 5)[3 * part + rb]
            packed[BLOCK * place : BLOCK * (place + 1), :] = value[128 * rb : 128 * (rb + 1), :]

    def share_all():
        for d in range(4):
            count = 256 if d < 2 else 128
            first = 256 * d if d < 2 else 256 + 128 * d

            @pl.when(jnp.logical_not(stays(d)))
            def _():
                share(d).start()

            @pl.when(stays(d))
            def _():
                gathered[s, 0:count, :] = packed[first : first + count, :]

    def normalize_slot(slot):
        norm_out[ROWS * slot : ROWS * (slot + 1), :] = normalize(
            raw[blocks[slot]].astype(F32), gain_ref[...][None], norm_bias_ref[...][None]
        )[2]

    def project(n, first, count):
        b = block_at(2 * n + core)
        columns = jnp.concatenate([weight[t, :, lanes(BLOCK * b)] for t in range(3)], axis=1)
        value = jnp.dot(norm_out[first : first + count, :], columns, preferred_element_type=F32)
        for t in range(3):
            part = value[:, BLOCK * t : BLOCK * (t + 1)]
            part = part + in_bias_ref[lanes(HD * t + BLOCK * b)][None]
            if t == 0:
                part = part * HEAD_DIM ** (-0.5)
            projected[n, t, :, first : first + count] = part.T.astype(BF16)

    pl.semaphore_wait(barrier, len(peers))

    @pl.when(inner | home)
    def _():
        for part in range(PARTS):
            send_tokens(part).start()

    load_in_scales.wait()
    load_codes.wait()
    dequantize_block(0)
    start_own(0)

    @pl.when(home)
    def _():
        for part in range(PARTS):
            pass_tokens(0, part).start()

    for p in range(1, 6):
        dequantize_block(p)
        start_own(p)

    load_layer_scale.wait()
    load_upstream.wait()
    scaled[...] = (upstream[...].astype(F32) * layer_scale_ref[...][None]).astype(BF16)
    load_out_scales.wait()
    load_out_codes.wait()
    head_gradients(0)
    head_gradients(1)

    @pl.when(outer & away)
    def _():
        for part in range(PARTS):
            send_tokens(part).start()

    share_all()

    load_gain.wait()
    load_norm_bias.wait()
    load_in_bias.wait()
    load_tokens.wait()
    normed, inverse, rounded = normalize(
        tokens[...].astype(F32), gain_ref[...][None], norm_bias_ref[...][None]
    )
    normed_buf[...] = normed
    inverse_buf[...] = inverse

    @pl.when(home)
    def _():
        norm_out[0:ROWS, :] = rounded

    def relay_inner(slot, *parts):
        @pl.when(home & inner)
        def _():
            for part in parts:
                relay(slot, part, slot > 1)

    def relay_outer(slot, *parts):
        @pl.when(home & outer)
        def _():
            for part in parts:
                relay(slot, part, False)

    def await_tokens(*slots):
        @pl.when(away)
        def _():
            for slot in slots:
                for part in range(PARTS):
                    tokens_here(slot, part)

    relay_inner(2, 0, 1)
    from_x(0)
    relay_outer(1, 0, 1)
    relay_inner(2, 2)
    relay_inner(1, 0, 1)
    from_x(1)
    relay_outer(1, 2, 3)
    from_x(2)
    relay_inner(2, 3)
    relay_inner(3, 0)
    from_y(0)
    relay_inner(3, 1)
    relay_outer(2, 0)
    from_x(3)
    from_y(1)
    relay_inner(1, 2, 3)
    relay_outer(2, 1)
    relay_inner(3, 2)
    from_x(4)
    from_y(2)
    relay_outer(2, 2, 3)
    relay_inner(3, 3)
    await_tokens(0, 1)

    @pl.when(away)
    def _():
        normalize_slot(0)

    normalize_slot(1)
    from_x(5)
    from_y(3)
    relay_outer(3, 0)
    await_tokens(2)
    normalize_slot(2)
    from_x(6)
    from_y(4)
    relay_outer(3, 1)
    weight_ready(core)
    project(0, 0, 3 * ROWS)
    from_x(7)
    from_y(5)
    relay_outer(3, 2, 3)
    await_tokens(3)
    normalize_slot(3)
    project(0, 3 * ROWS, ROWS)

    for z in range(4):

        @pl.when(jnp.logical_not(home & (s == z)) & inner)
        def _():
            share_done(z, 256).wait_recv()

        @pl.when(jnp.logical_not(home & (s == z)) & outer)
        def _():
            share_done(z, 128).wait_recv()

    def grad_copy(h, slot, b, peer):
        rows = pl.ds(pl.multiple_of(BLOCK * b + HEAD_DIM * (h % 2), 64), HEAD_DIM)
        return remote(
            grads.at[h, slot],
            grad_proj.at[:, rows, :],
            g_send.at[h, slot],
            g_recv.at[2 * b + h % 2],
            peer,
        )

    def send_grads(h, slot):
        b = block_at(h // 2 * 2 + core)
        return grad_copy(h, slot, b, {"seq": blocks[slot], "weight": owner})

    def attend(h):
        n, i = h // 2, h % 2
        rows = slice(HEAD_DIM * i, HEAD_DIM * (i + 1))
        q_t, k_t, v_t = (projected[n, t, rows, :] for t in range(3))
        g_rows = slice(HEAD_DIM * h, HEAD_DIM * (h + 1))
        g_t = jnp.concatenate([gathered[z, g_rows, :] for z in blocks], axis=1)
        scores = jnp.dot(k_t.T, q_t, preferred_element_type=F32)
        dprob = jnp.dot(v_t.T, g_t, preferred_element_type=F32)
        expo = jnp.exp(scores - jnp.max(scores, axis=0, keepdims=True))
        probs = expo * (1.0 / jnp.sum(expo, axis=0, keepdims=True))
        delta = jnp.sum(probs * dprob, axis=0, keepdims=True)
        dscore = (probs * (dprob - delta)).astype(BF16)
        parts = (
            jnp.dot(k_t, dscore, preferred_element_type=F32) * HEAD_DIM ** (-0.5),
            lax.dot_general(q_t, dscore, NT, preferred_element_type=F32),
            lax.dot_general(g_t, probs.astype(BF16), NT, preferred_element_type=F32),
        )
        for t in range(3):
            value = parts[t].astype(BF16)
            for slot in range(4):
                grads[h, slot, t] = value[:, ROWS * slot : ROWS * (slot + 1)]
        for slot in (3, 2, 1):
            send_grads(h, slot).start()

        @pl.when(home)
        def _():
            first = BLOCK * block_at(2 * n + core) + HEAD_DIM * i
            own = pl.ds(pl.multiple_of(first, 64), HEAD_DIM)
            grad_proj[:, own, :] = grads[h, 0]

        @pl.when(away)
        def _():
            send_grads(h, 0).start()

    attend(0)
    from_x(8)
    from_y(6)
    attend(1)
    from_x(9)
    from_y(7)
    from_x(10)
    from_y(8)

    @pl.when(inner)
    def _():
        weight_ready(2 + core)
        project(1, 0, 4 * ROWS)
        attend(2)
        from_x(11)
        from_y(9)
        attend(3)

    @pl.when(outer)
    def _():
        from_x(11)
        from_y(9)
        weight_ready(2 + core)

    from_y(10)
    from_y(11)
    weight_ready(1 - core)
    weight_ready(3 - core)
    weight_ready(4)
    weight_ready(5)

    def grads_ready(first, count):
        for b in range(first, first + count):
            mine = home & (inner if b < 4 else outer) & (core == b % 2)
            for i in range(2):

                @pl.when(jnp.logical_not(mine))
                def _():
                    grad_copy(i, 0, b, {"weight": sibling}).wait_recv()

    def back(first, count):
        total = None
        part = slice(BLOCK * first, BLOCK * (first + count))
        for t in range(3):
            term = lax.dot_general(
                grad_proj[t, part, :].T, weight[t, :, part], NT, preferred_element_type=F32
            )
            total = term if total is None else total + term
        return total

    grads_ready(0, 4)
    out_ref[0] = back(0, 4)
    grads_ready(4, 2)
    grad_norm = out_ref[0] + back(4, 2)
    out_ref[0] = norm_backward(grad_norm, normed_buf[...], inverse_buf[...], gain_ref[...][None])

    for c in range(len(CHUNKS)):
        x_copy(c, w).wait_send()
        y_copy(c, g).wait_send()
        passed_copy(c, across).wait_send()
    for p in range(6):
        own_copy(p, w).wait_send()
    for part in range(PARTS):
        send_tokens(part).wait_send()

        @pl.when(home)
        def _():
            for slot in range(4):
                pass_tokens(slot, part).wait_send()

        @pl.when(home & inner)
        def _():
            for slot in (2, 3):
                forward_tokens(slot, part).wait_send()

    for d in range(4):

        @pl.when(jnp.logical_not(stays(d)))
        def _():
            share(d).wait_send()

    def grads_sent(heads):
        for h in heads:
            for slot in (1, 2, 3):
                send_grads(h, slot).wait_send()

            @pl.when(away)
            def _():
                send_grads(h, 0).wait_send()

    grads_sent((0, 1))

    @pl.when(inner)
    def _():
        grads_sent((2, 3))


def fused(
    tokens,
    upstream_grad,
    norm_gain,
    norm_bias,
    input_codes,
    input_scales,
    input_bias,
    output_codes,
    output_scales,
    layer_scale,
):
    hbm = pl.BlockSpec(memory_space=pltpu.HBM)
    vmem = pl.BlockSpec(memory_space=pltpu.VMEM)
    return pl.pallas_call(
        fused_kernel,
        out_shape=jax.ShapeDtypeStruct((1, ROWS, WIDTH), F32),
        in_specs=[hbm] * 10,
        out_specs=vmem,
        scratch_shapes=[
            pltpu.VMEM((WIDTH,), F32),
            pltpu.VMEM((WIDTH,), F32),
            pltpu.SMEM((3, 18), F32),
            pltpu.VMEM((3 * HD,), F32),
            pltpu.SMEM((6, 12), F32),
            pltpu.VMEM((WIDTH,), F32),
            pltpu.VMEM((3, WIDTH, HD), BF16),
            pltpu.VMEM((SHARD, 3 * HD), BF16),
            pltpu.VMEM((HD, WIDTH), BF16),
            pltpu.VMEM((HALF, WIDTH), BF16),
            pltpu.VMEM((ROWS, WIDTH), BF16),
            pltpu.VMEM((ROWS, WIDTH), BF16),
            pltpu.VMEM((ROWS, WIDTH), F32),
            pltpu.VMEM((ROWS, 1), F32),
            pltpu.VMEM((4, ROWS, WIDTH), BF16),
            pltpu.VMEM((4 * ROWS, WIDTH), BF16),
            pltpu.VMEM((ROWS, WIDTH), BF16),
            pltpu.VMEM((HD, ROWS), BF16),
            pltpu.VMEM((4, 2 * BLOCK, ROWS), BF16),
            pltpu.VMEM((2, 3, BLOCK, 4 * ROWS), BF16),
            pltpu.VMEM((4, 4, 3, HEAD_DIM, ROWS), BF16),
            pltpu.VMEM((3, HD, ROWS), BF16),
            pltpu.SemaphoreType.DMA((10,)),
            pltpu.SemaphoreType.DMA((4, len(CHUNKS))),
            pltpu.SemaphoreType.DMA((4, len(CHUNKS))),
            pltpu.SemaphoreType.DMA((3, PARTS)),
            pltpu.SemaphoreType.DMA((4, PARTS)),
            pltpu.SemaphoreType.DMA((4, PARTS)),
            pltpu.SemaphoreType.DMA((4,)),
            pltpu.SemaphoreType.DMA((4,)),
            pltpu.SemaphoreType.DMA((4, 4)),
            pltpu.SemaphoreType.DMA((12,)),
        ],
        compiler_params=pltpu.CompilerParams(
            collective_id=0, has_side_effects=True, vmem_limit_bytes=64 * 1024 * 1024 - 65536
        ),
        cost_estimate=pl.CostEstimate(
            flops=2500000000, bytes_accessed=8000000, transcendentals=1000000
        ),
    )(
        tokens,
        upstream_grad,
        norm_gain,
        norm_bias,
        input_codes,
        input_scales,
        input_bias,
        output_codes,
        output_scales,
        layer_scale,
    )


def solution(mesh):
    in_specs = (
        P(("groups", "weight"), "seq", None),
        P(("groups", "weight"), "seq", None),
        P(),
        P(),
        P("weight", None),
        P("weight", None),
        P(),
        P(),
        P(),
        P(),
    )
    out_specs = P(("groups", "weight"), "seq", None)
    local = fused if fits(mesh) else general
    return jax.shard_map(local, mesh=mesh, in_specs=in_specs, out_specs=out_specs, check_vma=False)
```

```python
import functools
import math

import jax
import jax.numpy as jnp
from jax import lax
from jax.experimental import pallas as pl
from jax.experimental.pallas import tpu as pltpu
from jax.sharding import PartitionSpec as P

HEADS = 12
HEAD_DIM = 64
QBLOCK = 128
HD = 768


def dequantize(codes, scales):
    expanded = jnp.repeat(jnp.repeat(scales, QBLOCK, axis=0), QBLOCK, axis=1)
    return (codes.astype(jnp.float32) * expanded).astype(jnp.bfloat16)


def normalize(rows, gain, shift):
    mean_value = jnp.mean(rows, axis=-1, keepdims=True)
    centered = rows - mean_value
    variance = jnp.mean(centered * centered, axis=-1, keepdims=True)
    inverse = lax.rsqrt(variance + 1e-06)
    normed = centered * inverse
    return (normed, inverse, (normed * gain + shift).astype(jnp.bfloat16))


def norm_backward(grad_norm, normed, inverse, gain):
    grad_hat = grad_norm * gain
    first_mean = jnp.mean(grad_hat, axis=-1, keepdims=True)
    second_mean = jnp.mean(grad_hat * normed, axis=-1, keepdims=True)
    return inverse * (grad_hat - first_mean - normed * second_mean)


def score_block(queries, head_grads, pair_block):
    row_count = pair_block.shape[0]
    keys_blk = pair_block[:, :HD].reshape(row_count, HEADS, HEAD_DIM)
    values_blk = pair_block[:, HD:].reshape(row_count, HEADS, HEAD_DIM)
    scores = jnp.einsum(
        "qhd,khd->hqk", queries, keys_blk, preferred_element_type=jnp.float32
    ) * HEAD_DIM ** (-0.5)
    dprob = jnp.einsum("qhd,khd->hqk", head_grads, values_blk, preferred_element_type=jnp.float32)
    return (keys_blk, scores, dprob)


def update_stats(statistics, queries, head_grads, pair_rows):
    sub_size = math.gcd(pair_rows.shape[0], 512)

    def visit_block(block_index, running):
        run_max, run_total, run_mix = running
        pair_block = lax.dynamic_slice_in_dim(pair_rows, block_index * sub_size, sub_size, 0)
        keys_blk, scores, dprob = score_block(queries, head_grads, pair_block)
        new_max = jnp.maximum(run_max, jnp.max(scores, axis=-1))
        factor = jnp.exp(run_max - new_max)
        expo = jnp.exp(scores - new_max[..., None])
        return (
            new_max,
            run_total * factor + jnp.sum(expo, axis=-1),
            run_mix * factor + jnp.sum(expo * dprob, axis=-1),
        )

    return lax.fori_loop(0, pair_rows.shape[0] // sub_size, visit_block, statistics)


def block_backward(queries, head_grads, pair_block, log_total, row_delta):
    keys_blk, scores, dprob = score_block(queries, head_grads, pair_block)
    weights = jnp.exp(scores - log_total[..., None])
    prob_weights = weights.astype(jnp.bfloat16)
    dscore = (weights * (dprob - row_delta[..., None])).astype(jnp.bfloat16)
    return (keys_blk, prob_weights, dscore)


def key_terms_from(queries, head_grads, prob_weights, dscore):
    key_part = jnp.einsum(
        "hqk,qhd->khd", dscore, queries, preferred_element_type=jnp.float32
    ) * HEAD_DIM ** (-0.5)
    value_part = jnp.einsum(
        "hqk,qhd->khd", prob_weights, head_grads, preferred_element_type=jnp.float32
    )
    row_count = key_part.shape[0]
    return jnp.concatenate(
        [key_part.reshape(row_count, HD), value_part.reshape(row_count, HD)], axis=1
    )


def query_side(queries, head_grads, keys_values, local_rows):
    seq_rows = local_rows * lax.axis_size("seq")
    start_stats = (
        jnp.full((HEADS, local_rows), -1e30, jnp.float32),
        jnp.zeros((HEADS, local_rows), jnp.float32),
        jnp.zeros((HEADS, local_rows), jnp.float32),
    )
    all_pairs = lax.all_gather(keys_values, "seq", axis=0, tiled=True)
    statistics = update_stats(start_stats, queries, head_grads, all_pairs)
    row_max, row_total, row_mix = statistics
    log_total = row_max + jnp.log(row_total)
    row_delta = row_mix / row_total
    sub_size = math.gcd(seq_rows, 512)
    block_count = seq_rows // sub_size
    empty_query = jnp.zeros((local_rows, HEADS, HEAD_DIM), jnp.float32)

    def backward_step(block_index, running):
        query_grad, buffer = running
        pair_block = lax.dynamic_slice_in_dim(all_pairs, block_index * sub_size, sub_size, 0)
        keys_blk, prob_weights, dscore = block_backward(
            queries, head_grads, pair_block, log_total, row_delta
        )
        query_grad = query_grad + jnp.einsum(
            "hqk,khd->qhd", dscore, keys_blk, preferred_element_type=jnp.float32
        )
        block_terms = key_terms_from(queries, head_grads, prob_weights, dscore)
        buffer = lax.dynamic_update_slice_in_dim(buffer, block_terms, block_index * sub_size, 0)
        return (query_grad, buffer)

    empty_terms = jnp.zeros((seq_rows, 2 * HD), jnp.float32)
    query_grad, buffer = lax.fori_loop(0, block_count, backward_step, (empty_query, empty_terms))
    pair_grads = lax.psum_scatter(
        buffer.astype(jnp.bfloat16), "seq", scatter_dimension=0, tiled=True
    ).astype(jnp.float32)
    return (query_grad, pair_grads)


def general(
    tokens,
    upstream_grad,
    norm_gain,
    norm_bias,
    input_codes,
    input_scales,
    input_bias,
    output_codes,
    output_scales,
    layer_scale,
):
    all_codes, all_scales = (
        lax.all_gather(input_codes.astype(jnp.float32), "weight", axis=0, tiled=True).astype(
            input_codes.dtype
        ),
        lax.all_gather(input_scales, "weight", axis=0, tiled=True),
    )
    input_weight = dequantize(all_codes, all_scales)
    output_weight = dequantize(output_codes, output_scales)
    normed, inverse, norm_out = normalize(tokens[0].astype(jnp.float32), norm_gain, norm_bias)
    projected = (
        jnp.dot(norm_out, input_weight, preferred_element_type=jnp.float32) + input_bias
    ).astype(jnp.bfloat16)
    local_rows = projected.shape[0]
    queries = projected[:, :HD].reshape(local_rows, HEADS, HEAD_DIM)
    keys_values = projected[:, HD:]
    scaled_grad = (upstream_grad[0].astype(jnp.float32) * layer_scale).astype(jnp.bfloat16)
    head_grads = jnp.dot(scaled_grad, output_weight.T, preferred_element_type=jnp.float32).astype(
        jnp.bfloat16
    )
    head_grads = head_grads.reshape(local_rows, HEADS, HEAD_DIM)
    query_grad, pair_grads = query_side(queries, head_grads, keys_values, local_rows)
    query_grad = (query_grad * HEAD_DIM ** (-0.5)).reshape(local_rows, HD)
    grad_proj = jnp.concatenate([query_grad, pair_grads], axis=1).astype(jnp.bfloat16)
    grad_norm = jnp.dot(grad_proj, input_weight.T, preferred_element_type=jnp.float32)
    result = norm_backward(grad_norm, normed, inverse, norm_gain)
    return result[None]


WIDTH = 1536
ROWS = 128
SHARD = 384
HALF = 384
CHUNKS = tuple((p, 192 * r) for p in range(6) for r in range(2))
CHUNK = 192
BLOCK = 128
PARTS = 4
PART = ROWS // PARTS
BF16 = jnp.bfloat16
F32 = jnp.float32
MESH = pl.DeviceIdType.MESH
NT = (((1,), (1,)), ((), ()))


def fits(mesh):
    return dict(mesh.shape) == {"groups": 2, "seq": 4, "weight": 4}


def fused_kernel(
    tokens_hbm,
    upstream_hbm,
    gain_hbm,
    norm_bias_hbm,
    codes_hbm,
    in_scales_hbm,
    in_bias_hbm,
    out_codes_hbm,
    out_scales_hbm,
    layer_scale_hbm,
    out_ref,
    gain_ref,
    norm_bias_ref,
    in_scales,
    in_bias_ref,
    out_scales,
    layer_scale_ref,
    weight,
    first_codes,
    codes,
    out_codes,
    out_weight,
    tokens,
    upstream,
    normed_buf,
    inverse_buf,
    raw,
    norm_out,
    scaled,
    packed,
    gathered,
    projected,
    grads,
    grad_proj,
    load_sem,
    w_send,
    w_recv,
    t_send,
    p_send,
    t_recv,
    a_send,
    a_recv,
    g_send,
    g_recv,
):
    g = lax.axis_index("groups")
    s = lax.axis_index("seq")
    w = lax.axis_index("weight")
    core = lax.rem(w, 2)
    across = lax.rem(w + 2, 4)
    sibling = w + 1 - 2 * core
    far_sibling = lax.rem(sibling + 2, 4)
    side = s // 2
    home = core == side
    inner = lax.rem(s + side, 2) == 1
    outer = jnp.logical_not(inner)
    away = jnp.logical_not(home)
    owner = w - core + side
    blocks = (s, s + 1 - 2 * lax.rem(s, 2), 2 - side, 3 - 3 * side)

    def block_at(p):
        return jnp.where(inner, p, lax.rem(p + 4, 6))

    def lanes(first):
        return pl.ds(pl.multiple_of(first, BLOCK), BLOCK)

    def load(index, source, target):
        copy = pltpu.make_async_copy(source, target, load_sem.at[index])
        copy.start()
        return copy

    load_in_scales = load(4, in_scales_hbm, in_scales)
    load_first = [
        load(10 + t, codes_hbm.at[:, lanes(HD * t + BLOCK * block_at(0))], first_codes.at[t])
        for t in range(3)
    ]
    load_codes = load(0, codes_hbm, codes)
    load_upstream = load(2, upstream_hbm.at[0], upstream)
    load_out_codes = load(3, out_codes_hbm, out_codes)
    load_tokens = load(1, tokens_hbm.at[0], tokens)
    load_out_scales = load(5, out_scales_hbm, out_scales)
    load_layer_scale = load(6, layer_scale_hbm, layer_scale_ref)
    load_gain = load(7, gain_hbm, gain_ref)
    load_norm_bias = load(8, norm_bias_hbm, norm_bias_ref)
    load_in_bias = load(9, in_bias_hbm, in_bias_ref)

    barrier = pltpu.get_barrier_semaphore()
    peers = [{"weight": across}, {"weight": sibling}, {"groups": 1 - g}]
    for k in (1, 2, 3):
        peers.append({"seq": lax.rem(s + k, 4)})
        peers.append({"seq": lax.rem(s + k, 4), "weight": sibling})
    for peer in peers:
        pl.semaphore_signal(barrier, inc=1, device_id=peer, device_id_type=MESH)

    def remote(source, target, send, recv, peer):
        return pltpu.make_async_remote_copy(
            src_ref=source,
            dst_ref=target,
            send_sem=send,
            recv_sem=recv,
            device_id=peer,
            device_id_type=MESH,
        )

    def dequantize_block(p):
        b = block_at(p)
        for t in range(3):
            for rb in range(3):
                rows = pl.ds(pl.multiple_of(SHARD * w + 128 * rb, 128), 128)
                if p == 0:
                    block = first_codes[t, 128 * rb : 128 * (rb + 1), :]
                else:
                    block = codes[128 * rb : 128 * (rb + 1), lanes(HD * t + BLOCK * b)]
                block = block.astype(F32)
                weight[t, rows, lanes(BLOCK * b)] = (block * in_scales[rb, 6 * t + b]).astype(BF16)

    def weight_copy(kind, index, p, row, count, peer):
        rows = pl.ds(pl.multiple_of(row, 32), count)
        part = weight.at[:, rows, lanes(BLOCK * block_at(p))]
        return remote(part, part, w_send.at[kind, index], w_recv.at[kind, index], peer)

    def x_copy(c, shard):
        p, first = CHUNKS[c]
        row = SHARD * shard + first + CHUNK // 2 * g
        return weight_copy(0, c, p, row, CHUNK // 2, {"weight": across})

    def y_copy(c, part):
        p, first = CHUNKS[c]
        row = SHARD * across + first + CHUNK // 2 * part
        return weight_copy(1, c, p, row, CHUNK // 2, {"groups": 1 - g})

    def own_copy(p, shard):
        return weight_copy(2, p, p, SHARD * shard, SHARD, {"weight": sibling})

    def passed_copy(c, shard):
        p, first = CHUNKS[c]
        return weight_copy(3, c, p, SHARD * shard + first, CHUNK, {"weight": sibling})

    def start_own(p):
        for r in range(2):
            x_copy(2 * p + r, w).start()
        own_copy(p, w).start()

    def from_x(c):
        x_copy(c, across).wait_recv()
        y_copy(c, g).start()

    def from_y(c):
        y_copy(c, 1 - g).wait_recv()
        passed_copy(c, across).start()

    def weight_ready(p):
        own_copy(p, sibling).wait_recv()
        for r in range(2):
            row = SHARD * far_sibling + CHUNK * r
            weight_copy(3, 2 * p + r, p, row, CHUNK, {"weight": sibling}).wait_recv()

    def part_rows(part):
        return pl.ds(PART * part, PART)

    def send_tokens(part):
        dest = jnp.where(home & inner, 3 * core, 1 + core)
        return remote(
            tokens_hbm.at[0, part_rows(part)],
            raw.at[s, part_rows(part)],
            t_send.at[0, part],
            t_recv.at[s, part],
            {"seq": dest},
        )

    def forward_tokens(slot, part):
        z = blocks[slot]
        rows = raw.at[z, part_rows(part)]
        return remote(
            rows, rows, t_send.at[slot - 1, part], t_recv.at[z, part], {"seq": 3 * core}
        )

    def pass_tokens(slot, part):
        z = blocks[slot]
        rows = raw.at[z, part_rows(part)]
        source = tokens_hbm.at[0, part_rows(part)] if slot == 0 else rows
        return remote(source, rows, p_send.at[slot, part], t_recv.at[z, part], {"weight": sibling})

    def tokens_here(slot, part):
        pass_tokens(slot, part).wait_recv()

    def relay(slot, part, forward):
        tokens_here(slot, part)
        if forward:
            forward_tokens(slot, part).start()
        pass_tokens(slot, part).start()

    def share(d):
        count = 256 if d < 2 else 128
        first = 256 * d if d < 2 else 256 + 128 * d
        rows = packed.at[first : first + count, :]
        peer = {"seq": 1 + core if d < 2 else 3 * core, "weight": w - core + d % 2}
        return remote(rows, gathered.at[s, 0:count, :], a_send.at[d], a_recv.at[s], peer)

    def share_done(z, count):
        return remote(
            packed.at[0:count, :],
            gathered.at[z, 0:count, :],
            a_send.at[0],
            a_recv.at[z],
            {"weight": sibling},
        )

    def stays(d):
        return home & (inner if d < 2 else outer) & (core == d % 2)

    def head_gradients(part):
        for rb in range(3):
            rows = slice(HALF * part + 128 * rb, HALF * part + 128 * (rb + 1))
            for cb in range(12):
                cols = slice(128 * cb, 128 * (cb + 1))
                block = out_codes[rows, cols].astype(F32)
                out_weight[128 * rb : 128 * (rb + 1), cols] = (
                    block * out_scales[3 * part + rb, cb]
                ).astype(BF16)
        value = lax.dot_general(out_weight[...], scaled[...], NT, preferred_element_type=F32)
        value = value.astype(BF16)
        for rb in range(3):
            place = (0, 2, 1, 3, 4, 5)[3 * part + rb]
            packed[BLOCK * place : BLOCK * (place + 1), :] = value[128 * rb : 128 * (rb + 1), :]

    def share_all():
        for d in range(4):
            count = 256 if d < 2 else 128
            first = 256 * d if d < 2 else 256 + 128 * d

            @pl.when(jnp.logical_not(stays(d)))
            def _():
                share(d).start()

            @pl.when(stays(d))
            def _():
                gathered[s, 0:count, :] = packed[first : first + count, :]

    def normalize_slot(slot):
        norm_out[ROWS * slot : ROWS * (slot + 1), :] = normalize(
            raw[blocks[slot]].astype(F32), gain_ref[...][None], norm_bias_ref[...][None]
        )[2]

    def project(n, first, count):
        b = block_at(2 * n + core)
        columns = jnp.concatenate([weight[t, :, lanes(BLOCK * b)] for t in range(3)], axis=1)
        value = jnp.dot(norm_out[first : first + count, :], columns, preferred_element_type=F32)
        for t in range(3):
            part = value[:, BLOCK * t : BLOCK * (t + 1)]
            part = part + in_bias_ref[lanes(HD * t + BLOCK * b)][None]
            if t == 0:
                part = part * HEAD_DIM ** (-0.5)
            projected[n, t, :, first : first + count] = part.T.astype(BF16)

    load_in_scales.wait()
    for copy in load_first:
        copy.wait()
    dequantize_block(0)
    pl.semaphore_wait(barrier, len(peers))

    @pl.when(inner | home)
    def _():
        for part in range(PARTS):
            send_tokens(part).start()

    start_own(0)

    @pl.when(home)
    def _():
        for part in range(PARTS):
            pass_tokens(0, part).start()

    load_codes.wait()
    for p in range(1, 6):
        dequantize_block(p)
        start_own(p)

    load_layer_scale.wait()
    load_upstream.wait()
    scaled[...] = (upstream[...].astype(F32) * layer_scale_ref[...][None]).astype(BF16)
    load_out_scales.wait()
    load_out_codes.wait()
    head_gradients(0)
    head_gradients(1)

    @pl.when(outer & away)
    def _():
        for part in range(PARTS):
            send_tokens(part).start()

    share_all()

    load_gain.wait()
    load_norm_bias.wait()
    load_in_bias.wait()
    load_tokens.wait()
    normed, inverse, rounded = normalize(
        tokens[...].astype(F32), gain_ref[...][None], norm_bias_ref[...][None]
    )
    normed_buf[...] = normed
    inverse_buf[...] = inverse

    @pl.when(home)
    def _():
        norm_out[0:ROWS, :] = rounded

    def relay_inner(slot, *parts):
        @pl.when(home & inner)
        def _():
            for part in parts:
                relay(slot, part, slot > 1)

    def relay_outer(slot, *parts):
        @pl.when(home & outer)
        def _():
            for part in parts:
                relay(slot, part, False)

    def await_tokens(*slots):
        @pl.when(away)
        def _():
            for slot in slots:
                for part in range(PARTS):
                    tokens_here(slot, part)

    relay_inner(2, 0, 1)
    from_x(0)
    relay_outer(1, 0, 1)
    relay_inner(2, 2)
    relay_inner(1, 0, 1)
    from_x(1)
    relay_outer(1, 2, 3)
    from_x(2)
    relay_inner(2, 3)
    relay_inner(3, 0)
    from_y(0)
    relay_inner(3, 1)
    relay_outer(2, 0)
    from_x(3)
    from_y(1)
    relay_inner(1, 2, 3)
    relay_outer(2, 1)
    relay_inner(3, 2)
    from_x(4)
    relay_outer(2, 2)
    relay_inner(3, 3)
    from_y(2)
    relay_outer(2, 3)
    @pl.when(away)
    def _():
        for slot in (0, 1):
            for part in range(PARTS):
                tokens_here(slot, part)
        normalize_slot(0)

    normalize_slot(1)

    def shared(count):
        for z in range(4):

            @pl.when(jnp.logical_not(home & (s == z)))
            def _():
                share_done(z, count).wait_recv()

    def grad_copy(h, slot, b, peer):
        rows = pl.ds(pl.multiple_of(BLOCK * b + HEAD_DIM * (h % 2), 64), HEAD_DIM)
        return remote(
            grads.at[h, slot],
            grad_proj.at[:, rows, :],
            g_send.at[h, slot],
            g_recv.at[2 * b + h % 2],
            peer,
        )

    def send_grads(h, slot):
        b = block_at(h // 2 * 2 + core)
        return grad_copy(h, slot, b, {"seq": blocks[slot], "weight": owner})

    def attend(h):
        n, i = h // 2, h % 2
        rows = slice(HEAD_DIM * i, HEAD_DIM * (i + 1))
        q_t, k_t, v_t = (projected[n, t, rows, :] for t in range(3))
        g_rows = slice(HEAD_DIM * h, HEAD_DIM * (h + 1))
        g_t = jnp.concatenate([gathered[z, g_rows, :] for z in blocks], axis=1)
        scores = jnp.dot(k_t.T, q_t, preferred_element_type=F32)
        dprob = jnp.dot(v_t.T, g_t, preferred_element_type=F32)
        expo = jnp.exp(scores - jnp.max(scores, axis=0, keepdims=True))
        probs = expo * (1.0 / jnp.sum(expo, axis=0, keepdims=True))
        delta = jnp.sum(probs * dprob, axis=0, keepdims=True)
        dscore = (probs * (dprob - delta)).astype(BF16)
        parts = (
            jnp.dot(k_t, dscore, preferred_element_type=F32) * HEAD_DIM ** (-0.5),
            lax.dot_general(q_t, dscore, NT, preferred_element_type=F32),
            lax.dot_general(g_t, probs.astype(BF16), NT, preferred_element_type=F32),
        )
        for t in range(3):
            value = parts[t].astype(BF16)
            for slot in range(4):
                grads[h, slot, t] = value[:, ROWS * slot : ROWS * (slot + 1)]
        for slot in (3, 2, 1):
            send_grads(h, slot).start()

        @pl.when(home)
        def _():
            first = BLOCK * block_at(2 * n + core) + HEAD_DIM * i
            own = pl.ds(pl.multiple_of(first, 64), HEAD_DIM)
            grad_proj[:, own, :] = grads[h, 0]

        @pl.when(away)
        def _():
            send_grads(h, 0).start()

    @pl.when(inner)
    def _():
        await_tokens(2, 3)
        normalize_slot(2)
        normalize_slot(3)
        from_x(5)
        from_y(3)
        from_x(6)
        weight_ready(core)
        project(0, 0, 4 * ROWS)
        shared(256)

        @pl.when(core == 1)
        def _():
            from_x(7)

        attend(0)

        @pl.when(core == 0)
        def _():
            from_x(7)

        from_y(4)
        attend(1)
        from_x(8)
        from_y(5)
        from_x(9)
        from_y(6)

        @pl.when(core == 0)
        def _():
            weight_ready(2)
            project(1, 0, 4 * ROWS)

        from_x(10)
        from_y(7)

        @pl.when(core == 1)
        def _():
            weight_ready(3)
            project(1, 0, 4 * ROWS)

        attend(2)
        from_x(11)
        from_y(8)
        attend(3)

    @pl.when(outer)
    def _():
        from_x(5)
        relay_outer(3, 0)
        await_tokens(2)
        normalize_slot(2)
        from_y(3)
        from_x(6)
        relay_outer(3, 1)
        weight_ready(core)
        project(0, 0, 3 * ROWS)
        from_x(7)
        from_y(4)
        relay_outer(3, 2)
        from_x(8)
        from_y(5)
        relay_outer(3, 3)
        await_tokens(3)
        normalize_slot(3)
        project(0, 3 * ROWS, ROWS)
        shared(128)
        from_x(9)
        attend(0)
        from_x(10)
        from_y(6)
        attend(1)
        from_x(11)
        from_y(7)
        from_y(8)

    from_y(9)

    def grads_ready(first, count):
        for b in range(first, first + count):
            mine = home & (inner if b < 4 else outer) & (core == b % 2)
            for i in range(2):

                @pl.when(jnp.logical_not(mine))
                def _():
                    grad_copy(i, 0, b, {"weight": sibling}).wait_recv()

    def back(first, count):
        total = None
        part = slice(BLOCK * first, BLOCK * (first + count))
        for t in range(3):
            term = lax.dot_general(
                grad_proj[t, part, :].T, weight[t, :, part], NT, preferred_element_type=F32
            )
            total = term if total is None else total + term
        return total

    @pl.when(inner)
    def _():
        weight_ready(1 - core)

    @pl.when(outer)
    def _():
        weight_ready(2)
        weight_ready(3)

    from_y(10)
    from_y(11)
    grads_ready(0, 2)
    out_ref[0] = back(0, 2)

    @pl.when(inner)
    def _():
        weight_ready(4)
        weight_ready(5)

    @pl.when(outer)
    def _():
        weight_ready(1 - core)

    grads_ready(4, 2)
    out_ref[0] += back(4, 2)

    @pl.when(inner)
    def _():
        weight_ready(3 - core)

    @pl.when(outer)
    def _():
        weight_ready(4)
        weight_ready(5)

    grads_ready(2, 1)
    out_ref[0] += back(2, 1)
    grads_ready(3, 1)
    grad_norm = out_ref[0] + back(3, 1)
    out_ref[0] = norm_backward(grad_norm, normed_buf[...], inverse_buf[...], gain_ref[...][None])

    for c in range(len(CHUNKS)):
        x_copy(c, w).wait_send()
        y_copy(c, g).wait_send()
        passed_copy(c, across).wait_send()
    for p in range(6):
        own_copy(p, w).wait_send()
    for part in range(PARTS):
        send_tokens(part).wait_send()

        @pl.when(home)
        def _():
            for slot in range(4):
                pass_tokens(slot, part).wait_send()

        @pl.when(home & inner)
        def _():
            for slot in (2, 3):
                forward_tokens(slot, part).wait_send()

    for d in range(4):

        @pl.when(jnp.logical_not(stays(d)))
        def _():
            share(d).wait_send()

    def grads_sent(heads):
        for h in heads:
            for slot in (1, 2, 3):
                send_grads(h, slot).wait_send()

            @pl.when(away)
            def _():
                send_grads(h, 0).wait_send()

    grads_sent((0, 1))

    @pl.when(inner)
    def _():
        grads_sent((2, 3))


def fused(
    tokens,
    upstream_grad,
    norm_gain,
    norm_bias,
    input_codes,
    input_scales,
    input_bias,
    output_codes,
    output_scales,
    layer_scale,
):
    hbm = pl.BlockSpec(memory_space=pltpu.HBM)
    vmem = pl.BlockSpec(memory_space=pltpu.VMEM)
    return pl.pallas_call(
        fused_kernel,
        out_shape=jax.ShapeDtypeStruct((1, ROWS, WIDTH), F32),
        in_specs=[hbm] * 10,
        out_specs=vmem,
        scratch_shapes=[
            pltpu.VMEM((WIDTH,), F32),
            pltpu.VMEM((WIDTH,), F32),
            pltpu.SMEM((3, 18), F32),
            pltpu.VMEM((3 * HD,), F32),
            pltpu.SMEM((6, 12), F32),
            pltpu.VMEM((WIDTH,), F32),
            pltpu.VMEM((3, WIDTH, HD), BF16),
            pltpu.VMEM((3, SHARD, BLOCK), BF16),
            pltpu.VMEM((SHARD, 3 * HD), BF16),
            pltpu.VMEM((HD, WIDTH), BF16),
            pltpu.VMEM((HALF, WIDTH), BF16),
            pltpu.VMEM((ROWS, WIDTH), BF16),
            pltpu.VMEM((ROWS, WIDTH), BF16),
            pltpu.VMEM((ROWS, WIDTH), F32),
            pltpu.VMEM((ROWS, 1), F32),
            pltpu.VMEM((4, ROWS, WIDTH), BF16),
            pltpu.VMEM((4 * ROWS, WIDTH), BF16),
            pltpu.VMEM((ROWS, WIDTH), BF16),
            pltpu.VMEM((HD, ROWS), BF16),
            pltpu.VMEM((4, 2 * BLOCK, ROWS), BF16),
            pltpu.VMEM((2, 3, BLOCK, 4 * ROWS), BF16),
            pltpu.VMEM((4, 4, 3, HEAD_DIM, ROWS), BF16),
            pltpu.VMEM((3, HD, ROWS), BF16),
            pltpu.SemaphoreType.DMA((13,)),
            pltpu.SemaphoreType.DMA((4, len(CHUNKS))),
            pltpu.SemaphoreType.DMA((4, len(CHUNKS))),
            pltpu.SemaphoreType.DMA((3, PARTS)),
            pltpu.SemaphoreType.DMA((4, PARTS)),
            pltpu.SemaphoreType.DMA((4, PARTS)),
            pltpu.SemaphoreType.DMA((4,)),
            pltpu.SemaphoreType.DMA((4,)),
            pltpu.SemaphoreType.DMA((4, 4)),
            pltpu.SemaphoreType.DMA((12,)),
        ],
        compiler_params=pltpu.CompilerParams(
            collective_id=0, has_side_effects=True, vmem_limit_bytes=64 * 1024 * 1024 - 65536
        ),
        cost_estimate=pl.CostEstimate(
            flops=2500000000, bytes_accessed=8000000, transcendentals=1000000
        ),
    )(
        tokens,
        upstream_grad,
        norm_gain,
        norm_bias,
        input_codes,
        input_scales,
        input_bias,
        output_codes,
        output_scales,
        layer_scale,
    )


def solution(mesh):
    in_specs = (
        P(("groups", "weight"), "seq", None),
        P(("groups", "weight"), "seq", None),
        P(),
        P(),
        P("weight", None),
        P("weight", None),
        P(),
        P(),
        P(),
        P(),
    )
    out_specs = P(("groups", "weight"), "seq", None)
    local = fused if fits(mesh) else general
    return jax.shard_map(local, mesh=mesh, in_specs=in_specs, out_specs=out_specs, check_vma=False)
```

```python
import functools
import math

import jax
import jax.numpy as jnp
from jax import lax
from jax.experimental import pallas as pl
from jax.experimental.pallas import tpu as pltpu
from jax.sharding import PartitionSpec as P

HEADS = 12
HEAD_DIM = 64
QBLOCK = 128
HD = 768


def dequantize(codes, scales):
    expanded = jnp.repeat(jnp.repeat(scales, QBLOCK, axis=0), QBLOCK, axis=1)
    return (codes.astype(jnp.float32) * expanded).astype(jnp.bfloat16)


def normalize(rows, gain, shift):
    mean_value = jnp.mean(rows, axis=-1, keepdims=True)
    centered = rows - mean_value
    variance = jnp.mean(centered * centered, axis=-1, keepdims=True)
    inverse = lax.rsqrt(variance + 1e-06)
    normed = centered * inverse
    return (normed, inverse, (normed * gain + shift).astype(jnp.bfloat16))


def norm_backward(grad_norm, normed, inverse, gain):
    grad_hat = grad_norm * gain
    first_mean = jnp.mean(grad_hat, axis=-1, keepdims=True)
    second_mean = jnp.mean(grad_hat * normed, axis=-1, keepdims=True)
    return inverse * (grad_hat - first_mean - normed * second_mean)


def score_block(queries, head_grads, pair_block):
    row_count = pair_block.shape[0]
    keys_blk = pair_block[:, :HD].reshape(row_count, HEADS, HEAD_DIM)
    values_blk = pair_block[:, HD:].reshape(row_count, HEADS, HEAD_DIM)
    scores = jnp.einsum(
        "qhd,khd->hqk", queries, keys_blk, preferred_element_type=jnp.float32
    ) * HEAD_DIM ** (-0.5)
    dprob = jnp.einsum("qhd,khd->hqk", head_grads, values_blk, preferred_element_type=jnp.float32)
    return (keys_blk, scores, dprob)


def update_stats(statistics, queries, head_grads, pair_rows):
    sub_size = math.gcd(pair_rows.shape[0], 512)

    def visit_block(block_index, running):
        run_max, run_total, run_mix = running
        pair_block = lax.dynamic_slice_in_dim(pair_rows, block_index * sub_size, sub_size, 0)
        keys_blk, scores, dprob = score_block(queries, head_grads, pair_block)
        new_max = jnp.maximum(run_max, jnp.max(scores, axis=-1))
        factor = jnp.exp(run_max - new_max)
        expo = jnp.exp(scores - new_max[..., None])
        return (
            new_max,
            run_total * factor + jnp.sum(expo, axis=-1),
            run_mix * factor + jnp.sum(expo * dprob, axis=-1),
        )

    return lax.fori_loop(0, pair_rows.shape[0] // sub_size, visit_block, statistics)


def block_backward(queries, head_grads, pair_block, log_total, row_delta):
    keys_blk, scores, dprob = score_block(queries, head_grads, pair_block)
    weights = jnp.exp(scores - log_total[..., None])
    prob_weights = weights.astype(jnp.bfloat16)
    dscore = (weights * (dprob - row_delta[..., None])).astype(jnp.bfloat16)
    return (keys_blk, prob_weights, dscore)


def key_terms_from(queries, head_grads, prob_weights, dscore):
    key_part = jnp.einsum(
        "hqk,qhd->khd", dscore, queries, preferred_element_type=jnp.float32
    ) * HEAD_DIM ** (-0.5)
    value_part = jnp.einsum(
        "hqk,qhd->khd", prob_weights, head_grads, preferred_element_type=jnp.float32
    )
    row_count = key_part.shape[0]
    return jnp.concatenate(
        [key_part.reshape(row_count, HD), value_part.reshape(row_count, HD)], axis=1
    )


def query_side(queries, head_grads, keys_values, local_rows):
    seq_rows = local_rows * lax.axis_size("seq")
    start_stats = (
        jnp.full((HEADS, local_rows), -1e30, jnp.float32),
        jnp.zeros((HEADS, local_rows), jnp.float32),
        jnp.zeros((HEADS, local_rows), jnp.float32),
    )
    all_pairs = lax.all_gather(keys_values, "seq", axis=0, tiled=True)
    statistics = update_stats(start_stats, queries, head_grads, all_pairs)
    row_max, row_total, row_mix = statistics
    log_total = row_max + jnp.log(row_total)
    row_delta = row_mix / row_total
    sub_size = math.gcd(seq_rows, 512)
    block_count = seq_rows // sub_size
    empty_query = jnp.zeros((local_rows, HEADS, HEAD_DIM), jnp.float32)

    def backward_step(block_index, running):
        query_grad, buffer = running
        pair_block = lax.dynamic_slice_in_dim(all_pairs, block_index * sub_size, sub_size, 0)
        keys_blk, prob_weights, dscore = block_backward(
            queries, head_grads, pair_block, log_total, row_delta
        )
        query_grad = query_grad + jnp.einsum(
            "hqk,khd->qhd", dscore, keys_blk, preferred_element_type=jnp.float32
        )
        block_terms = key_terms_from(queries, head_grads, prob_weights, dscore)
        buffer = lax.dynamic_update_slice_in_dim(buffer, block_terms, block_index * sub_size, 0)
        return (query_grad, buffer)

    empty_terms = jnp.zeros((seq_rows, 2 * HD), jnp.float32)
    query_grad, buffer = lax.fori_loop(0, block_count, backward_step, (empty_query, empty_terms))
    pair_grads = lax.psum_scatter(
        buffer.astype(jnp.bfloat16), "seq", scatter_dimension=0, tiled=True
    ).astype(jnp.float32)
    return (query_grad, pair_grads)


def general(
    tokens,
    upstream_grad,
    norm_gain,
    norm_bias,
    input_codes,
    input_scales,
    input_bias,
    output_codes,
    output_scales,
    layer_scale,
):
    all_codes, all_scales = (
        lax.all_gather(input_codes.astype(jnp.float32), "weight", axis=0, tiled=True).astype(
            input_codes.dtype
        ),
        lax.all_gather(input_scales, "weight", axis=0, tiled=True),
    )
    input_weight = dequantize(all_codes, all_scales)
    output_weight = dequantize(output_codes, output_scales)
    normed, inverse, norm_out = normalize(tokens[0].astype(jnp.float32), norm_gain, norm_bias)
    projected = (
        jnp.dot(norm_out, input_weight, preferred_element_type=jnp.float32) + input_bias
    ).astype(jnp.bfloat16)
    local_rows = projected.shape[0]
    queries = projected[:, :HD].reshape(local_rows, HEADS, HEAD_DIM)
    keys_values = projected[:, HD:]
    scaled_grad = (upstream_grad[0].astype(jnp.float32) * layer_scale).astype(jnp.bfloat16)
    head_grads = jnp.dot(scaled_grad, output_weight.T, preferred_element_type=jnp.float32).astype(
        jnp.bfloat16
    )
    head_grads = head_grads.reshape(local_rows, HEADS, HEAD_DIM)
    query_grad, pair_grads = query_side(queries, head_grads, keys_values, local_rows)
    query_grad = (query_grad * HEAD_DIM ** (-0.5)).reshape(local_rows, HD)
    grad_proj = jnp.concatenate([query_grad, pair_grads], axis=1).astype(jnp.bfloat16)
    grad_norm = jnp.dot(grad_proj, input_weight.T, preferred_element_type=jnp.float32)
    result = norm_backward(grad_norm, normed, inverse, norm_gain)
    return result[None]


WIDTH = 1536
ROWS = 128
SHARD = 384
HALF = 384
CHUNKS = tuple((p, 192 * r) for p in range(6) for r in range(2))
CHUNK = 192
BLOCK = 128
PARTS = 4
PART = ROWS // PARTS
BF16 = jnp.bfloat16
F32 = jnp.float32
MESH = pl.DeviceIdType.MESH
NT = (((1,), (1,)), ((), ()))


def fits(mesh):
    return dict(mesh.shape) == {"groups": 2, "seq": 4, "weight": 4}


def fused_kernel(
    tokens_hbm,
    upstream_hbm,
    gain_hbm,
    norm_bias_hbm,
    codes_hbm,
    in_scales_hbm,
    in_bias_hbm,
    out_codes_hbm,
    out_scales_hbm,
    layer_scale_hbm,
    out_ref,
    gain_ref,
    norm_bias_ref,
    in_scales,
    in_bias_ref,
    out_scales,
    layer_scale_ref,
    weight,
    first_codes,
    codes,
    out_codes,
    out_weight,
    tokens,
    upstream,
    normed_buf,
    inverse_buf,
    raw,
    norm_out,
    scaled,
    packed,
    gathered,
    partial,
    projected,
    grads,
    grad_proj,
    load_sem,
    w_send,
    w_recv,
    t_send,
    p_send,
    t_recv,
    a_send,
    a_recv,
    g_send,
    g_recv,
):
    g = lax.axis_index("groups")
    s = lax.axis_index("seq")
    w = lax.axis_index("weight")
    core = lax.rem(w, 2)
    across = lax.rem(w + 2, 4)
    sibling = w + 1 - 2 * core
    far_sibling = lax.rem(sibling + 2, 4)
    side = s // 2
    home = core == side
    inner = lax.rem(s + side, 2) == 1
    outer = jnp.logical_not(inner)
    away = jnp.logical_not(home)
    owner = w - core + side
    blocks = (s, s + 1 - 2 * lax.rem(s, 2), 2 - side, 3 - 3 * side)

    def block_at(p):
        return jnp.where(inner, p, lax.rem(p + 4, 6))

    def lanes(first):
        return pl.ds(pl.multiple_of(first, BLOCK), BLOCK)

    def load(index, source, target):
        copy = pltpu.make_async_copy(source, target, load_sem.at[index])
        copy.start()
        return copy

    load_in_scales = load(4, in_scales_hbm, in_scales)
    load_first = [
        load(10 + t, codes_hbm.at[:, lanes(HD * t + BLOCK * block_at(0))], first_codes.at[t])
        for t in range(3)
    ]
    load_codes = load(0, codes_hbm, codes)
    load_upstream = load(2, upstream_hbm.at[0], upstream)
    load_out_codes = load(3, out_codes_hbm, out_codes)
    load_tokens = load(1, tokens_hbm.at[0], tokens)
    load_out_scales = load(5, out_scales_hbm, out_scales)
    load_layer_scale = load(6, layer_scale_hbm, layer_scale_ref)
    load_gain = load(7, gain_hbm, gain_ref)
    load_norm_bias = load(8, norm_bias_hbm, norm_bias_ref)
    load_in_bias = load(9, in_bias_hbm, in_bias_ref)

    barrier = pltpu.get_barrier_semaphore()
    peers = [{"weight": across}, {"weight": sibling}, {"groups": 1 - g}]
    for k in (1, 2, 3):
        peers.append({"seq": lax.rem(s + k, 4)})
        peers.append({"seq": lax.rem(s + k, 4), "weight": sibling})
    for peer in peers:
        pl.semaphore_signal(barrier, inc=1, device_id=peer, device_id_type=MESH)

    def remote(source, target, send, recv, peer):
        return pltpu.make_async_remote_copy(
            src_ref=source,
            dst_ref=target,
            send_sem=send,
            recv_sem=recv,
            device_id=peer,
            device_id_type=MESH,
        )

    def dequantize_block(p):
        b = block_at(p)
        for t in range(3):
            for rb in range(3):
                rows = pl.ds(pl.multiple_of(SHARD * w + 128 * rb, 128), 128)
                if p == 0:
                    block = first_codes[t, 128 * rb : 128 * (rb + 1), :]
                else:
                    block = codes[128 * rb : 128 * (rb + 1), lanes(HD * t + BLOCK * b)]
                block = block.astype(F32)
                weight[t, rows, lanes(BLOCK * b)] = (block * in_scales[rb, 6 * t + b]).astype(BF16)

    def weight_copy(kind, index, p, row, count, peer):
        rows = pl.ds(pl.multiple_of(row, 32), count)
        part = weight.at[:, rows, lanes(BLOCK * block_at(p))]
        return remote(part, part, w_send.at[kind, index], w_recv.at[kind, index], peer)

    def x_copy(c, shard):
        p, first = CHUNKS[c]
        row = SHARD * shard + first + CHUNK // 2 * g
        return weight_copy(0, c, p, row, CHUNK // 2, {"weight": across})

    def y_copy(c, part):
        p, first = CHUNKS[c]
        row = SHARD * across + first + CHUNK // 2 * part
        return weight_copy(1, c, p, row, CHUNK // 2, {"groups": 1 - g})

    def own_copy(p, shard):
        return weight_copy(2, p, p, SHARD * shard, SHARD, {"weight": sibling})

    def passed_copy(c, shard):
        p, first = CHUNKS[c]
        return weight_copy(3, c, p, SHARD * shard + first, CHUNK, {"weight": sibling})

    def start_own(p):
        for r in range(2):
            x_copy(2 * p + r, w).start()
        own_copy(p, w).start()

    def from_x(c):
        x_copy(c, across).wait_recv()
        y_copy(c, g).start()

    def from_y(c):
        y_copy(c, 1 - g).wait_recv()
        passed_copy(c, across).start()

    def weight_near(p):
        own_copy(p, sibling).wait_recv()

    def weight_ready(p, near=True):
        if near:
            weight_near(p)
        for r in range(2):
            row = SHARD * far_sibling + CHUNK * r
            weight_copy(3, 2 * p + r, p, row, CHUNK, {"weight": sibling}).wait_recv()

    def part_rows(part):
        return pl.ds(PART * part, PART)

    def send_tokens(part):
        dest = jnp.where(home & inner, 3 * core, 1 + core)
        return remote(
            tokens_hbm.at[0, part_rows(part)],
            raw.at[s, part_rows(part)],
            t_send.at[0, part],
            t_recv.at[s, part],
            {"seq": dest},
        )

    def forward_tokens(slot, part):
        z = blocks[slot]
        rows = raw.at[z, part_rows(part)]
        return remote(
            rows, rows, t_send.at[slot - 1, part], t_recv.at[z, part], {"seq": 3 * core}
        )

    def pass_tokens(slot, part):
        z = blocks[slot]
        rows = raw.at[z, part_rows(part)]
        source = tokens_hbm.at[0, part_rows(part)] if slot == 0 else rows
        return remote(source, rows, p_send.at[slot, part], t_recv.at[z, part], {"weight": sibling})

    def tokens_here(slot, part):
        pass_tokens(slot, part).wait_recv()

    def relay(slot, part, forward):
        tokens_here(slot, part)
        if forward:
            forward_tokens(slot, part).start()
        pass_tokens(slot, part).start()

    def share(d):
        count = 256 if d < 2 else 128
        first = 256 * d if d < 2 else 256 + 128 * d
        rows = packed.at[first : first + count, :]
        peer = {"seq": 1 + core if d < 2 else 3 * core, "weight": w - core + d % 2}
        return remote(rows, gathered.at[s, 0:count, :], a_send.at[d], a_recv.at[s], peer)

    def share_done(z, count):
        return remote(
            packed.at[0:count, :],
            gathered.at[z, 0:count, :],
            a_send.at[0],
            a_recv.at[z],
            {"weight": sibling},
        )

    def stays(d):
        return home & (inner if d < 2 else outer) & (core == d % 2)

    def head_gradients(part):
        for rb in range(3):
            rows = slice(HALF * part + 128 * rb, HALF * part + 128 * (rb + 1))
            for cb in range(12):
                cols = slice(128 * cb, 128 * (cb + 1))
                block = out_codes[rows, cols].astype(F32)
                out_weight[128 * rb : 128 * (rb + 1), cols] = (
                    block * out_scales[3 * part + rb, cb]
                ).astype(BF16)
        value = lax.dot_general(out_weight[...], scaled[...], NT, preferred_element_type=F32)
        value = value.astype(BF16)
        for rb in range(3):
            place = (0, 2, 1, 3, 4, 5)[3 * part + rb]
            packed[BLOCK * place : BLOCK * (place + 1), :] = value[128 * rb : 128 * (rb + 1), :]

    def share_all():
        for d in range(4):
            count = 256 if d < 2 else 128
            first = 256 * d if d < 2 else 256 + 128 * d

            @pl.when(jnp.logical_not(stays(d)))
            def _():
                share(d).start()

            @pl.when(stays(d))
            def _():
                gathered[s, 0:count, :] = packed[first : first + count, :]

    def normalize_slot(slot):
        norm_out[ROWS * slot : ROWS * (slot + 1), :] = normalize(
            raw[blocks[slot]].astype(F32), gain_ref[...][None], norm_bias_ref[...][None]
        )[2]

    def product(n, first, count, chip):
        b = block_at(2 * n + core)
        span = pl.ds(pl.multiple_of(2 * SHARD * chip, 128), 2 * SHARD)
        columns = jnp.concatenate([weight[t, span, lanes(BLOCK * b)] for t in range(3)], axis=1)
        rows = norm_out[first : first + count, span]
        return jnp.dot(rows, columns, preferred_element_type=F32)

    def project_near(n, first, count):
        partial[first : first + count, :] = product(n, first, count, w // 2)

    def project(n, first, count):
        b = block_at(2 * n + core)
        value = partial[first : first + count, :] + product(n, first, count, 1 - w // 2)
        for t in range(3):
            part = value[:, BLOCK * t : BLOCK * (t + 1)]
            part = part + in_bias_ref[lanes(HD * t + BLOCK * b)][None]
            if t == 0:
                part = part * HEAD_DIM ** (-0.5)
            projected[n, t, :, first : first + count] = part.T.astype(BF16)

    load_in_scales.wait()
    for copy in load_first:
        copy.wait()
    dequantize_block(0)
    pl.semaphore_wait(barrier, len(peers))

    @pl.when(inner | home)
    def _():
        for part in range(PARTS):
            send_tokens(part).start()

    start_own(0)

    @pl.when(home)
    def _():
        for part in range(PARTS):
            pass_tokens(0, part).start()

    load_codes.wait()
    for p in range(1, 6):
        dequantize_block(p)
        start_own(p)

    load_layer_scale.wait()
    load_upstream.wait()
    scaled[...] = (upstream[...].astype(F32) * layer_scale_ref[...][None]).astype(BF16)
    load_out_scales.wait()
    load_out_codes.wait()
    head_gradients(0)
    head_gradients(1)

    @pl.when(outer & away)
    def _():
        for part in range(PARTS):
            send_tokens(part).start()

    share_all()

    load_gain.wait()
    load_norm_bias.wait()
    load_in_bias.wait()
    load_tokens.wait()
    normed, inverse, rounded = normalize(
        tokens[...].astype(F32), gain_ref[...][None], norm_bias_ref[...][None]
    )
    normed_buf[...] = normed
    inverse_buf[...] = inverse

    @pl.when(home)
    def _():
        norm_out[0:ROWS, :] = rounded

    def relay_inner(slot, *parts):
        @pl.when(home & inner)
        def _():
            for part in parts:
                relay(slot, part, slot > 1)

    def relay_outer(slot, *parts):
        @pl.when(home & outer)
        def _():
            for part in parts:
                relay(slot, part, False)

    def await_tokens(*slots):
        @pl.when(away)
        def _():
            for slot in slots:
                for part in range(PARTS):
                    tokens_here(slot, part)

    relay_inner(2, 0, 1)
    from_x(0)
    relay_outer(1, 0, 1)
    relay_inner(2, 2)
    relay_inner(1, 0, 1)
    from_x(1)
    relay_outer(1, 2, 3)
    from_x(2)
    relay_inner(2, 3)
    relay_inner(3, 0)
    from_y(0)
    relay_inner(3, 1)
    relay_outer(2, 0)
    from_x(3)
    from_y(1)
    relay_inner(1, 2, 3)
    relay_outer(2, 1)
    relay_inner(3, 2)
    from_x(4)
    relay_outer(2, 2)
    relay_inner(3, 3)
    from_y(2)
    relay_outer(2, 3)
    @pl.when(away)
    def _():
        for slot in (0, 1):
            for part in range(PARTS):
                tokens_here(slot, part)
        normalize_slot(0)

    normalize_slot(1)

    def shared(count):
        for z in range(4):

            @pl.when(jnp.logical_not(home & (s == z)))
            def _():
                share_done(z, count).wait_recv()

    def grad_copy(h, slot, b, peer):
        rows = pl.ds(pl.multiple_of(BLOCK * b + HEAD_DIM * (h % 2), 64), HEAD_DIM)
        return remote(
            grads.at[h, slot],
            grad_proj.at[:, rows, :],
            g_send.at[h, slot],
            g_recv.at[2 * b + h % 2],
            peer,
        )

    def send_grads(h, slot):
        b = block_at(h // 2 * 2 + core)
        return grad_copy(h, slot, b, {"seq": blocks[slot], "weight": owner})

    def attend(h):
        n, i = h // 2, h % 2
        rows = slice(HEAD_DIM * i, HEAD_DIM * (i + 1))
        q_t, k_t, v_t = (projected[n, t, rows, :] for t in range(3))
        g_rows = slice(HEAD_DIM * h, HEAD_DIM * (h + 1))
        g_t = jnp.concatenate([gathered[z, g_rows, :] for z in blocks], axis=1)
        scores = jnp.dot(k_t.T, q_t, preferred_element_type=F32)
        dprob = jnp.dot(v_t.T, g_t, preferred_element_type=F32)
        expo = jnp.exp(scores - jnp.max(scores, axis=0, keepdims=True))
        probs = expo * (1.0 / jnp.sum(expo, axis=0, keepdims=True))
        delta = jnp.sum(probs * dprob, axis=0, keepdims=True)
        dscore = (probs * (dprob - delta)).astype(BF16)
        parts = (
            jnp.dot(k_t, dscore, preferred_element_type=F32) * HEAD_DIM ** (-0.5),
            lax.dot_general(q_t, dscore, NT, preferred_element_type=F32),
            lax.dot_general(g_t, probs.astype(BF16), NT, preferred_element_type=F32),
        )
        for t in range(3):
            value = parts[t].astype(BF16)
            for slot in range(4):
                grads[h, slot, t] = value[:, ROWS * slot : ROWS * (slot + 1)]
        for slot in (3, 1) if h == 2 else (3, 2, 1):
            send_grads(h, slot).start()
        if h == 3:
            send_grads(2, 2).start()

        @pl.when(home)
        def _():
            first = BLOCK * block_at(2 * n + core) + HEAD_DIM * i
            own = pl.ds(pl.multiple_of(first, 64), HEAD_DIM)
            grad_proj[:, own, :] = grads[h, 0]

        @pl.when(away)
        def _():
            send_grads(h, 0).start()

    @pl.when(inner)
    def _():
        await_tokens(2, 3)
        normalize_slot(2)
        normalize_slot(3)
        from_x(5)
        weight_near(core)
        project_near(0, 0, 4 * ROWS)
        from_y(3)
        from_x(6)
        weight_ready(core, False)
        project(0, 0, 4 * ROWS)
        shared(256)

        from_x(7)
        attend(0)
        from_y(4)

        @pl.when(core == 1)
        def _():
            from_x(8)
            from_y(5)

        attend(1)

        @pl.when(core == 0)
        def _():
            from_x(8)
            from_y(5)

        from_x(9)
        weight_near(2 + core)
        project_near(1, 0, 4 * ROWS)
        from_y(6)
        from_y(7)
        weight_ready(2 + core, False)
        project(1, 0, 4 * ROWS)
        from_x(10)
        attend(2)
        from_x(11)
        from_y(8)
        attend(3)

    @pl.when(outer)
    def _():
        from_x(5)
        relay_outer(3, 0)
        await_tokens(2)
        normalize_slot(2)
        from_y(3)
        from_x(6)
        relay_outer(3, 1)
        weight_near(core)
        project_near(0, 0, 3 * ROWS)
        weight_ready(core, False)
        project(0, 0, 3 * ROWS)
        from_x(7)
        from_y(4)
        relay_outer(3, 2)
        from_x(8)
        from_y(5)
        relay_outer(3, 3)
        await_tokens(3)
        normalize_slot(3)
        project_near(0, 3 * ROWS, ROWS)
        project(0, 3 * ROWS, ROWS)
        shared(128)
        from_x(9)
        attend(0)
        from_x(10)
        from_y(6)
        attend(1)
        from_x(11)
        from_y(7)
        from_y(8)

    from_y(9)

    def grads_ready(first, count):
        for b in range(first, first + count):
            mine = home & (inner if b < 4 else outer) & (core == b % 2)
            for i in range(2):

                @pl.when(jnp.logical_not(mine))
                def _():
                    grad_copy(i, 0, b, {"weight": sibling}).wait_recv()

    def back(first, count):
        total = None
        part = slice(BLOCK * first, BLOCK * (first + count))
        for t in range(3):
            term = lax.dot_general(
                grad_proj[t, part, :].T, weight[t, :, part], NT, preferred_element_type=F32
            )
            total = term if total is None else total + term
        return total

    @pl.when(inner)
    def _():
        weight_ready(1 - core)

    @pl.when(outer)
    def _():
        weight_ready(2)
        weight_ready(3)

    from_y(10)
    from_y(11)
    grads_ready(0, 2)
    out_ref[0] = back(0, 2)

    @pl.when(inner)
    def _():
        weight_ready(4)
        weight_ready(5)

    @pl.when(outer)
    def _():
        weight_ready(1 - core)

    grads_ready(4, 2)
    out_ref[0] += back(4, 2)

    @pl.when(inner)
    def _():
        weight_ready(3 - core)

    @pl.when(outer)
    def _():
        weight_ready(4)
        weight_ready(5)

    for c in range(len(CHUNKS)):
        x_copy(c, w).wait_send()
        y_copy(c, g).wait_send()
        passed_copy(c, across).wait_send()
    for p in range(6):
        own_copy(p, w).wait_send()
    for part in range(PARTS):
        send_tokens(part).wait_send()

        @pl.when(home)
        def _():
            for slot in range(4):
                pass_tokens(slot, part).wait_send()

        @pl.when(home & inner)
        def _():
            for slot in (2, 3):
                forward_tokens(slot, part).wait_send()

    for d in range(4):

        @pl.when(jnp.logical_not(stays(d)))
        def _():
            share(d).wait_send()

    def grads_sent(heads):
        for h in heads:
            for slot in (1, 2, 3):
                send_grads(h, slot).wait_send()

            @pl.when(away)
            def _():
                send_grads(h, 0).wait_send()

    grads_sent((0, 1))
    grads_ready(2, 1)
    out_ref[0] += back(2, 1)
    grads_ready(3, 1)
    grad_norm = out_ref[0] + back(3, 1)
    out_ref[0] = norm_backward(grad_norm, normed_buf[...], inverse_buf[...], gain_ref[...][None])

    @pl.when(inner)
    def _():
        grads_sent((2, 3))


def fused(
    tokens,
    upstream_grad,
    norm_gain,
    norm_bias,
    input_codes,
    input_scales,
    input_bias,
    output_codes,
    output_scales,
    layer_scale,
):
    hbm = pl.BlockSpec(memory_space=pltpu.HBM)
    vmem = pl.BlockSpec(memory_space=pltpu.VMEM)
    return pl.pallas_call(
        fused_kernel,
        out_shape=jax.ShapeDtypeStruct((1, ROWS, WIDTH), F32),
        in_specs=[hbm] * 10,
        out_specs=vmem,
        scratch_shapes=[
            pltpu.VMEM((WIDTH,), F32),
            pltpu.VMEM((WIDTH,), F32),
            pltpu.SMEM((3, 18), F32),
            pltpu.VMEM((3 * HD,), F32),
            pltpu.SMEM((6, 12), F32),
            pltpu.VMEM((WIDTH,), F32),
            pltpu.VMEM((3, WIDTH, HD), BF16),
            pltpu.VMEM((3, SHARD, BLOCK), BF16),
            pltpu.VMEM((SHARD, 3 * HD), BF16),
            pltpu.VMEM((HD, WIDTH), BF16),
            pltpu.VMEM((HALF, WIDTH), BF16),
            pltpu.VMEM((ROWS, WIDTH), BF16),
            pltpu.VMEM((ROWS, WIDTH), BF16),
            pltpu.VMEM((ROWS, WIDTH), F32),
            pltpu.VMEM((ROWS, 1), F32),
            pltpu.VMEM((4, ROWS, WIDTH), BF16),
            pltpu.VMEM((4 * ROWS, WIDTH), BF16),
            pltpu.VMEM((ROWS, WIDTH), BF16),
            pltpu.VMEM((HD, ROWS), BF16),
            pltpu.VMEM((4, 2 * BLOCK, ROWS), BF16),
            pltpu.VMEM((4 * ROWS, 3 * BLOCK), F32),
            pltpu.VMEM((2, 3, BLOCK, 4 * ROWS), BF16),
            pltpu.VMEM((4, 4, 3, HEAD_DIM, ROWS), BF16),
            pltpu.VMEM((3, HD, ROWS), BF16),
            pltpu.SemaphoreType.DMA((13,)),
            pltpu.SemaphoreType.DMA((4, len(CHUNKS))),
            pltpu.SemaphoreType.DMA((4, len(CHUNKS))),
            pltpu.SemaphoreType.DMA((3, PARTS)),
            pltpu.SemaphoreType.DMA((4, PARTS)),
            pltpu.SemaphoreType.DMA((4, PARTS)),
            pltpu.SemaphoreType.DMA((4,)),
            pltpu.SemaphoreType.DMA((4,)),
            pltpu.SemaphoreType.DMA((4, 4)),
            pltpu.SemaphoreType.DMA((12,)),
        ],
        compiler_params=pltpu.CompilerParams(
            collective_id=0, has_side_effects=True, vmem_limit_bytes=64 * 1024 * 1024 - 65536
        ),
        cost_estimate=pl.CostEstimate(
            flops=2500000000, bytes_accessed=8000000, transcendentals=1000000
        ),
    )(
        tokens,
        upstream_grad,
        norm_gain,
        norm_bias,
        input_codes,
        input_scales,
        input_bias,
        output_codes,
        output_scales,
        layer_scale,
    )


def solution(mesh):
    in_specs = (
        P(("groups", "weight"), "seq", None),
        P(("groups", "weight"), "seq", None),
        P(),
        P(),
        P("weight", None),
        P("weight", None),
        P(),
        P(),
        P(),
        P(),
    )
    out_specs = P(("groups", "weight"), "seq", None)
    local = fused if fits(mesh) else general
    return jax.shard_map(local, mesh=mesh, in_specs=in_specs, out_specs=out_specs, check_vma=False)
```

```python
import functools
import math

import jax
import jax.numpy as jnp
from jax import lax
from jax.experimental import pallas as pl
from jax.experimental.pallas import tpu as pltpu
from jax.sharding import PartitionSpec as P

HEADS = 12
HEAD_DIM = 64
QBLOCK = 128
HD = 768


def dequantize(codes, scales):
    expanded = jnp.repeat(jnp.repeat(scales, QBLOCK, axis=0), QBLOCK, axis=1)
    return (codes.astype(jnp.float32) * expanded).astype(jnp.bfloat16)


def normalize(rows, gain, shift):
    mean_value = jnp.mean(rows, axis=-1, keepdims=True)
    centered = rows - mean_value
    variance = jnp.mean(centered * centered, axis=-1, keepdims=True)
    inverse = lax.rsqrt(variance + 1e-06)
    normed = centered * inverse
    return (normed, inverse, (normed * gain + shift).astype(jnp.bfloat16))


def norm_backward(grad_norm, normed, inverse, gain):
    grad_hat = grad_norm * gain
    first_mean = jnp.mean(grad_hat, axis=-1, keepdims=True)
    second_mean = jnp.mean(grad_hat * normed, axis=-1, keepdims=True)
    return inverse * (grad_hat - first_mean - normed * second_mean)


def score_block(queries, head_grads, pair_block):
    row_count = pair_block.shape[0]
    keys_blk = pair_block[:, :HD].reshape(row_count, HEADS, HEAD_DIM)
    values_blk = pair_block[:, HD:].reshape(row_count, HEADS, HEAD_DIM)
    scores = jnp.einsum(
        "qhd,khd->hqk", queries, keys_blk, preferred_element_type=jnp.float32
    ) * HEAD_DIM ** (-0.5)
    dprob = jnp.einsum("qhd,khd->hqk", head_grads, values_blk, preferred_element_type=jnp.float32)
    return (keys_blk, scores, dprob)


def update_stats(statistics, queries, head_grads, pair_rows):
    sub_size = math.gcd(pair_rows.shape[0], 512)

    def visit_block(block_index, running):
        run_max, run_total, run_mix = running
        pair_block = lax.dynamic_slice_in_dim(pair_rows, block_index * sub_size, sub_size, 0)
        keys_blk, scores, dprob = score_block(queries, head_grads, pair_block)
        new_max = jnp.maximum(run_max, jnp.max(scores, axis=-1))
        factor = jnp.exp(run_max - new_max)
        expo = jnp.exp(scores - new_max[..., None])
        return (
            new_max,
            run_total * factor + jnp.sum(expo, axis=-1),
            run_mix * factor + jnp.sum(expo * dprob, axis=-1),
        )

    return lax.fori_loop(0, pair_rows.shape[0] // sub_size, visit_block, statistics)


def block_backward(queries, head_grads, pair_block, log_total, row_delta):
    keys_blk, scores, dprob = score_block(queries, head_grads, pair_block)
    weights = jnp.exp(scores - log_total[..., None])
    prob_weights = weights.astype(jnp.bfloat16)
    dscore = (weights * (dprob - row_delta[..., None])).astype(jnp.bfloat16)
    return (keys_blk, prob_weights, dscore)


def key_terms_from(queries, head_grads, prob_weights, dscore):
    key_part = jnp.einsum(
        "hqk,qhd->khd", dscore, queries, preferred_element_type=jnp.float32
    ) * HEAD_DIM ** (-0.5)
    value_part = jnp.einsum(
        "hqk,qhd->khd", prob_weights, head_grads, preferred_element_type=jnp.float32
    )
    row_count = key_part.shape[0]
    return jnp.concatenate(
        [key_part.reshape(row_count, HD), value_part.reshape(row_count, HD)], axis=1
    )


def query_side(queries, head_grads, keys_values, local_rows):
    seq_rows = local_rows * lax.axis_size("seq")
    start_stats = (
        jnp.full((HEADS, local_rows), -1e30, jnp.float32),
        jnp.zeros((HEADS, local_rows), jnp.float32),
        jnp.zeros((HEADS, local_rows), jnp.float32),
    )
    all_pairs = lax.all_gather(keys_values, "seq", axis=0, tiled=True)
    statistics = update_stats(start_stats, queries, head_grads, all_pairs)
    row_max, row_total, row_mix = statistics
    log_total = row_max + jnp.log(row_total)
    row_delta = row_mix / row_total
    sub_size = math.gcd(seq_rows, 512)
    block_count = seq_rows // sub_size
    empty_query = jnp.zeros((local_rows, HEADS, HEAD_DIM), jnp.float32)

    def backward_step(block_index, running):
        query_grad, buffer = running
        pair_block = lax.dynamic_slice_in_dim(all_pairs, block_index * sub_size, sub_size, 0)
        keys_blk, prob_weights, dscore = block_backward(
            queries, head_grads, pair_block, log_total, row_delta
        )
        query_grad = query_grad + jnp.einsum(
            "hqk,khd->qhd", dscore, keys_blk, preferred_element_type=jnp.float32
        )
        block_terms = key_terms_from(queries, head_grads, prob_weights, dscore)
        buffer = lax.dynamic_update_slice_in_dim(buffer, block_terms, block_index * sub_size, 0)
        return (query_grad, buffer)

    empty_terms = jnp.zeros((seq_rows, 2 * HD), jnp.float32)
    query_grad, buffer = lax.fori_loop(0, block_count, backward_step, (empty_query, empty_terms))
    pair_grads = lax.psum_scatter(
        buffer.astype(jnp.bfloat16), "seq", scatter_dimension=0, tiled=True
    ).astype(jnp.float32)
    return (query_grad, pair_grads)


def general(
    tokens,
    upstream_grad,
    norm_gain,
    norm_bias,
    input_codes,
    input_scales,
    input_bias,
    output_codes,
    output_scales,
    layer_scale,
):
    all_codes, all_scales = (
        lax.all_gather(input_codes.astype(jnp.float32), "weight", axis=0, tiled=True).astype(
            input_codes.dtype
        ),
        lax.all_gather(input_scales, "weight", axis=0, tiled=True),
    )
    input_weight = dequantize(all_codes, all_scales)
    output_weight = dequantize(output_codes, output_scales)
    normed, inverse, norm_out = normalize(tokens[0].astype(jnp.float32), norm_gain, norm_bias)
    projected = (
        jnp.dot(norm_out, input_weight, preferred_element_type=jnp.float32) + input_bias
    ).astype(jnp.bfloat16)
    local_rows = projected.shape[0]
    queries = projected[:, :HD].reshape(local_rows, HEADS, HEAD_DIM)
    keys_values = projected[:, HD:]
    scaled_grad = (upstream_grad[0].astype(jnp.float32) * layer_scale).astype(jnp.bfloat16)
    head_grads = jnp.dot(scaled_grad, output_weight.T, preferred_element_type=jnp.float32).astype(
        jnp.bfloat16
    )
    head_grads = head_grads.reshape(local_rows, HEADS, HEAD_DIM)
    query_grad, pair_grads = query_side(queries, head_grads, keys_values, local_rows)
    query_grad = (query_grad * HEAD_DIM ** (-0.5)).reshape(local_rows, HD)
    grad_proj = jnp.concatenate([query_grad, pair_grads], axis=1).astype(jnp.bfloat16)
    grad_norm = jnp.dot(grad_proj, input_weight.T, preferred_element_type=jnp.float32)
    result = norm_backward(grad_norm, normed, inverse, norm_gain)
    return result[None]


WIDTH = 1536
ROWS = 128
SHARD = 384
HALF = 384
CHUNKS = tuple((p, 192 * r) for p in range(6) for r in range(2))
CHUNK = 192
BLOCK = 128
PARTS = 4
PART = ROWS // PARTS
BF16 = jnp.bfloat16
F32 = jnp.float32
MESH = pl.DeviceIdType.MESH
NT = (((1,), (1,)), ((), ()))


def fits(mesh):
    return dict(mesh.shape) == {"groups": 2, "seq": 4, "weight": 4}


def fused_kernel(
    tokens_hbm,
    upstream_hbm,
    gain_hbm,
    norm_bias_hbm,
    codes_hbm,
    in_scales_hbm,
    in_bias_hbm,
    out_codes_hbm,
    out_scales_hbm,
    layer_scale_hbm,
    out_ref,
    gain_ref,
    norm_bias_ref,
    in_scales,
    in_bias_ref,
    out_scales,
    layer_scale_ref,
    weight,
    first_codes,
    codes,
    out_codes,
    out_weight,
    tokens,
    upstream,
    normed_buf,
    inverse_buf,
    raw,
    norm_out,
    scaled,
    packed,
    gathered,
    partial,
    projected,
    grads,
    grad_proj,
    load_sem,
    w_send,
    w_recv,
    t_send,
    p_send,
    t_recv,
    a_send,
    a_recv,
    g_send,
    g_recv,
):
    g = lax.axis_index("groups")
    s = lax.axis_index("seq")
    w = lax.axis_index("weight")
    core = lax.rem(w, 2)
    across = lax.rem(w + 2, 4)
    sibling = w + 1 - 2 * core
    far_sibling = lax.rem(sibling + 2, 4)
    side = s // 2
    home = core == side
    inner = lax.rem(s + side, 2) == 1
    outer = jnp.logical_not(inner)
    away = jnp.logical_not(home)
    owner = w - core + side
    blocks = (s, s + 1 - 2 * lax.rem(s, 2), 2 - side, 3 - 3 * side)

    def block_at(p):
        return jnp.where(inner, p, lax.rem(p + 4, 6))

    def lanes(first):
        return pl.ds(pl.multiple_of(first, BLOCK), BLOCK)

    def load(index, source, target):
        copy = pltpu.make_async_copy(source, target, load_sem.at[index])
        copy.start()
        return copy

    load_in_scales = load(4, in_scales_hbm, in_scales)
    load_first = [
        load(10 + t, codes_hbm.at[:, lanes(HD * t + BLOCK * block_at(0))], first_codes.at[t])
        for t in range(3)
    ]
    load_codes = load(0, codes_hbm, codes)
    load_upstream = load(2, upstream_hbm.at[0], upstream)
    load_out_codes = load(3, out_codes_hbm, out_codes)
    load_tokens = load(1, tokens_hbm.at[0], tokens)
    load_out_scales = load(5, out_scales_hbm, out_scales)
    load_layer_scale = load(6, layer_scale_hbm, layer_scale_ref)
    load_gain = load(7, gain_hbm, gain_ref)
    load_norm_bias = load(8, norm_bias_hbm, norm_bias_ref)
    load_in_bias = load(9, in_bias_hbm, in_bias_ref)

    barrier = pltpu.get_barrier_semaphore()
    peers = [{"weight": across}, {"weight": sibling}, {"groups": 1 - g}]
    for k in (1, 2, 3):
        peers.append({"seq": lax.rem(s + k, 4)})
        peers.append({"seq": lax.rem(s + k, 4), "weight": sibling})
    for peer in peers:
        pl.semaphore_signal(barrier, inc=1, device_id=peer, device_id_type=MESH)

    def remote(source, target, send, recv, peer):
        return pltpu.make_async_remote_copy(
            src_ref=source,
            dst_ref=target,
            send_sem=send,
            recv_sem=recv,
            device_id=peer,
            device_id_type=MESH,
        )

    def dequantize_block(p):
        b = block_at(p)
        for t in range(3):
            for rb in range(3):
                rows = pl.ds(pl.multiple_of(SHARD * w + 128 * rb, 128), 128)
                if p == 0:
                    block = first_codes[t, 128 * rb : 128 * (rb + 1), :]
                else:
                    block = codes[128 * rb : 128 * (rb + 1), lanes(HD * t + BLOCK * b)]
                block = block.astype(F32)
                weight[t, rows, lanes(BLOCK * b)] = (block * in_scales[rb, 6 * t + b]).astype(BF16)

    def weight_copy(kind, index, p, row, count, peer):
        rows = pl.ds(pl.multiple_of(row, 32), count)
        part = weight.at[:, rows, lanes(BLOCK * block_at(p))]
        return remote(part, part, w_send.at[kind, index], w_recv.at[kind, index], peer)

    def x_copy(c, shard):
        p, first = CHUNKS[c]
        row = SHARD * shard + first + CHUNK // 2 * g
        return weight_copy(0, c, p, row, CHUNK // 2, {"weight": across})

    def y_copy(c, part):
        p, first = CHUNKS[c]
        row = SHARD * across + first + CHUNK // 2 * part
        return weight_copy(1, c, p, row, CHUNK // 2, {"groups": 1 - g})

    def own_copy(p, shard):
        return weight_copy(2, p, p, SHARD * shard, SHARD, {"weight": sibling})

    def passed_copy(c, shard):
        p, first = CHUNKS[c]
        return weight_copy(3, c, p, SHARD * shard + first, CHUNK, {"weight": sibling})

    def start_own(p):
        for r in range(2):
            x_copy(2 * p + r, w).start()
        own_copy(p, w).start()

    def from_x(c):
        x_copy(c, across).wait_recv()
        y_copy(c, g).start()

    def from_y(c):
        y_copy(c, 1 - g).wait_recv()
        passed_copy(c, across).start()

    def weight_near(p):
        own_copy(p, sibling).wait_recv()

    def weight_ready(p, near=True):
        if near:
            weight_near(p)
        for r in range(2):
            row = SHARD * far_sibling + CHUNK * r
            weight_copy(3, 2 * p + r, p, row, CHUNK, {"weight": sibling}).wait_recv()

    def part_rows(part):
        return pl.ds(PART * part, PART)

    def send_tokens(part):
        dest = jnp.where(home & inner, 3 * core, 1 + core)
        return remote(
            tokens_hbm.at[0, part_rows(part)],
            raw.at[s, part_rows(part)],
            t_send.at[0, part],
            t_recv.at[s, part],
            {"seq": dest},
        )

    def forward_tokens(slot, part):
        z = blocks[slot]
        rows = raw.at[z, part_rows(part)]
        return remote(
            rows, rows, t_send.at[slot - 1, part], t_recv.at[z, part], {"seq": 3 * core}
        )

    def pass_tokens(slot, part):
        z = blocks[slot]
        rows = raw.at[z, part_rows(part)]
        source = tokens_hbm.at[0, part_rows(part)] if slot == 0 else rows
        return remote(source, rows, p_send.at[slot, part], t_recv.at[z, part], {"weight": sibling})

    def tokens_here(slot, part):
        pass_tokens(slot, part).wait_recv()

    def relay(slot, part, forward):
        tokens_here(slot, part)
        if forward:
            forward_tokens(slot, part).start()
        pass_tokens(slot, part).start()

    def share(d):
        count = 256 if d < 2 else 128
        first = 256 * d if d < 2 else 256 + 128 * d
        rows = packed.at[first : first + count, :]
        peer = {"seq": 1 + core if d < 2 else 3 * core, "weight": w - core + d % 2}
        return remote(rows, gathered.at[s, 0:count, :], a_send.at[d], a_recv.at[s], peer)

    def share_done(z, count):
        return remote(
            packed.at[0:count, :],
            gathered.at[z, 0:count, :],
            a_send.at[0],
            a_recv.at[z],
            {"weight": sibling},
        )

    def stays(d):
        return home & (inner if d < 2 else outer) & (core == d % 2)

    def head_gradients(part):
        for rb in range(3):
            rows = slice(HALF * part + 128 * rb, HALF * part + 128 * (rb + 1))
            for cb in range(12):
                cols = slice(128 * cb, 128 * (cb + 1))
                block = out_codes[rows, cols].astype(F32)
                out_weight[128 * rb : 128 * (rb + 1), cols] = (
                    block * out_scales[3 * part + rb, cb]
                ).astype(BF16)
        value = lax.dot_general(out_weight[...], scaled[...], NT, preferred_element_type=F32)
        value = value.astype(BF16)
        for rb in range(3):
            place = (0, 2, 1, 3, 4, 5)[3 * part + rb]
            packed[BLOCK * place : BLOCK * (place + 1), :] = value[128 * rb : 128 * (rb + 1), :]

    def share_all():
        for d in range(4):
            count = 256 if d < 2 else 128
            first = 256 * d if d < 2 else 256 + 128 * d

            @pl.when(jnp.logical_not(stays(d)))
            def _():
                share(d).start()

            @pl.when(stays(d))
            def _():
                gathered[s, 0:count, :] = packed[first : first + count, :]

    def normalize_slot(slot):
        norm_out[ROWS * slot : ROWS * (slot + 1), :] = normalize(
            raw[blocks[slot]].astype(F32), gain_ref[...][None], norm_bias_ref[...][None]
        )[2]

    def product(n, first, count, chip):
        b = block_at(2 * n + core)
        span = pl.ds(pl.multiple_of(2 * SHARD * chip, 128), 2 * SHARD)
        columns = jnp.concatenate([weight[t, span, lanes(BLOCK * b)] for t in range(3)], axis=1)
        rows = norm_out[first : first + count, span]
        return jnp.dot(rows, columns, preferred_element_type=F32)

    def project_near(n, first, count):
        partial[first : first + count, :] = product(n, first, count, w // 2)

    def project(n, first, count):
        b = block_at(2 * n + core)
        value = partial[first : first + count, :] + product(n, first, count, 1 - w // 2)
        for t in range(3):
            part = value[:, BLOCK * t : BLOCK * (t + 1)]
            part = part + in_bias_ref[lanes(HD * t + BLOCK * b)][None]
            if t == 0:
                part = part * HEAD_DIM ** (-0.5)
            projected[n, t, :, first : first + count] = part.T.astype(BF16)

    load_in_scales.wait()
    for copy in load_first:
        copy.wait()
    dequantize_block(0)
    pl.semaphore_wait(barrier, len(peers))

    @pl.when(inner | home)
    def _():
        for part in range(PARTS):
            send_tokens(part).start()

    start_own(0)

    @pl.when(home)
    def _():
        for part in range(PARTS):
            pass_tokens(0, part).start()

    load_codes.wait()
    for p in range(1, 6):
        dequantize_block(p)
        start_own(p)

    load_layer_scale.wait()
    load_upstream.wait()
    scaled[...] = (upstream[...].astype(F32) * layer_scale_ref[...][None]).astype(BF16)
    load_out_scales.wait()
    load_out_codes.wait()
    head_gradients(0)
    head_gradients(1)

    @pl.when(outer & away)
    def _():
        for part in range(PARTS):
            send_tokens(part).start()

    @pl.when(outer | home)
    def _():
        share_all()

    load_gain.wait()
    load_norm_bias.wait()
    load_in_bias.wait()
    load_tokens.wait()
    normed, inverse, rounded = normalize(
        tokens[...].astype(F32), gain_ref[...][None], norm_bias_ref[...][None]
    )
    normed_buf[...] = normed
    inverse_buf[...] = inverse

    @pl.when(home)
    def _():
        norm_out[0:ROWS, :] = rounded

    def relay_inner(slot, *parts):
        @pl.when(home & inner)
        def _():
            for part in parts:
                relay(slot, part, slot > 1)

    def relay_outer(slot, *parts):
        @pl.when(home & outer)
        def _():
            for part in parts:
                relay(slot, part, False)

    def await_tokens(*slots):
        @pl.when(away)
        def _():
            for slot in slots:
                for part in range(PARTS):
                    tokens_here(slot, part)

    relay_inner(2, 0, 1)
    from_x(0)
    relay_outer(1, 0, 1)
    relay_inner(2, 2)
    relay_inner(1, 0, 1)
    from_x(1)

    @pl.when(inner & away)
    def _():
        share_all()

    relay_outer(1, 2, 3)
    from_x(2)
    relay_inner(2, 3)
    relay_inner(3, 0)
    from_y(0)
    relay_inner(3, 1)
    relay_outer(2, 0)
    from_x(3)
    from_y(1)
    relay_inner(1, 2, 3)
    relay_outer(2, 1)
    relay_inner(3, 2)
    from_x(4)
    relay_outer(2, 2)
    relay_inner(3, 3)
    from_y(2)
    relay_outer(2, 3)
    @pl.when(away)
    def _():
        for slot in (0, 1):
            for part in range(PARTS):
                tokens_here(slot, part)
        normalize_slot(0)

    normalize_slot(1)

    def shared(count):
        for z in range(4):

            @pl.when(jnp.logical_not(home & (s == z)))
            def _():
                share_done(z, count).wait_recv()

    def grad_copy(h, slot, b, peer):
        rows = pl.ds(pl.multiple_of(BLOCK * b + HEAD_DIM * (h % 2), 64), HEAD_DIM)
        return remote(
            grads.at[h, slot],
            grad_proj.at[:, rows, :],
            g_send.at[h, slot],
            g_recv.at[2 * b + h % 2],
            peer,
        )

    def send_grads(h, slot):
        b = block_at(h // 2 * 2 + core)
        return grad_copy(h, slot, b, {"seq": blocks[slot], "weight": owner})

    def attend(h):
        n, i = h // 2, h % 2
        rows = slice(HEAD_DIM * i, HEAD_DIM * (i + 1))
        q_t, k_t, v_t = (projected[n, t, rows, :] for t in range(3))
        g_rows = slice(HEAD_DIM * h, HEAD_DIM * (h + 1))
        g_t = jnp.concatenate([gathered[z, g_rows, :] for z in blocks], axis=1)
        scores = jnp.dot(k_t.T, q_t, preferred_element_type=F32)
        dprob = jnp.dot(v_t.T, g_t, preferred_element_type=F32)
        expo = jnp.exp(scores - jnp.max(scores, axis=0, keepdims=True))
        probs = expo * (1.0 / jnp.sum(expo, axis=0, keepdims=True))
        delta = jnp.sum(probs * dprob, axis=0, keepdims=True)
        dscore = (probs * (dprob - delta)).astype(BF16)
        parts = (
            jnp.dot(k_t, dscore, preferred_element_type=F32) * HEAD_DIM ** (-0.5),
            lax.dot_general(q_t, dscore, NT, preferred_element_type=F32),
            lax.dot_general(g_t, probs.astype(BF16), NT, preferred_element_type=F32),
        )
        for t in range(3):
            value = parts[t].astype(BF16)
            for slot in range(4):
                grads[h, slot, t] = value[:, ROWS * slot : ROWS * (slot + 1)]
        for slot in (3, 1) if h == 2 else (3, 2, 1):
            send_grads(h, slot).start()
        if h == 3:
            send_grads(2, 2).start()

        @pl.when(home)
        def _():
            first = BLOCK * block_at(2 * n + core) + HEAD_DIM * i
            own = pl.ds(pl.multiple_of(first, 64), HEAD_DIM)
            grad_proj[:, own, :] = grads[h, 0]

        @pl.when(away)
        def _():
            send_grads(h, 0).start()

    @pl.when(inner)
    def _():
        await_tokens(2)
        normalize_slot(2)
        from_x(5)
        from_y(3)
        await_tokens(3)
        normalize_slot(3)
        weight_near(core)
        project_near(0, 0, 4 * ROWS)
        from_x(6)
        weight_ready(core, False)
        project(0, 0, 4 * ROWS)
        shared(256)

        from_x(7)
        attend(0)
        from_y(4)

        @pl.when(core == 1)
        def _():
            from_x(8)
            from_y(5)

        attend(1)

        @pl.when(core == 0)
        def _():
            from_x(8)
            from_y(5)

        from_x(9)
        weight_near(2 + core)
        project_near(1, 0, 4 * ROWS)
        from_y(6)
        from_y(7)
        weight_ready(2 + core, False)
        project(1, 0, 4 * ROWS)
        from_x(10)
        attend(2)
        from_x(11)
        from_y(8)
        attend(3)

    @pl.when(outer)
    def _():
        from_x(5)
        relay_outer(3, 0)
        await_tokens(2)
        normalize_slot(2)
        from_y(3)
        from_x(6)
        relay_outer(3, 1)
        weight_near(core)
        project_near(0, 0, 3 * ROWS)
        weight_ready(core, False)
        project(0, 0, 3 * ROWS)
        from_x(7)
        from_y(4)
        relay_outer(3, 2)
        from_x(8)
        from_y(5)
        relay_outer(3, 3)
        await_tokens(3)
        normalize_slot(3)
        project_near(0, 3 * ROWS, ROWS)
        project(0, 3 * ROWS, ROWS)
        shared(128)
        from_x(9)
        attend(0)
        from_x(10)
        from_y(6)
        attend(1)
        from_x(11)
        from_y(7)
        from_y(8)

    from_y(9)

    def grads_ready(first, count):
        for b in range(first, first + count):
            mine = home & (inner if b < 4 else outer) & (core == b % 2)
            for i in range(2):

                @pl.when(jnp.logical_not(mine))
                def _():
                    grad_copy(i, 0, b, {"weight": sibling}).wait_recv()

    def back(first, count):
        total = None
        part = slice(BLOCK * first, BLOCK * (first + count))
        for t in range(3):
            term = lax.dot_general(
                grad_proj[t, part, :].T, weight[t, :, part], NT, preferred_element_type=F32
            )
            total = term if total is None else total + term
        return total

    @pl.when(inner)
    def _():
        weight_ready(1 - core)

    @pl.when(outer)
    def _():
        weight_ready(2)
        weight_ready(3)

    grads_ready(0, 1)
    out_ref[0] = back(0, 1)
    from_y(10)
    from_y(11)
    grads_ready(1, 1)
    out_ref[0] += back(1, 1)

    @pl.when(inner)
    def _():
        weight_ready(4)
        weight_ready(5)

    @pl.when(outer)
    def _():
        weight_ready(1 - core)

    grads_ready(4, 2)
    out_ref[0] += back(4, 2)

    @pl.when(inner)
    def _():
        weight_ready(3 - core)

    @pl.when(outer)
    def _():
        weight_ready(4)
        weight_ready(5)

    for c in range(len(CHUNKS)):
        x_copy(c, w).wait_send()
        y_copy(c, g).wait_send()
        passed_copy(c, across).wait_send()
    for p in range(6):
        own_copy(p, w).wait_send()
    for part in range(PARTS):
        send_tokens(part).wait_send()

        @pl.when(home)
        def _():
            for slot in range(4):
                pass_tokens(slot, part).wait_send()

        @pl.when(home & inner)
        def _():
            for slot in (2, 3):
                forward_tokens(slot, part).wait_send()

    for d in range(4):

        @pl.when(jnp.logical_not(stays(d)))
        def _():
            share(d).wait_send()

    def grads_sent(heads):
        for h in heads:
            for slot in (1, 2, 3):
                send_grads(h, slot).wait_send()

            @pl.when(away)
            def _():
                send_grads(h, 0).wait_send()

    grads_sent((0, 1))
    grads_ready(2, 1)
    out_ref[0] += back(2, 1)
    grads_ready(3, 1)
    grad_norm = out_ref[0] + back(3, 1)
    out_ref[0] = norm_backward(grad_norm, normed_buf[...], inverse_buf[...], gain_ref[...][None])

    @pl.when(inner)
    def _():
        grads_sent((2, 3))


def fused(
    tokens,
    upstream_grad,
    norm_gain,
    norm_bias,
    input_codes,
    input_scales,
    input_bias,
    output_codes,
    output_scales,
    layer_scale,
):
    hbm = pl.BlockSpec(memory_space=pltpu.HBM)
    vmem = pl.BlockSpec(memory_space=pltpu.VMEM)
    return pl.pallas_call(
        fused_kernel,
        out_shape=jax.ShapeDtypeStruct((1, ROWS, WIDTH), F32),
        in_specs=[hbm] * 10,
        out_specs=vmem,
        scratch_shapes=[
            pltpu.VMEM((WIDTH,), F32),
            pltpu.VMEM((WIDTH,), F32),
            pltpu.SMEM((3, 18), F32),
            pltpu.VMEM((3 * HD,), F32),
            pltpu.SMEM((6, 12), F32),
            pltpu.VMEM((WIDTH,), F32),
            pltpu.VMEM((3, WIDTH, HD), BF16),
            pltpu.VMEM((3, SHARD, BLOCK), BF16),
            pltpu.VMEM((SHARD, 3 * HD), BF16),
            pltpu.VMEM((HD, WIDTH), BF16),
            pltpu.VMEM((HALF, WIDTH), BF16),
            pltpu.VMEM((ROWS, WIDTH), BF16),
            pltpu.VMEM((ROWS, WIDTH), BF16),
            pltpu.VMEM((ROWS, WIDTH), F32),
            pltpu.VMEM((ROWS, 1), F32),
            pltpu.VMEM((4, ROWS, WIDTH), BF16),
            pltpu.VMEM((4 * ROWS, WIDTH), BF16),
            pltpu.VMEM((ROWS, WIDTH), BF16),
            pltpu.VMEM((HD, ROWS), BF16),
            pltpu.VMEM((4, 2 * BLOCK, ROWS), BF16),
            pltpu.VMEM((4 * ROWS, 3 * BLOCK), F32),
            pltpu.VMEM((2, 3, BLOCK, 4 * ROWS), BF16),
            pltpu.VMEM((4, 4, 3, HEAD_DIM, ROWS), BF16),
            pltpu.VMEM((3, HD, ROWS), BF16),
            pltpu.SemaphoreType.DMA((13,)),
            pltpu.SemaphoreType.DMA((4, len(CHUNKS))),
            pltpu.SemaphoreType.DMA((4, len(CHUNKS))),
            pltpu.SemaphoreType.DMA((3, PARTS)),
            pltpu.SemaphoreType.DMA((4, PARTS)),
            pltpu.SemaphoreType.DMA((4, PARTS)),
            pltpu.SemaphoreType.DMA((4,)),
            pltpu.SemaphoreType.DMA((4,)),
            pltpu.SemaphoreType.DMA((4, 4)),
            pltpu.SemaphoreType.DMA((12,)),
        ],
        compiler_params=pltpu.CompilerParams(
            collective_id=0, has_side_effects=True, vmem_limit_bytes=64 * 1024 * 1024 - 65536
        ),
        cost_estimate=pl.CostEstimate(
            flops=2500000000, bytes_accessed=8000000, transcendentals=1000000
        ),
    )(
        tokens,
        upstream_grad,
        norm_gain,
        norm_bias,
        input_codes,
        input_scales,
        input_bias,
        output_codes,
        output_scales,
        layer_scale,
    )


def solution(mesh):
    in_specs = (
        P(("groups", "weight"), "seq", None),
        P(("groups", "weight"), "seq", None),
        P(),
        P(),
        P("weight", None),
        P("weight", None),
        P(),
        P(),
        P(),
        P(),
    )
    out_specs = P(("groups", "weight"), "seq", None)
    local = fused if fits(mesh) else general
    return jax.shard_map(local, mesh=mesh, in_specs=in_specs, out_specs=out_specs, check_vma=False)
```

```python
import functools
import math

import jax
import jax.numpy as jnp
from jax import lax
from jax.experimental import pallas as pl
from jax.experimental.pallas import tpu as pltpu
from jax.sharding import PartitionSpec as P

HEADS = 12
HEAD_DIM = 64
QBLOCK = 128
HD = 768


def dequantize(codes, scales):
    expanded = jnp.repeat(jnp.repeat(scales, QBLOCK, axis=0), QBLOCK, axis=1)
    return (codes.astype(jnp.float32) * expanded).astype(jnp.bfloat16)


def normalize(rows, gain, shift):
    mean_value = jnp.mean(rows, axis=-1, keepdims=True)
    centered = rows - mean_value
    variance = jnp.mean(centered * centered, axis=-1, keepdims=True)
    inverse = lax.rsqrt(variance + 1e-06)
    normed = centered * inverse
    return (normed, inverse, (normed * gain + shift).astype(jnp.bfloat16))


def norm_backward(grad_norm, normed, inverse, gain):
    grad_hat = grad_norm * gain
    first_mean = jnp.mean(grad_hat, axis=-1, keepdims=True)
    second_mean = jnp.mean(grad_hat * normed, axis=-1, keepdims=True)
    return inverse * (grad_hat - first_mean - normed * second_mean)


def score_block(queries, head_grads, pair_block):
    row_count = pair_block.shape[0]
    keys_blk = pair_block[:, :HD].reshape(row_count, HEADS, HEAD_DIM)
    values_blk = pair_block[:, HD:].reshape(row_count, HEADS, HEAD_DIM)
    scores = jnp.einsum(
        "qhd,khd->hqk", queries, keys_blk, preferred_element_type=jnp.float32
    ) * HEAD_DIM ** (-0.5)
    dprob = jnp.einsum("qhd,khd->hqk", head_grads, values_blk, preferred_element_type=jnp.float32)
    return (keys_blk, scores, dprob)


def update_stats(statistics, queries, head_grads, pair_rows):
    sub_size = math.gcd(pair_rows.shape[0], 512)

    def visit_block(block_index, running):
        run_max, run_total, run_mix = running
        pair_block = lax.dynamic_slice_in_dim(pair_rows, block_index * sub_size, sub_size, 0)
        keys_blk, scores, dprob = score_block(queries, head_grads, pair_block)
        new_max = jnp.maximum(run_max, jnp.max(scores, axis=-1))
        factor = jnp.exp(run_max - new_max)
        expo = jnp.exp(scores - new_max[..., None])
        return (
            new_max,
            run_total * factor + jnp.sum(expo, axis=-1),
            run_mix * factor + jnp.sum(expo * dprob, axis=-1),
        )

    return lax.fori_loop(0, pair_rows.shape[0] // sub_size, visit_block, statistics)


def block_backward(queries, head_grads, pair_block, log_total, row_delta):
    keys_blk, scores, dprob = score_block(queries, head_grads, pair_block)
    weights = jnp.exp(scores - log_total[..., None])
    prob_weights = weights.astype(jnp.bfloat16)
    dscore = (weights * (dprob - row_delta[..., None])).astype(jnp.bfloat16)
    return (keys_blk, prob_weights, dscore)


def key_terms_from(queries, head_grads, prob_weights, dscore):
    key_part = jnp.einsum(
        "hqk,qhd->khd", dscore, queries, preferred_element_type=jnp.float32
    ) * HEAD_DIM ** (-0.5)
    value_part = jnp.einsum(
        "hqk,qhd->khd", prob_weights, head_grads, preferred_element_type=jnp.float32
    )
    row_count = key_part.shape[0]
    return jnp.concatenate(
        [key_part.reshape(row_count, HD), value_part.reshape(row_count, HD)], axis=1
    )


def query_side(queries, head_grads, keys_values, local_rows):
    seq_rows = local_rows * lax.axis_size("seq")
    start_stats = (
        jnp.full((HEADS, local_rows), -1e30, jnp.float32),
        jnp.zeros((HEADS, local_rows), jnp.float32),
        jnp.zeros((HEADS, local_rows), jnp.float32),
    )
    all_pairs = lax.all_gather(keys_values, "seq", axis=0, tiled=True)
    statistics = update_stats(start_stats, queries, head_grads, all_pairs)
    row_max, row_total, row_mix = statistics
    log_total = row_max + jnp.log(row_total)
    row_delta = row_mix / row_total
    sub_size = math.gcd(seq_rows, 512)
    block_count = seq_rows // sub_size
    empty_query = jnp.zeros((local_rows, HEADS, HEAD_DIM), jnp.float32)

    def backward_step(block_index, running):
        query_grad, buffer = running
        pair_block = lax.dynamic_slice_in_dim(all_pairs, block_index * sub_size, sub_size, 0)
        keys_blk, prob_weights, dscore = block_backward(
            queries, head_grads, pair_block, log_total, row_delta
        )
        query_grad = query_grad + jnp.einsum(
            "hqk,khd->qhd", dscore, keys_blk, preferred_element_type=jnp.float32
        )
        block_terms = key_terms_from(queries, head_grads, prob_weights, dscore)
        buffer = lax.dynamic_update_slice_in_dim(buffer, block_terms, block_index * sub_size, 0)
        return (query_grad, buffer)

    empty_terms = jnp.zeros((seq_rows, 2 * HD), jnp.float32)
    query_grad, buffer = lax.fori_loop(0, block_count, backward_step, (empty_query, empty_terms))
    pair_grads = lax.psum_scatter(
        buffer.astype(jnp.bfloat16), "seq", scatter_dimension=0, tiled=True
    ).astype(jnp.float32)
    return (query_grad, pair_grads)


def general(
    tokens,
    upstream_grad,
    norm_gain,
    norm_bias,
    input_codes,
    input_scales,
    input_bias,
    output_codes,
    output_scales,
    layer_scale,
):
    all_codes, all_scales = (
        lax.all_gather(input_codes.astype(jnp.float32), "weight", axis=0, tiled=True).astype(
            input_codes.dtype
        ),
        lax.all_gather(input_scales, "weight", axis=0, tiled=True),
    )
    input_weight = dequantize(all_codes, all_scales)
    output_weight = dequantize(output_codes, output_scales)
    normed, inverse, norm_out = normalize(tokens[0].astype(jnp.float32), norm_gain, norm_bias)
    projected = (
        jnp.dot(norm_out, input_weight, preferred_element_type=jnp.float32) + input_bias
    ).astype(jnp.bfloat16)
    local_rows = projected.shape[0]
    queries = projected[:, :HD].reshape(local_rows, HEADS, HEAD_DIM)
    keys_values = projected[:, HD:]
    scaled_grad = (upstream_grad[0].astype(jnp.float32) * layer_scale).astype(jnp.bfloat16)
    head_grads = jnp.dot(scaled_grad, output_weight.T, preferred_element_type=jnp.float32).astype(
        jnp.bfloat16
    )
    head_grads = head_grads.reshape(local_rows, HEADS, HEAD_DIM)
    query_grad, pair_grads = query_side(queries, head_grads, keys_values, local_rows)
    query_grad = (query_grad * HEAD_DIM ** (-0.5)).reshape(local_rows, HD)
    grad_proj = jnp.concatenate([query_grad, pair_grads], axis=1).astype(jnp.bfloat16)
    grad_norm = jnp.dot(grad_proj, input_weight.T, preferred_element_type=jnp.float32)
    result = norm_backward(grad_norm, normed, inverse, norm_gain)
    return result[None]


WIDTH = 1536
ROWS = 128
SHARD = 384
HALF = 384
CHUNKS = tuple((p, 192 * r) for p in range(6) for r in range(2))
CHUNK = 192
BLOCK = 128
PARTS = 4
PART = ROWS // PARTS
BF16 = jnp.bfloat16
F32 = jnp.float32
MESH = pl.DeviceIdType.MESH
NT = (((1,), (1,)), ((), ()))


def fits(mesh):
    return dict(mesh.shape) == {"groups": 2, "seq": 4, "weight": 4}


def fused_kernel(
    tokens_hbm,
    upstream_hbm,
    gain_hbm,
    norm_bias_hbm,
    codes_hbm,
    in_scales_hbm,
    in_bias_hbm,
    out_codes_hbm,
    out_scales_hbm,
    layer_scale_hbm,
    out_ref,
    gain_ref,
    norm_bias_ref,
    in_scales,
    in_bias_ref,
    out_scales,
    layer_scale_ref,
    weight,
    first_codes,
    codes,
    out_codes,
    out_weight,
    tokens,
    upstream,
    normed_buf,
    inverse_buf,
    raw,
    norm_out,
    scaled,
    packed,
    gathered,
    partial,
    projected,
    grads,
    grad_proj,
    load_sem,
    w_send,
    w_recv,
    t_send,
    p_send,
    t_recv,
    a_send,
    a_recv,
    g_send,
    g_recv,
):
    g = lax.axis_index("groups")
    s = lax.axis_index("seq")
    w = lax.axis_index("weight")
    core = lax.rem(w, 2)
    across = lax.rem(w + 2, 4)
    sibling = w + 1 - 2 * core
    far_sibling = lax.rem(sibling + 2, 4)
    side = s // 2
    home = core == side
    inner = lax.rem(s + side, 2) == 1
    outer = jnp.logical_not(inner)
    away = jnp.logical_not(home)
    owner = w - core + side
    blocks = (s, s + 1 - 2 * lax.rem(s, 2), 2 - side, 3 - 3 * side)

    def block_at(p):
        return jnp.where(inner, p, lax.rem(p + 4, 6))

    def lanes(first):
        return pl.ds(pl.multiple_of(first, BLOCK), BLOCK)

    def load(index, source, target):
        copy = pltpu.make_async_copy(source, target, load_sem.at[index])
        copy.start()
        return copy

    load_in_scales = load(4, in_scales_hbm, in_scales)
    load_first = [
        load(10 + t, codes_hbm.at[:, lanes(HD * t + BLOCK * block_at(0))], first_codes.at[t])
        for t in range(3)
    ]
    load_codes = load(0, codes_hbm, codes)
    load_upstream = load(2, upstream_hbm.at[0], upstream)
    load_out_codes = load(3, out_codes_hbm, out_codes)
    load_tokens = load(1, tokens_hbm.at[0], tokens)
    load_out_scales = load(5, out_scales_hbm, out_scales)
    load_layer_scale = load(6, layer_scale_hbm, layer_scale_ref)
    load_gain = load(7, gain_hbm, gain_ref)
    load_norm_bias = load(8, norm_bias_hbm, norm_bias_ref)
    load_in_bias = load(9, in_bias_hbm, in_bias_ref)

    barrier = pltpu.get_barrier_semaphore()
    peers = [{"weight": across}, {"weight": sibling}, {"groups": 1 - g}]
    for k in (1, 2, 3):
        peers.append({"seq": lax.rem(s + k, 4)})
        peers.append({"seq": lax.rem(s + k, 4), "weight": sibling})
    for peer in peers:
        pl.semaphore_signal(barrier, inc=1, device_id=peer, device_id_type=MESH)

    def remote(source, target, send, recv, peer):
        return pltpu.make_async_remote_copy(
            src_ref=source,
            dst_ref=target,
            send_sem=send,
            recv_sem=recv,
            device_id=peer,
            device_id_type=MESH,
        )

    def dequantize_block(p):
        b = block_at(p)
        for t in range(3):
            for rb in range(3):
                rows = pl.ds(pl.multiple_of(SHARD * w + 128 * rb, 128), 128)
                if p == 0:
                    block = first_codes[t, 128 * rb : 128 * (rb + 1), :]
                else:
                    block = codes[128 * rb : 128 * (rb + 1), lanes(HD * t + BLOCK * b)]
                block = block.astype(F32)
                weight[t, rows, lanes(BLOCK * b)] = (block * in_scales[rb, 6 * t + b]).astype(BF16)

    def weight_copy(kind, index, p, row, count, peer):
        rows = pl.ds(pl.multiple_of(row, 32), count)
        part = weight.at[:, rows, lanes(BLOCK * block_at(p))]
        return remote(part, part, w_send.at[kind, index], w_recv.at[kind, index], peer)

    def x_copy(c, shard):
        p, first = CHUNKS[c]
        row = SHARD * shard + first + CHUNK // 2 * g
        return weight_copy(0, c, p, row, CHUNK // 2, {"weight": across})

    def y_copy(c, part):
        p, first = CHUNKS[c]
        row = SHARD * across + first + CHUNK // 2 * part
        return weight_copy(1, c, p, row, CHUNK // 2, {"groups": 1 - g})

    def own_copy(p, shard):
        return weight_copy(2, p, p, SHARD * shard, SHARD, {"weight": sibling})

    def passed_copy(c, shard):
        p, first = CHUNKS[c]
        return weight_copy(3, c, p, SHARD * shard + first, CHUNK, {"weight": sibling})

    def start_own(p):
        for r in range(2):
            x_copy(2 * p + r, w).start()
        own_copy(p, w).start()

    def from_x(c):
        x_copy(c, across).wait_recv()
        y_copy(c, g).start()

    def from_y(c):
        y_copy(c, 1 - g).wait_recv()
        passed_copy(c, across).start()

    def weight_near(p):
        own_copy(p, sibling).wait_recv()

    def weight_ready(p, near=True):
        if near:
            weight_near(p)
        for r in range(2):
            row = SHARD * far_sibling + CHUNK * r
            weight_copy(3, 2 * p + r, p, row, CHUNK, {"weight": sibling}).wait_recv()

    def part_rows(part):
        return pl.ds(PART * part, PART)

    def send_tokens(part):
        dest = jnp.where(home & inner, 3 * core, 1 + core)
        return remote(
            tokens_hbm.at[0, part_rows(part)],
            raw.at[s, part_rows(part)],
            t_send.at[0, part],
            t_recv.at[s, part],
            {"seq": dest},
        )

    def forward_tokens(slot, part):
        z = blocks[slot]
        rows = raw.at[z, part_rows(part)]
        return remote(
            rows, rows, t_send.at[slot - 1, part], t_recv.at[z, part], {"seq": 3 * core}
        )

    def pass_tokens(slot, part):
        z = blocks[slot]
        rows = raw.at[z, part_rows(part)]
        source = tokens_hbm.at[0, part_rows(part)] if slot == 0 else rows
        return remote(source, rows, p_send.at[slot, part], t_recv.at[z, part], {"weight": sibling})

    def tokens_here(slot, part):
        pass_tokens(slot, part).wait_recv()

    def relay(slot, part, forward):
        tokens_here(slot, part)
        if forward:
            forward_tokens(slot, part).start()
        pass_tokens(slot, part).start()

    def share(d):
        count = 256 if d < 2 else 128
        first = 256 * d if d < 2 else 256 + 128 * d
        rows = packed.at[first : first + count, :]
        peer = {"seq": 1 + core if d < 2 else 3 * core, "weight": w - core + d % 2}
        return remote(rows, gathered.at[s, 0:count, :], a_send.at[d], a_recv.at[s], peer)

    def share_done(z, count):
        return remote(
            packed.at[0:count, :],
            gathered.at[z, 0:count, :],
            a_send.at[0],
            a_recv.at[z],
            {"weight": sibling},
        )

    def stays(d):
        return home & (inner if d < 2 else outer) & (core == d % 2)

    def head_gradients(part):
        for rb in range(3):
            rows = slice(HALF * part + 128 * rb, HALF * part + 128 * (rb + 1))
            for cb in range(12):
                cols = slice(128 * cb, 128 * (cb + 1))
                block = out_codes[rows, cols].astype(F32)
                out_weight[128 * rb : 128 * (rb + 1), cols] = (
                    block * out_scales[3 * part + rb, cb]
                ).astype(BF16)
        value = lax.dot_general(out_weight[...], scaled[...], NT, preferred_element_type=F32)
        value = value.astype(BF16)
        for rb in range(3):
            place = (0, 2, 1, 3, 4, 5)[3 * part + rb]
            packed[BLOCK * place : BLOCK * (place + 1), :] = value[128 * rb : 128 * (rb + 1), :]

    def share_all():
        for d in range(4):
            count = 256 if d < 2 else 128
            first = 256 * d if d < 2 else 256 + 128 * d

            @pl.when(jnp.logical_not(stays(d)))
            def _():
                share(d).start()

            @pl.when(stays(d))
            def _():
                gathered[s, 0:count, :] = packed[first : first + count, :]

    def normalize_slot(slot):
        norm_out[ROWS * slot : ROWS * (slot + 1), :] = normalize(
            raw[blocks[slot]].astype(F32), gain_ref[...][None], norm_bias_ref[...][None]
        )[2]

    def product(n, first, count, chip):
        b = block_at(2 * n + core)
        span = pl.ds(pl.multiple_of(2 * SHARD * chip, 128), 2 * SHARD)
        columns = jnp.concatenate([weight[t, span, lanes(BLOCK * b)] for t in range(3)], axis=1)
        rows = norm_out[first : first + count, span]
        return jnp.dot(rows, columns, preferred_element_type=F32)

    def project_near(n, first, count):
        partial[first : first + count, :] = product(n, first, count, w // 2)

    def project(n, first, count):
        b = block_at(2 * n + core)
        value = partial[first : first + count, :] + product(n, first, count, 1 - w // 2)
        for t in range(3):
            part = value[:, BLOCK * t : BLOCK * (t + 1)]
            part = part + in_bias_ref[lanes(HD * t + BLOCK * b)][None]
            if t == 0:
                part = part * HEAD_DIM ** (-0.5)
            projected[n, t, :, first : first + count] = part.T.astype(BF16)

    load_in_scales.wait()
    for copy in load_first:
        copy.wait()
    dequantize_block(0)
    pl.semaphore_wait(barrier, len(peers))

    @pl.when(inner | home)
    def _():
        for part in range(PARTS):
            send_tokens(part).start()

    start_own(0)

    @pl.when(home)
    def _():
        for part in range(PARTS):
            pass_tokens(0, part).start()

    load_codes.wait()
    for p in range(1, 6):
        dequantize_block(p)
        start_own(p)

    load_layer_scale.wait()
    load_upstream.wait()
    scaled[...] = (upstream[...].astype(F32) * layer_scale_ref[...][None]).astype(BF16)
    load_out_scales.wait()
    load_out_codes.wait()
    head_gradients(0)
    head_gradients(1)

    @pl.when(outer & away)
    def _():
        for part in range(PARTS):
            send_tokens(part).start()

    @pl.when(outer | home)
    def _():
        share_all()

    load_gain.wait()
    load_norm_bias.wait()
    load_in_bias.wait()
    load_tokens.wait()
    normed, inverse, rounded = normalize(
        tokens[...].astype(F32), gain_ref[...][None], norm_bias_ref[...][None]
    )
    normed_buf[...] = normed
    inverse_buf[...] = inverse

    @pl.when(home)
    def _():
        norm_out[0:ROWS, :] = rounded

    def relay_inner(slot, *parts):
        @pl.when(home & inner)
        def _():
            for part in parts:
                relay(slot, part, slot > 1)

    def relay_outer(slot, *parts):
        @pl.when(home & outer)
        def _():
            for part in parts:
                relay(slot, part, False)

    def await_tokens(*slots):
        @pl.when(away)
        def _():
            for slot in slots:
                for part in range(PARTS):
                    tokens_here(slot, part)

    relay_inner(2, 0, 1)
    from_x(0)
    relay_outer(1, 0, 1)
    relay_inner(2, 2)
    relay_inner(1, 0, 1)
    from_x(1)

    @pl.when(inner & away)
    def _():
        share_all()

    relay_outer(1, 2, 3)
    from_x(2)
    relay_inner(2, 3)
    relay_inner(3, 0)
    from_y(0)
    relay_inner(3, 1)
    relay_outer(2, 0)
    from_x(3)
    from_y(1)
    relay_inner(1, 2, 3)
    relay_outer(2, 1)
    relay_inner(3, 2)
    from_x(4)
    relay_outer(2, 2)
    relay_inner(3, 3)
    from_y(2)
    relay_outer(2, 3)
    @pl.when(away)
    def _():
        for slot in (0, 1):
            for part in range(PARTS):
                tokens_here(slot, part)
        normalize_slot(0)

    normalize_slot(1)

    def shared(count):
        for z in range(4):

            @pl.when(jnp.logical_not(home & (s == z)))
            def _():
                share_done(z, count).wait_recv()

    def grad_copy(h, slot, b, peer):
        rows = pl.ds(pl.multiple_of(BLOCK * b + HEAD_DIM * (h % 2), 64), HEAD_DIM)
        return remote(
            grads.at[h, slot],
            grad_proj.at[:, rows, :],
            g_send.at[h, slot],
            g_recv.at[2 * b + h % 2],
            peer,
        )

    def send_grads(h, slot):
        b = block_at(h // 2 * 2 + core)
        return grad_copy(h, slot, b, {"seq": blocks[slot], "weight": owner})

    def send_across(h, turn):
        b = block_at(h // 2 * 2 + core)
        slot = 2 + side if turn == 0 else 3 - side
        return grad_copy(h, slot, b, {"seq": turn + 2 - 2 * side, "weight": owner})

    def attend(h):
        n, i = h // 2, h % 2
        rows = slice(HEAD_DIM * i, HEAD_DIM * (i + 1))
        q_t, k_t, v_t = (projected[n, t, rows, :] for t in range(3))
        g_rows = slice(HEAD_DIM * h, HEAD_DIM * (h + 1))
        g_t = jnp.concatenate([gathered[z, g_rows, :] for z in blocks], axis=1)
        scores = jnp.dot(k_t.T, q_t, preferred_element_type=F32)
        dprob = jnp.dot(v_t.T, g_t, preferred_element_type=F32)
        expo = jnp.exp(scores - jnp.max(scores, axis=0, keepdims=True))
        probs = expo * (1.0 / jnp.sum(expo, axis=0, keepdims=True))
        delta = jnp.sum(probs * dprob, axis=0, keepdims=True)
        dscore = (probs * (dprob - delta)).astype(BF16)
        parts = (
            jnp.dot(k_t, dscore, preferred_element_type=F32) * HEAD_DIM ** (-0.5),
            lax.dot_general(q_t, dscore, NT, preferred_element_type=F32),
            lax.dot_general(g_t, probs.astype(BF16), NT, preferred_element_type=F32),
        )
        for t in range(3):
            value = parts[t].astype(BF16)
            for slot in range(4):
                grads[h, slot, t] = value[:, ROWS * slot : ROWS * (slot + 1)]
        send_across(h, 0).start()
        if h % 2 == 1:
            send_across(h, 1).start()
        send_grads(h, 1).start()
        if h % 2 == 1:
            send_across(h - 1, 1).start()

        @pl.when(home)
        def _():
            first = BLOCK * block_at(2 * n + core) + HEAD_DIM * i
            own = pl.ds(pl.multiple_of(first, 64), HEAD_DIM)
            grad_proj[:, own, :] = grads[h, 0]

        @pl.when(away)
        def _():
            send_grads(h, 0).start()

    @pl.when(inner)
    def _():
        await_tokens(2)
        normalize_slot(2)
        from_x(5)
        from_y(3)
        await_tokens(3)
        normalize_slot(3)
        weight_near(core)
        project_near(0, 0, 4 * ROWS)
        from_x(6)
        weight_ready(core, False)
        project(0, 0, 4 * ROWS)
        shared(256)

        from_x(7)
        attend(0)
        from_y(4)

        @pl.when(core == 1)
        def _():
            from_x(8)
            from_y(5)

        attend(1)

        @pl.when(core == 0)
        def _():
            from_x(8)
            from_y(5)

        from_x(9)
        weight_near(2 + core)
        project_near(1, 0, 4 * ROWS)
        from_y(6)
        from_y(7)
        weight_ready(2 + core, False)
        project(1, 0, 4 * ROWS)
        from_x(10)
        attend(2)
        from_x(11)
        from_y(8)
        attend(3)

    @pl.when(outer)
    def _():
        from_x(5)
        relay_outer(3, 0)
        await_tokens(2)
        normalize_slot(2)
        from_y(3)
        from_x(6)
        relay_outer(3, 1)
        weight_near(core)
        project_near(0, 0, 3 * ROWS)
        weight_ready(core, False)
        project(0, 0, 3 * ROWS)
        from_x(7)
        from_y(4)
        relay_outer(3, 2)
        from_x(8)
        from_y(5)
        relay_outer(3, 3)
        await_tokens(3)
        normalize_slot(3)
        project_near(0, 3 * ROWS, ROWS)
        project(0, 3 * ROWS, ROWS)
        shared(128)
        from_x(9)
        attend(0)
        from_x(10)
        from_y(6)
        attend(1)
        from_x(11)
        from_y(7)
        from_y(8)

    from_y(9)

    def grads_ready(first, count):
        for b in range(first, first + count):
            mine = home & (inner if b < 4 else outer) & (core == b % 2)
            for i in range(2):

                @pl.when(jnp.logical_not(mine))
                def _():
                    grad_copy(i, 0, b, {"weight": sibling}).wait_recv()

    def back(first, count):
        total = None
        part = slice(BLOCK * first, BLOCK * (first + count))
        for t in range(3):
            term = lax.dot_general(
                grad_proj[t, part, :].T, weight[t, :, part], NT, preferred_element_type=F32
            )
            total = term if total is None else total + term
        return total

    @pl.when(inner)
    def _():
        weight_ready(1 - core)

    @pl.when(outer)
    def _():
        weight_ready(2)
        weight_ready(3)

    grads_ready(0, 1)
    out_ref[0] = back(0, 1)
    from_y(10)
    from_y(11)
    grads_ready(1, 1)
    out_ref[0] += back(1, 1)

    @pl.when(inner)
    def _():
        weight_ready(4)
        weight_ready(5)

    @pl.when(outer)
    def _():
        weight_ready(1 - core)

    grads_ready(4, 2)
    out_ref[0] += back(4, 2)

    @pl.when(inner)
    def _():
        weight_ready(3 - core)

    @pl.when(outer)
    def _():
        weight_ready(4)
        weight_ready(5)

    for c in range(len(CHUNKS)):
        x_copy(c, w).wait_send()
        y_copy(c, g).wait_send()
        passed_copy(c, across).wait_send()
    for p in range(6):
        own_copy(p, w).wait_send()
    for part in range(PARTS):
        send_tokens(part).wait_send()

        @pl.when(home)
        def _():
            for slot in range(4):
                pass_tokens(slot, part).wait_send()

        @pl.when(home & inner)
        def _():
            for slot in (2, 3):
                forward_tokens(slot, part).wait_send()

    for d in range(4):

        @pl.when(jnp.logical_not(stays(d)))
        def _():
            share(d).wait_send()

    def grads_sent(heads):
        for h in heads:
            for slot in (1, 2, 3):
                send_grads(h, slot).wait_send()

            @pl.when(away)
            def _():
                send_grads(h, 0).wait_send()

    grads_sent((0, 1))
    grads_ready(2, 1)
    out_ref[0] += back(2, 1)
    grads_ready(3, 1)
    grad_norm = out_ref[0] + back(3, 1)
    out_ref[0] = norm_backward(grad_norm, normed_buf[...], inverse_buf[...], gain_ref[...][None])

    @pl.when(inner)
    def _():
        grads_sent((2, 3))


def fused(
    tokens,
    upstream_grad,
    norm_gain,
    norm_bias,
    input_codes,
    input_scales,
    input_bias,
    output_codes,
    output_scales,
    layer_scale,
):
    hbm = pl.BlockSpec(memory_space=pltpu.HBM)
    vmem = pl.BlockSpec(memory_space=pltpu.VMEM)
    return pl.pallas_call(
        fused_kernel,
        out_shape=jax.ShapeDtypeStruct((1, ROWS, WIDTH), F32),
        in_specs=[hbm] * 10,
        out_specs=vmem,
        scratch_shapes=[
            pltpu.VMEM((WIDTH,), F32),
            pltpu.VMEM((WIDTH,), F32),
            pltpu.SMEM((3, 18), F32),
            pltpu.VMEM((3 * HD,), F32),
            pltpu.SMEM((6, 12), F32),
            pltpu.VMEM((WIDTH,), F32),
            pltpu.VMEM((3, WIDTH, HD), BF16),
            pltpu.VMEM((3, SHARD, BLOCK), BF16),
            pltpu.VMEM((SHARD, 3 * HD), BF16),
            pltpu.VMEM((HD, WIDTH), BF16),
            pltpu.VMEM((HALF, WIDTH), BF16),
            pltpu.VMEM((ROWS, WIDTH), BF16),
            pltpu.VMEM((ROWS, WIDTH), BF16),
            pltpu.VMEM((ROWS, WIDTH), F32),
            pltpu.VMEM((ROWS, 1), F32),
            pltpu.VMEM((4, ROWS, WIDTH), BF16),
            pltpu.VMEM((4 * ROWS, WIDTH), BF16),
            pltpu.VMEM((ROWS, WIDTH), BF16),
            pltpu.VMEM((HD, ROWS), BF16),
            pltpu.VMEM((4, 2 * BLOCK, ROWS), BF16),
            pltpu.VMEM((4 * ROWS, 3 * BLOCK), F32),
            pltpu.VMEM((2, 3, BLOCK, 4 * ROWS), BF16),
            pltpu.VMEM((4, 4, 3, HEAD_DIM, ROWS), BF16),
            pltpu.VMEM((3, HD, ROWS), BF16),
            pltpu.SemaphoreType.DMA((13,)),
            pltpu.SemaphoreType.DMA((4, len(CHUNKS))),
            pltpu.SemaphoreType.DMA((4, len(CHUNKS))),
            pltpu.SemaphoreType.DMA((3, PARTS)),
            pltpu.SemaphoreType.DMA((4, PARTS)),
            pltpu.SemaphoreType.DMA((4, PARTS)),
            pltpu.SemaphoreType.DMA((4,)),
            pltpu.SemaphoreType.DMA((4,)),
            pltpu.SemaphoreType.DMA((4, 4)),
            pltpu.SemaphoreType.DMA((12,)),
        ],
        compiler_params=pltpu.CompilerParams(
            collective_id=0, has_side_effects=True, vmem_limit_bytes=64 * 1024 * 1024 - 65536
        ),
        cost_estimate=pl.CostEstimate(
            flops=2500000000, bytes_accessed=8000000, transcendentals=1000000
        ),
    )(
        tokens,
        upstream_grad,
        norm_gain,
        norm_bias,
        input_codes,
        input_scales,
        input_bias,
        output_codes,
        output_scales,
        layer_scale,
    )


def solution(mesh):
    in_specs = (
        P(("groups", "weight"), "seq", None),
        P(("groups", "weight"), "seq", None),
        P(),
        P(),
        P("weight", None),
        P("weight", None),
        P(),
        P(),
        P(),
        P(),
    )
    out_specs = P(("groups", "weight"), "seq", None)
    local = fused if fits(mesh) else general
    return jax.shard_map(local, mesh=mesh, in_specs=in_specs, out_specs=out_specs, check_vma=False)
```

```python
import functools
import math

import jax
import jax.numpy as jnp
from jax import lax
from jax.experimental import pallas as pl
from jax.experimental.pallas import tpu as pltpu
from jax.sharding import PartitionSpec as P

HEADS = 12
HEAD_DIM = 64
QBLOCK = 128
HD = 768


def dequantize(codes, scales):
    expanded = jnp.repeat(jnp.repeat(scales, QBLOCK, axis=0), QBLOCK, axis=1)
    return (codes.astype(jnp.float32) * expanded).astype(jnp.bfloat16)


def normalize(rows, gain, shift):
    mean_value = jnp.mean(rows, axis=-1, keepdims=True)
    centered = rows - mean_value
    variance = jnp.mean(centered * centered, axis=-1, keepdims=True)
    inverse = lax.rsqrt(variance + 1e-06)
    normed = centered * inverse
    return (normed, inverse, (normed * gain + shift).astype(jnp.bfloat16))


def norm_backward(grad_norm, normed, inverse, gain):
    grad_hat = grad_norm * gain
    first_mean = jnp.mean(grad_hat, axis=-1, keepdims=True)
    second_mean = jnp.mean(grad_hat * normed, axis=-1, keepdims=True)
    return inverse * (grad_hat - first_mean - normed * second_mean)


def score_block(queries, head_grads, pair_block):
    row_count = pair_block.shape[0]
    keys_blk = pair_block[:, :HD].reshape(row_count, HEADS, HEAD_DIM)
    values_blk = pair_block[:, HD:].reshape(row_count, HEADS, HEAD_DIM)
    scores = jnp.einsum(
        "qhd,khd->hqk", queries, keys_blk, preferred_element_type=jnp.float32
    ) * HEAD_DIM ** (-0.5)
    dprob = jnp.einsum("qhd,khd->hqk", head_grads, values_blk, preferred_element_type=jnp.float32)
    return (keys_blk, scores, dprob)


def update_stats(statistics, queries, head_grads, pair_rows):
    sub_size = math.gcd(pair_rows.shape[0], 512)

    def visit_block(block_index, running):
        run_max, run_total, run_mix = running
        pair_block = lax.dynamic_slice_in_dim(pair_rows, block_index * sub_size, sub_size, 0)
        keys_blk, scores, dprob = score_block(queries, head_grads, pair_block)
        new_max = jnp.maximum(run_max, jnp.max(scores, axis=-1))
        factor = jnp.exp(run_max - new_max)
        expo = jnp.exp(scores - new_max[..., None])
        return (
            new_max,
            run_total * factor + jnp.sum(expo, axis=-1),
            run_mix * factor + jnp.sum(expo * dprob, axis=-1),
        )

    return lax.fori_loop(0, pair_rows.shape[0] // sub_size, visit_block, statistics)


def block_backward(queries, head_grads, pair_block, log_total, row_delta):
    keys_blk, scores, dprob = score_block(queries, head_grads, pair_block)
    weights = jnp.exp(scores - log_total[..., None])
    prob_weights = weights.astype(jnp.bfloat16)
    dscore = (weights * (dprob - row_delta[..., None])).astype(jnp.bfloat16)
    return (keys_blk, prob_weights, dscore)


def key_terms_from(queries, head_grads, prob_weights, dscore):
    key_part = jnp.einsum(
        "hqk,qhd->khd", dscore, queries, preferred_element_type=jnp.float32
    ) * HEAD_DIM ** (-0.5)
    value_part = jnp.einsum(
        "hqk,qhd->khd", prob_weights, head_grads, preferred_element_type=jnp.float32
    )
    row_count = key_part.shape[0]
    return jnp.concatenate(
        [key_part.reshape(row_count, HD), value_part.reshape(row_count, HD)], axis=1
    )


def query_side(queries, head_grads, keys_values, local_rows):
    seq_rows = local_rows * lax.axis_size("seq")
    start_stats = (
        jnp.full((HEADS, local_rows), -1e30, jnp.float32),
        jnp.zeros((HEADS, local_rows), jnp.float32),
        jnp.zeros((HEADS, local_rows), jnp.float32),
    )
    all_pairs = lax.all_gather(keys_values, "seq", axis=0, tiled=True)
    statistics = update_stats(start_stats, queries, head_grads, all_pairs)
    row_max, row_total, row_mix = statistics
    log_total = row_max + jnp.log(row_total)
    row_delta = row_mix / row_total
    sub_size = math.gcd(seq_rows, 512)
    block_count = seq_rows // sub_size
    empty_query = jnp.zeros((local_rows, HEADS, HEAD_DIM), jnp.float32)

    def backward_step(block_index, running):
        query_grad, buffer = running
        pair_block = lax.dynamic_slice_in_dim(all_pairs, block_index * sub_size, sub_size, 0)
        keys_blk, prob_weights, dscore = block_backward(
            queries, head_grads, pair_block, log_total, row_delta
        )
        query_grad = query_grad + jnp.einsum(
            "hqk,khd->qhd", dscore, keys_blk, preferred_element_type=jnp.float32
        )
        block_terms = key_terms_from(queries, head_grads, prob_weights, dscore)
        buffer = lax.dynamic_update_slice_in_dim(buffer, block_terms, block_index * sub_size, 0)
        return (query_grad, buffer)

    empty_terms = jnp.zeros((seq_rows, 2 * HD), jnp.float32)
    query_grad, buffer = lax.fori_loop(0, block_count, backward_step, (empty_query, empty_terms))
    pair_grads = lax.psum_scatter(
        buffer.astype(jnp.bfloat16), "seq", scatter_dimension=0, tiled=True
    ).astype(jnp.float32)
    return (query_grad, pair_grads)


def general(
    tokens,
    upstream_grad,
    norm_gain,
    norm_bias,
    input_codes,
    input_scales,
    input_bias,
    output_codes,
    output_scales,
    layer_scale,
):
    all_codes, all_scales = (
        lax.all_gather(input_codes.astype(jnp.float32), "weight", axis=0, tiled=True).astype(
            input_codes.dtype
        ),
        lax.all_gather(input_scales, "weight", axis=0, tiled=True),
    )
    input_weight = dequantize(all_codes, all_scales)
    output_weight = dequantize(output_codes, output_scales)
    normed, inverse, norm_out = normalize(tokens[0].astype(jnp.float32), norm_gain, norm_bias)
    projected = (
        jnp.dot(norm_out, input_weight, preferred_element_type=jnp.float32) + input_bias
    ).astype(jnp.bfloat16)
    local_rows = projected.shape[0]
    queries = projected[:, :HD].reshape(local_rows, HEADS, HEAD_DIM)
    keys_values = projected[:, HD:]
    scaled_grad = (upstream_grad[0].astype(jnp.float32) * layer_scale).astype(jnp.bfloat16)
    head_grads = jnp.dot(scaled_grad, output_weight.T, preferred_element_type=jnp.float32).astype(
        jnp.bfloat16
    )
    head_grads = head_grads.reshape(local_rows, HEADS, HEAD_DIM)
    query_grad, pair_grads = query_side(queries, head_grads, keys_values, local_rows)
    query_grad = (query_grad * HEAD_DIM ** (-0.5)).reshape(local_rows, HD)
    grad_proj = jnp.concatenate([query_grad, pair_grads], axis=1).astype(jnp.bfloat16)
    grad_norm = jnp.dot(grad_proj, input_weight.T, preferred_element_type=jnp.float32)
    result = norm_backward(grad_norm, normed, inverse, norm_gain)
    return result[None]


WIDTH = 1536
ROWS = 128
SHARD = 384
HALF = 384
CHUNKS = tuple((p, 192 * r) for p in range(6) for r in range(2))
CHUNK = 192
BLOCK = 128
PARTS = 4
PART = ROWS // PARTS
BF16 = jnp.bfloat16
F32 = jnp.float32
MESH = pl.DeviceIdType.MESH
NT = (((1,), (1,)), ((), ()))


def fits(mesh):
    return dict(mesh.shape) == {"groups": 2, "seq": 4, "weight": 4}


def fused_kernel(
    tokens_hbm,
    upstream_hbm,
    gain_hbm,
    norm_bias_hbm,
    codes_hbm,
    in_scales_hbm,
    in_bias_hbm,
    out_codes_hbm,
    out_scales_hbm,
    layer_scale_hbm,
    out_ref,
    gain_ref,
    norm_bias_ref,
    in_scales,
    in_bias_ref,
    out_scales,
    layer_scale_ref,
    weight,
    first_codes,
    codes,
    out_codes,
    out_weight,
    tokens,
    upstream,
    normed_buf,
    inverse_buf,
    raw,
    norm_out,
    scaled,
    packed,
    gathered,
    total,
    partial,
    projected,
    grads,
    grad_proj,
    load_sem,
    w_send,
    w_recv,
    t_send,
    p_send,
    t_recv,
    a_send,
    a_recv,
    g_send,
    g_recv,
):
    g = lax.axis_index("groups")
    s = lax.axis_index("seq")
    w = lax.axis_index("weight")
    core = lax.rem(w, 2)
    across = lax.rem(w + 2, 4)
    sibling = w + 1 - 2 * core
    far_sibling = lax.rem(sibling + 2, 4)
    side = s // 2
    home = core == side
    inner = lax.rem(s + side, 2) == 1
    outer = jnp.logical_not(inner)
    away = jnp.logical_not(home)
    owner = w - core + side
    blocks = (s, s + 1 - 2 * lax.rem(s, 2), 2 - side, 3 - 3 * side)

    def block_at(p):
        return jnp.where(inner, p, lax.rem(p + 4, 6))

    def lanes(first):
        return pl.ds(pl.multiple_of(first, BLOCK), BLOCK)

    def load(index, source, target):
        copy = pltpu.make_async_copy(source, target, load_sem.at[index])
        copy.start()
        return copy

    load_in_scales = load(4, in_scales_hbm, in_scales)
    load_first = [
        load(10 + t, codes_hbm.at[:, lanes(HD * t + BLOCK * block_at(0))], first_codes.at[t])
        for t in range(3)
    ]
    load_codes = load(0, codes_hbm, codes)
    load_upstream = load(2, upstream_hbm.at[0], upstream)
    load_out_codes = load(3, out_codes_hbm, out_codes)
    load_tokens = load(1, tokens_hbm.at[0], tokens)
    load_out_scales = load(5, out_scales_hbm, out_scales)
    load_layer_scale = load(6, layer_scale_hbm, layer_scale_ref)
    load_gain = load(7, gain_hbm, gain_ref)
    load_norm_bias = load(8, norm_bias_hbm, norm_bias_ref)
    load_in_bias = load(9, in_bias_hbm, in_bias_ref)

    barrier = pltpu.get_barrier_semaphore()
    peers = [{"weight": across}, {"weight": sibling}, {"groups": 1 - g}]
    for k in (1, 2, 3):
        peers.append({"seq": lax.rem(s + k, 4)})
        peers.append({"seq": lax.rem(s + k, 4), "weight": sibling})
    for peer in peers:
        pl.semaphore_signal(barrier, inc=1, device_id=peer, device_id_type=MESH)

    def remote(source, target, send, recv, peer):
        return pltpu.make_async_remote_copy(
            src_ref=source,
            dst_ref=target,
            send_sem=send,
            recv_sem=recv,
            device_id=peer,
            device_id_type=MESH,
        )

    def dequantize_block(p):
        b = block_at(p)
        for t in range(3):
            for rb in range(3):
                rows = pl.ds(pl.multiple_of(SHARD * w + 128 * rb, 128), 128)
                if p == 0:
                    block = first_codes[t, 128 * rb : 128 * (rb + 1), :]
                else:
                    block = codes[128 * rb : 128 * (rb + 1), lanes(HD * t + BLOCK * b)]
                block = block.astype(F32)
                weight[t, rows, lanes(BLOCK * b)] = (block * in_scales[rb, 6 * t + b]).astype(BF16)

    def weight_copy(kind, index, p, row, count, peer):
        rows = pl.ds(pl.multiple_of(row, 32), count)
        part = weight.at[:, rows, lanes(BLOCK * block_at(p))]
        return remote(part, part, w_send.at[kind, index], w_recv.at[kind, index], peer)

    def x_copy(c, shard):
        p, first = CHUNKS[c]
        row = SHARD * shard + first + CHUNK // 2 * g
        return weight_copy(0, c, p, row, CHUNK // 2, {"weight": across})

    def y_copy(c, part):
        p, first = CHUNKS[c]
        row = SHARD * across + first + CHUNK // 2 * part
        return weight_copy(1, c, p, row, CHUNK // 2, {"groups": 1 - g})

    def own_copy(p, shard):
        return weight_copy(2, p, p, SHARD * shard, SHARD, {"weight": sibling})

    def passed_copy(c, shard):
        p, first = CHUNKS[c]
        return weight_copy(3, c, p, SHARD * shard + first, CHUNK, {"weight": sibling})

    def start_own(p):
        for r in range(2):
            x_copy(2 * p + r, w).start()
        own_copy(p, w).start()

    def from_x(c):
        x_copy(c, across).wait_recv()
        y_copy(c, g).start()

    def from_y(c):
        y_copy(c, 1 - g).wait_recv()
        passed_copy(c, across).start()

    def weight_near(p):
        own_copy(p, sibling).wait_recv()

    def weight_ready(p, near=True):
        if near:
            weight_near(p)
        for r in range(2):
            row = SHARD * far_sibling + CHUNK * r
            weight_copy(3, 2 * p + r, p, row, CHUNK, {"weight": sibling}).wait_recv()

    def part_rows(part):
        return pl.ds(PART * part, PART)

    def send_tokens(part):
        dest = jnp.where(home & inner, 3 * core, 1 + core)
        return remote(
            tokens_hbm.at[0, part_rows(part)],
            raw.at[s, part_rows(part)],
            t_send.at[0, part],
            t_recv.at[s, part],
            {"seq": dest},
        )

    def forward_tokens(slot, part):
        z = blocks[slot]
        rows = raw.at[z, part_rows(part)]
        return remote(
            rows, rows, t_send.at[slot - 1, part], t_recv.at[z, part], {"seq": 3 * core}
        )

    def pass_tokens(slot, part):
        z = blocks[slot]
        rows = raw.at[z, part_rows(part)]
        source = tokens_hbm.at[0, part_rows(part)] if slot == 0 else rows
        return remote(source, rows, p_send.at[slot, part], t_recv.at[z, part], {"weight": sibling})

    def tokens_here(slot, part):
        pass_tokens(slot, part).wait_recv()

    def relay(slot, part, forward):
        tokens_here(slot, part)
        if forward:
            forward_tokens(slot, part).start()
        pass_tokens(slot, part).start()

    def share(d):
        count = 256 if d < 2 else 128
        first = 256 * d if d < 2 else 256 + 128 * d
        rows = packed.at[first : first + count, :]
        peer = {"seq": 1 + core if d < 2 else 3 * core, "weight": w - core + d % 2}
        return remote(rows, gathered.at[s, 0:count, :], a_send.at[d], a_recv.at[s], peer)

    def share_done(z, count):
        return remote(
            packed.at[0:count, :],
            gathered.at[z, 0:count, :],
            a_send.at[0],
            a_recv.at[z],
            {"weight": sibling},
        )

    def stays(d):
        return home & (inner if d < 2 else outer) & (core == d % 2)

    def head_gradients(part):
        for rb in range(3):
            rows = slice(HALF * part + 128 * rb, HALF * part + 128 * (rb + 1))
            for cb in range(12):
                cols = slice(128 * cb, 128 * (cb + 1))
                block = out_codes[rows, cols].astype(F32)
                out_weight[128 * rb : 128 * (rb + 1), cols] = (
                    block * out_scales[3 * part + rb, cb]
                ).astype(BF16)
        value = lax.dot_general(out_weight[...], scaled[...], NT, preferred_element_type=F32)
        value = value.astype(BF16)
        for rb in range(3):
            place = (0, 2, 1, 3, 4, 5)[3 * part + rb]
            packed[BLOCK * place : BLOCK * (place + 1), :] = value[128 * rb : 128 * (rb + 1), :]

    def share_all():
        for d in range(4):
            count = 256 if d < 2 else 128
            first = 256 * d if d < 2 else 256 + 128 * d

            @pl.when(jnp.logical_not(stays(d)))
            def _():
                share(d).start()

            @pl.when(stays(d))
            def _():
                gathered[s, 0:count, :] = packed[first : first + count, :]

    def normalize_slot(slot):
        norm_out[ROWS * slot : ROWS * (slot + 1), :] = normalize(
            raw[blocks[slot]].astype(F32), gain_ref[...][None], norm_bias_ref[...][None]
        )[2]

    def product(n, first, count, chip):
        b = block_at(2 * n + core)
        span = pl.ds(pl.multiple_of(2 * SHARD * chip, 128), 2 * SHARD)
        columns = jnp.concatenate([weight[t, span, lanes(BLOCK * b)] for t in range(3)], axis=1)
        rows = norm_out[first : first + count, span]
        return jnp.dot(rows, columns, preferred_element_type=F32)

    def project_near(n, first, count):
        partial[first : first + count, :] = product(n, first, count, w // 2)

    def project(n, first, count):
        b = block_at(2 * n + core)
        value = partial[first : first + count, :] + product(n, first, count, 1 - w // 2)
        for t in range(3):
            part = value[:, BLOCK * t : BLOCK * (t + 1)]
            part = part + in_bias_ref[lanes(HD * t + BLOCK * b)][None]
            if t == 0:
                part = part * HEAD_DIM ** (-0.5)
            projected[n, t, :, first : first + count] = part.T.astype(BF16)

    load_in_scales.wait()
    for copy in load_first:
        copy.wait()
    dequantize_block(0)
    pl.semaphore_wait(barrier, len(peers))

    @pl.when(inner | home)
    def _():
        for part in range(PARTS):
            send_tokens(part).start()

    start_own(0)

    @pl.when(home)
    def _():
        for part in range(PARTS):
            pass_tokens(0, part).start()

    load_codes.wait()
    for p in range(1, 6):
        dequantize_block(p)
        start_own(p)

    load_layer_scale.wait()
    load_upstream.wait()
    scaled[...] = (upstream[...].astype(F32) * layer_scale_ref[...][None]).astype(BF16)
    load_out_scales.wait()
    load_out_codes.wait()
    head_gradients(0)
    head_gradients(1)

    @pl.when(outer & away)
    def _():
        for part in range(PARTS):
            send_tokens(part).start()

    @pl.when(outer | home)
    def _():
        share_all()

    load_gain.wait()
    load_norm_bias.wait()
    load_in_bias.wait()
    load_tokens.wait()
    normed, inverse, rounded = normalize(
        tokens[...].astype(F32), gain_ref[...][None], norm_bias_ref[...][None]
    )
    normed_buf[...] = normed
    inverse_buf[...] = inverse

    @pl.when(home)
    def _():
        norm_out[0:ROWS, :] = rounded

    def relay_inner(slot, *parts):
        @pl.when(home & inner)
        def _():
            for part in parts:
                relay(slot, part, slot > 1)

    def relay_outer(slot, *parts):
        @pl.when(home & outer)
        def _():
            for part in parts:
                relay(slot, part, False)

    def await_tokens(*slots):
        @pl.when(away)
        def _():
            for slot in slots:
                for part in range(PARTS):
                    tokens_here(slot, part)

    relay_inner(2, 0, 1)
    from_x(0)
    relay_outer(1, 0, 1)
    relay_inner(2, 2)
    relay_inner(1, 0, 1)
    from_x(1)

    @pl.when(inner & away)
    def _():
        share_all()

    relay_outer(1, 2, 3)
    from_x(2)
    relay_inner(2, 3)
    relay_inner(3, 0)
    from_y(0)
    relay_inner(3, 1)
    relay_outer(2, 0)
    from_x(3)
    from_y(1)
    relay_inner(1, 2, 3)
    relay_outer(2, 1)
    relay_inner(3, 2)
    from_x(4)
    relay_outer(2, 2)
    relay_inner(3, 3)
    from_y(2)
    relay_outer(2, 3)
    @pl.when(away)
    def _():
        for slot in (0, 1):
            for part in range(PARTS):
                tokens_here(slot, part)
        normalize_slot(0)

    normalize_slot(1)

    def shared(count):
        for z in range(4):

            @pl.when(jnp.logical_not(home & (s == z)))
            def _():
                share_done(z, count).wait_recv()

    def grad_copy(h, slot, b, peer):
        rows = pl.ds(pl.multiple_of(BLOCK * b + HEAD_DIM * (h % 2), 64), HEAD_DIM)
        return remote(
            grads.at[h, slot],
            grad_proj.at[:, rows, :],
            g_send.at[h, slot],
            g_recv.at[2 * b + h % 2],
            peer,
        )

    def send_grads(h, slot):
        b = block_at(h // 2 * 2 + core)
        return grad_copy(h, slot, b, {"seq": blocks[slot], "weight": owner})

    def send_across(h, turn):
        b = block_at(h // 2 * 2 + core)
        slot = 2 + side if turn == 0 else 3 - side
        return grad_copy(h, slot, b, {"seq": turn + 2 - 2 * side, "weight": owner})

    def attend(h):
        n, i = h // 2, h % 2
        rows = slice(HEAD_DIM * i, HEAD_DIM * (i + 1))
        q_t, k_t, v_t = (projected[n, t, rows, :] for t in range(3))
        g_rows = slice(HEAD_DIM * h, HEAD_DIM * (h + 1))
        g_t = jnp.concatenate([gathered[z, g_rows, :] for z in blocks], axis=1)
        scores = jnp.dot(k_t.T, q_t, preferred_element_type=F32)
        dprob = jnp.dot(v_t.T, g_t, preferred_element_type=F32)
        expo = jnp.exp(scores - jnp.max(scores, axis=0, keepdims=True))
        probs = expo * (1.0 / jnp.sum(expo, axis=0, keepdims=True))
        delta = jnp.sum(probs * dprob, axis=0, keepdims=True)
        dscore = (probs * (dprob - delta)).astype(BF16)
        parts = (
            jnp.dot(k_t, dscore, preferred_element_type=F32) * HEAD_DIM ** (-0.5),
            lax.dot_general(q_t, dscore, NT, preferred_element_type=F32),
            lax.dot_general(g_t, probs.astype(BF16), NT, preferred_element_type=F32),
        )
        for t in range(3):
            value = parts[t].astype(BF16)
            for slot in range(4):
                grads[h, slot, t] = value[:, ROWS * slot : ROWS * (slot + 1)]
        send_across(h, 0).start()
        if h % 2 == 1:
            send_across(h, 1).start()
        send_grads(h, 1).start()
        if h % 2 == 1:
            send_across(h - 1, 1).start()

        @pl.when(home)
        def _():
            first = BLOCK * block_at(2 * n + core) + HEAD_DIM * i
            own = pl.ds(pl.multiple_of(first, 64), HEAD_DIM)
            grad_proj[:, own, :] = grads[h, 0]

        @pl.when(away)
        def _():
            send_grads(h, 0).start()

    @pl.when(inner)
    def _():
        await_tokens(2)
        normalize_slot(2)
        from_x(5)
        from_y(3)
        await_tokens(3)
        normalize_slot(3)
        weight_near(core)
        project_near(0, 0, 4 * ROWS)
        from_x(6)
        weight_ready(core, False)
        project(0, 0, 4 * ROWS)
        shared(256)

        from_x(7)
        attend(0)
        from_y(4)

        @pl.when(core == 1)
        def _():
            from_x(8)
            from_y(5)

        attend(1)

        @pl.when(core == 0)
        def _():
            from_x(8)
            from_y(5)

        from_x(9)
        weight_near(2 + core)
        project_near(1, 0, 4 * ROWS)
        from_y(6)
        from_y(7)
        weight_ready(2 + core, False)
        project(1, 0, 4 * ROWS)
        from_x(10)
        attend(2)
        from_x(11)
        from_y(8)
        attend(3)

    @pl.when(outer)
    def _():
        from_x(5)
        relay_outer(3, 0)
        await_tokens(2)
        normalize_slot(2)
        from_y(3)
        from_x(6)
        relay_outer(3, 1)
        weight_near(core)
        project_near(0, 0, 3 * ROWS)
        weight_ready(core, False)
        project(0, 0, 3 * ROWS)
        from_x(7)
        from_y(4)
        relay_outer(3, 2)
        from_x(8)
        from_y(5)
        relay_outer(3, 3)
        await_tokens(3)
        normalize_slot(3)
        project_near(0, 3 * ROWS, ROWS)
        project(0, 3 * ROWS, ROWS)
        shared(128)
        from_x(9)
        attend(0)
        from_x(10)
        from_y(6)
        attend(1)
        from_x(11)
        from_y(7)
        from_y(8)

    from_y(9)

    def grads_ready(first, count):
        for b in range(first, first + count):
            mine = home & (inner if b < 4 else outer) & (core == b % 2)
            for i in range(2):

                @pl.when(jnp.logical_not(mine))
                def _():
                    grad_copy(i, 0, b, {"weight": sibling}).wait_recv()

    def back(first, count):
        result = None
        part = slice(BLOCK * first, BLOCK * (first + count))
        for t in range(3):
            term = lax.dot_general(
                grad_proj[t, part, :].T, weight[t, :, part], NT, preferred_element_type=F32
            )
            result = term if result is None else result + term
        return result

    @pl.when(inner)
    def _():
        weight_ready(1 - core)

    @pl.when(outer)
    def _():
        weight_ready(2)
        weight_ready(3)

    grads_ready(0, 1)
    total[...] = back(0, 1)
    from_y(10)
    from_y(11)
    grads_ready(1, 1)
    total[...] += back(1, 1)

    @pl.when(inner)
    def _():
        weight_ready(4)
        weight_ready(5)

    @pl.when(outer)
    def _():
        weight_ready(1 - core)

    grads_ready(4, 2)
    total[...] += back(4, 2)

    @pl.when(inner)
    def _():
        weight_ready(3 - core)

    @pl.when(outer)
    def _():
        weight_ready(4)
        weight_ready(5)

    for c in range(len(CHUNKS)):
        x_copy(c, w).wait_send()
        y_copy(c, g).wait_send()
        passed_copy(c, across).wait_send()
    for p in range(6):
        own_copy(p, w).wait_send()
    for part in range(PARTS):
        send_tokens(part).wait_send()

        @pl.when(home)
        def _():
            for slot in range(4):
                pass_tokens(slot, part).wait_send()

        @pl.when(home & inner)
        def _():
            for slot in (2, 3):
                forward_tokens(slot, part).wait_send()

    for d in range(4):

        @pl.when(jnp.logical_not(stays(d)))
        def _():
            share(d).wait_send()

    def grads_sent(heads):
        for h in heads:
            for slot in (1, 2, 3):
                send_grads(h, slot).wait_send()

            @pl.when(away)
            def _():
                send_grads(h, 0).wait_send()

    grads_sent((0, 1))
    grads_ready(2, 1)
    total[...] += back(2, 1)
    grads_ready(3, 1)
    grad_norm = total[...] + back(3, 1)
    result = norm_backward(grad_norm, normed_buf[...], inverse_buf[...], gain_ref[...][None])
    out_ref[0] = result.astype(BF16)

    @pl.when(inner)
    def _():
        grads_sent((2, 3))


def fused(
    tokens,
    upstream_grad,
    norm_gain,
    norm_bias,
    input_codes,
    input_scales,
    input_bias,
    output_codes,
    output_scales,
    layer_scale,
):
    hbm = pl.BlockSpec(memory_space=pltpu.HBM)
    vmem = pl.BlockSpec(memory_space=pltpu.VMEM)
    return pl.pallas_call(
        fused_kernel,
        out_shape=jax.ShapeDtypeStruct((1, ROWS, WIDTH), BF16),
        in_specs=[hbm] * 10,
        out_specs=vmem,
        scratch_shapes=[
            pltpu.VMEM((WIDTH,), F32),
            pltpu.VMEM((WIDTH,), F32),
            pltpu.SMEM((3, 18), F32),
            pltpu.VMEM((3 * HD,), F32),
            pltpu.SMEM((6, 12), F32),
            pltpu.VMEM((WIDTH,), F32),
            pltpu.VMEM((3, WIDTH, HD), BF16),
            pltpu.VMEM((3, SHARD, BLOCK), BF16),
            pltpu.VMEM((SHARD, 3 * HD), BF16),
            pltpu.VMEM((HD, WIDTH), BF16),
            pltpu.VMEM((HALF, WIDTH), BF16),
            pltpu.VMEM((ROWS, WIDTH), BF16),
            pltpu.VMEM((ROWS, WIDTH), BF16),
            pltpu.VMEM((ROWS, WIDTH), F32),
            pltpu.VMEM((ROWS, 1), F32),
            pltpu.VMEM((4, ROWS, WIDTH), BF16),
            pltpu.VMEM((4 * ROWS, WIDTH), BF16),
            pltpu.VMEM((ROWS, WIDTH), BF16),
            pltpu.VMEM((HD, ROWS), BF16),
            pltpu.VMEM((4, 2 * BLOCK, ROWS), BF16),
            pltpu.VMEM((ROWS, WIDTH), F32),
            pltpu.VMEM((4 * ROWS, 3 * BLOCK), F32),
            pltpu.VMEM((2, 3, BLOCK, 4 * ROWS), BF16),
            pltpu.VMEM((4, 4, 3, HEAD_DIM, ROWS), BF16),
            pltpu.VMEM((3, HD, ROWS), BF16),
            pltpu.SemaphoreType.DMA((13,)),
            pltpu.SemaphoreType.DMA((4, len(CHUNKS))),
            pltpu.SemaphoreType.DMA((4, len(CHUNKS))),
            pltpu.SemaphoreType.DMA((3, PARTS)),
            pltpu.SemaphoreType.DMA((4, PARTS)),
            pltpu.SemaphoreType.DMA((4, PARTS)),
            pltpu.SemaphoreType.DMA((4,)),
            pltpu.SemaphoreType.DMA((4,)),
            pltpu.SemaphoreType.DMA((4, 4)),
            pltpu.SemaphoreType.DMA((12,)),
        ],
        compiler_params=pltpu.CompilerParams(
            collective_id=0, has_side_effects=True, vmem_limit_bytes=64 * 1024 * 1024 - 65536
        ),
        cost_estimate=pl.CostEstimate(
            flops=2500000000, bytes_accessed=8000000, transcendentals=1000000
        ),
    )(
        tokens,
        upstream_grad,
        norm_gain,
        norm_bias,
        input_codes,
        input_scales,
        input_bias,
        output_codes,
        output_scales,
        layer_scale,
    ).astype(F32)


def solution(mesh):
    in_specs = (
        P(("groups", "weight"), "seq", None),
        P(("groups", "weight"), "seq", None),
        P(),
        P(),
        P("weight", None),
        P("weight", None),
        P(),
        P(),
        P(),
        P(),
    )
    out_specs = P(("groups", "weight"), "seq", None)
    local = fused if fits(mesh) else general
    return jax.shard_map(local, mesh=mesh, in_specs=in_specs, out_specs=out_specs, check_vma=False)
```
